256 devices in a mesh: dp: 4 (over y), ctx: 64 (over x, z, core).
Axes of the slice: x: 4, y: 4, z: 8, core: 2. Of those that a mesh axis runs over, the one named last changes fastest.
Arguments:
- queries: bfloat16 [4, 8192, 2048], P('dp', 'ctx'), may hold values from -6 to 6
- key_rows: bfloat16 [4, 8192, 2048], P('dp', 'ctx'), may hold values from -6 to 6
- value_rows: bfloat16 [4, 8192, 2048], P('dp', 'ctx'), may hold values from -6 to 6
- out_grad: bfloat16 [4, 8192, 2048], P('dp', 'ctx'), may hold values from -8 to 8
- norm_gain: float32 [2048], replicated, may hold values from 0.1 to 1.9
Outputs:
- query_grad: bfloat16 [4, 8192, 2048], P('dp', 'ctx')
- key_grad: bfloat16 [4, 8192, 2048], P('dp', 'ctx')
- value_grad: bfloat16 [4, 8192, 2048], P('dp', 'ctx')
- gain_grad: float32 [2048], P(('dp', 'ctx'))
The draws below stay inside these ranges and needn't reach their ends.
All inputs are finite; a program needn't handle non-finite values.
Results may differ from the reference program's by a relative error of at most 0.0065.
Values sent between devices are 32-bit elements; how exact they have to be, the bound alone decides.
A program may use at most 256 MiB of HBM per device.

```python
import math
import jax
import jax.numpy as jnp
from jax import lax

HEADS = 16
HEAD_DIM = 128
TOK_DEV = 128
HD = 2048
SEQLEN = 8192
BATCH = 4


def strengthened(entries, own_key, source, target, blocks, factor):
    def block_of(dim):
        return (jnp.arange(entries.shape[dim]) // (entries.shape[dim] // blocks)).reshape((-1,) + (1,) * (entries.ndim - 1 - dim))

    first = jax.random.permutation(own_key, blocks)[block_of(target)]
    other_side = (block_of(target) + blocks // 2) % blocks
    return jnp.where((block_of(source) == first) | (block_of(source) == other_side), factor * entries, entries)


def levels(own_key, dims, pieces, least, high):
    def one(dim, blocks):
        draws = jax.random.uniform(jax.random.fold_in(jax.random.fold_in(own_key, 6), dim), (blocks,), jnp.float32, least / len(pieces), high / len(pieces))
        return jnp.repeat(jnp.exp(draws), dims[dim] // blocks).reshape((-1,) + (1,) * (len(dims) - dim - 1))

    gain = one(*pieces[0])
    for cut in pieces[1:]:
        gain = gain * one(*cut)
    return gain


def gaussian(own_key, dims, width, reach, shards=(), held_as=jnp.bfloat16):
    level = levels(own_key, dims, shards, -0.22, 0.18) if shards else 1.0
    drawn = jax.random.normal(own_key, dims, jnp.float32) * width * level
    return jnp.minimum(jnp.maximum(drawn, -reach), reach).astype(held_as)


def noise_with(rng, shape, deviation, bound, cuts, heavy, held_as=jnp.bfloat16):
    drawn = deviation * jax.random.normal(rng, shape, jnp.float32)
    if cuts:
        drawn = drawn * levels(rng, shape, cuts, -0.22, 0.18)
    return jnp.clip(strengthened(drawn, jax.random.fold_in(rng, 3), *heavy), -bound, bound).astype(held_as)


def setup_inputs(seed: int = 0) -> dict:
    seeds = jax.random.split(jax.random.key(seed), 6)
    queries = gaussian(seeds[0], (BATCH, SEQLEN, HD), 1.0, 6.0, ((0, 4), (1, 64)))
    key_rows = gaussian(seeds[1], (BATCH, SEQLEN, HD), 1.0, 6.0, ((0, 4), (1, 64)))
    value_rows = gaussian(seeds[2], (BATCH, SEQLEN, HD), 1.0, 6.0, ((0, 4), (1, 64)))
    out_grad = noise_with(seeds[3], (BATCH, SEQLEN, HD), 1.0, 8.0, ((0, 4), (1, 64)), (1, 2, 64, 4.0))
    norm_gain = jnp.clip(1.0 + 0.18 * jax.random.normal(seeds[4], (HD,), jnp.float32), 0.1, 1.9)
    return dict(queries=queries, key_rows=key_rows, value_rows=value_rows, out_grad=out_grad, norm_gain=norm_gain)


EPSILON = 1e-05
BLOCK_ROWS = 512

def masked_scores(left_rows, right_rows):
    length = left_rows.shape[0]
    step_rows = min(BLOCK_ROWS, length)
    row_blocks = []
    for start in range(0, length, step_rows):
        stop = start + step_rows
        left_part = left_rows[start:stop].astype(jnp.float32)
        right_part = right_rows[:stop].astype(jnp.float32)
        products = jnp.einsum('lhe,mhe->hlm', left_part, right_part)
        rows_idx = start + lax.broadcasted_iota(jnp.int32, (step_rows, stop), 0)
        cols_idx = lax.broadcasted_iota(jnp.int32, (step_rows, stop), 1)
        kept = jnp.where((cols_idx <= rows_idx)[None], products, 0.0).astype(jnp.bfloat16)
        if stop < length:
            kept = jnp.concatenate([kept, jnp.zeros((kept.shape[0], step_rows, length - stop), jnp.bfloat16)], axis=2)
        row_blocks.append(kept)
    return jnp.concatenate(row_blocks, axis=1)

def first_pass(queries, key_rows, value_rows, out_grad, gain_heads, prior_state):
    scores_low = masked_scores(queries, key_rows)
    prior_low = prior_state.astype(jnp.bfloat16)
    output = jnp.einsum('hlm,mhf->lhf', scores_low.astype(jnp.float32), value_rows.astype(jnp.float32))
    output = output + jnp.einsum('lhe,hef->lhf', queries.astype(jnp.float32), prior_low.astype(jnp.float32))
    root_mean = jnp.sqrt(lax.optimization_barrier(jnp.mean(output * output, axis=-1, keepdims=True)) + EPSILON)
    normed = output / root_mean
    grad_float = out_grad.astype(jnp.float32)
    grad_normed = grad_float * gain_heads
    grad_output = ((grad_normed - normed * lax.optimization_barrier(jnp.mean(grad_normed * normed, axis=-1, keepdims=True))) / root_mean).astype(jnp.bfloat16)
    gain_term = lax.optimization_barrier(jnp.sum(grad_float * normed, axis=0))
    grad_local = jnp.einsum('lhe,lhf->hef', queries.astype(jnp.float32), grad_output.astype(jnp.float32))
    return (grad_output, grad_local, gain_term)

def second_pass(queries, key_rows, value_rows, grad_output, prior_state, later_state):
    scores_low = masked_scores(queries, key_rows).astype(jnp.float32)
    grad_scores = masked_scores(grad_output, value_rows).astype(jnp.float32)
    prior_low = prior_state.astype(jnp.bfloat16).astype(jnp.float32)
    later_low = later_state.astype(jnp.bfloat16).astype(jnp.float32)
    q_f = queries.astype(jnp.float32)
    k_f = key_rows.astype(jnp.float32)
    v_f = value_rows.astype(jnp.float32)
    d_f = grad_output.astype(jnp.float32)
    query_grad = jnp.einsum('hlm,mhe->lhe', grad_scores, k_f) + jnp.einsum('lhf,hef->lhe', d_f, prior_low)
    key_grad = jnp.einsum('hlm,lhe->mhe', grad_scores, q_f) + jnp.einsum('mhf,hef->mhe', v_f, later_low)
    value_grad = jnp.einsum('hlm,lhf->mhf', scores_low, d_f) + jnp.einsum('mhe,hef->mhf', k_f, later_low)
    return (query_grad.astype(jnp.bfloat16), key_grad.astype(jnp.bfloat16), value_grad.astype(jnp.bfloat16))

def reference(queries, key_rows, value_rows, out_grad, norm_gain):
    blocks = SEQLEN // TOK_DEV
    gain_heads = norm_gain.reshape(HEADS, HEAD_DIM)

    def to_blocks(array):
        return array.reshape(BATCH, blocks, TOK_DEV, HEADS, HEAD_DIM)

    def one_sequence(sequence_items):
        q_all, k_all, v_all, g_all = sequence_items

        def local_state(rows_pair):
            return jnp.einsum('lhe,lhf->hef', rows_pair[0].astype(jnp.float32), rows_pair[1].astype(jnp.float32))
        kv_local = lax.map(local_state, (k_all, v_all))
        zero_state = jnp.zeros((1, HEADS, HEAD_DIM, HEAD_DIM), jnp.float32)
        prior_all = jnp.concatenate([zero_state, jnp.cumsum(kv_local, axis=0)[:-1]], axis=0)

        def pass_one(block_items):
            return first_pass(block_items[0], block_items[1], block_items[2], block_items[3], gain_heads, block_items[4])
        grad_outs, grad_locals, gain_terms = lax.map(pass_one, (q_all, k_all, v_all, g_all, prior_all))
        suffix = jnp.cumsum(grad_locals[::-1], axis=0)[::-1]
        later_all = jnp.concatenate([suffix[1:], zero_state], axis=0)

        def pass_two(block_items):
            return second_pass(block_items[0], block_items[1], block_items[2], block_items[3], block_items[4], block_items[5])
        grads = lax.map(pass_two, (q_all, k_all, v_all, grad_outs, prior_all, later_all))
        return (grads[0], grads[1], grads[2], lax.optimization_barrier(jnp.sum(gain_terms, axis=0)))
    query_grad, key_grad, value_grad, gain_terms = lax.map(one_sequence, (to_blocks(queries), to_blocks(key_rows), to_blocks(value_rows), to_blocks(out_grad)))
    shape_out = (BATCH, SEQLEN, HEADS * HEAD_DIM)
    gain_grad = lax.optimization_barrier(jnp.sum(gain_terms, axis=0)).reshape(HEADS * HEAD_DIM) / math.sqrt(BATCH * SEQLEN)
    return (query_grad.reshape(shape_out), key_grad.reshape(shape_out), value_grad.reshape(shape_out), gain_grad)
```

```python
import functools
import math

import jax
import jax.numpy as jnp
from jax import lax
from jax.experimental import pallas as pl
from jax.experimental.pallas import tpu as pltpu
from jax.sharding import PartitionSpec as P

HEADS = 16
HALF = 8
DIM = 128
EPSILON = 1e-05
MESH = pl.DeviceIdType.MESH
F32 = jnp.float32
BF16 = jnp.bfloat16

CH = 2
HOP = 3
LAG = 2
ROWS = DIM // CH
CHUNKS = HALF * CH


def dot(a, b, ca, cb):
    return lax.dot_general(a, b, (((ca,), (cb,)), ((), ())), preferred_element_type=F32)


class Scan:
    def __init__(self, sizes, pos, order, bufs, sems):
        self.nx, self.nz = sizes
        self.y, self.x, self.z, self.c = pos
        self.order = order
        if order > 0:
            self.px, self.pz, self.pc = self.x, self.z, self.c
        else:
            self.px, self.pz, self.pc = self.nx - 1 - self.x, self.nz - 1 - self.z, 1 - self.c
        (self.own, self.exch, self.xin, self.a, self.upin, self.upout, self.dnin, self.dnout, self.bkin, self.bkout) = bufs
        self.re, self.rx, self.ru, self.rd, self.rb, self.sends = sems

    def device(self, x, z, c):
        return (self.y, (x * self.nz + z) * 2 + c)

    def partner(self):
        return self.device(self.x, self.z, 1 - self.c)

    def remote(self, src, dst, which, recv, to):
        return pltpu.make_async_remote_copy(
            src_ref=src, dst_ref=dst, send_sem=self.sends.at[which], recv_sem=recv, device_id=to, device_id_type=MESH
        )

    def exch_copy(self, m):
        src = self.own.at[pl.ds(((1 - self.c) * HALF + m) * CH, CH)]
        return self.remote(src, self.exch.at[pl.ds(m * CH, CH)], 0, self.re.at[m], self.partner())

    def x_copy(self, j):
        return self.remote(
            self.a.at[j], self.xin.at[j], 1, self.rx.at[j], self.device(self.x + self.order, self.z, self.c)
        )

    def up_copy(self, src, j):
        return self.remote(
            src.at[j], self.upin.at[j], 2, self.ru.at[j], self.device(self.x, self.z + self.order, self.c)
        )

    def dn_copy(self, src, j):
        return self.remote(
            src.at[j], self.dnin.at[j], 3, self.rd.at[j], self.device(self.x, self.z - self.order, self.c)
        )

    def bk_copy(self, m):
        part = pl.ds(m * CH, CH)
        return self.remote(self.bkout.at[part], self.bkin.at[part], 4, self.rb.at[m], self.partner())

    def clear(self):
        @pl.when(self.px == 0)
        def _():
            self.xin[...] = jnp.zeros(self.xin.shape, F32)

        @pl.when(self.pz == 0)
        def _():
            self.upin[...] = jnp.zeros(self.upin.shape, F32)

        @pl.when((self.px == 0) | (self.pz == self.nz - 1))
        def _():
            self.dnin[...] = jnp.zeros(self.dnin.shape, F32)

    def along_x(self, j):
        @pl.when(j % CH == 0)
        def _():
            self.exch_copy(j // CH).wait_recv()

        @pl.when(self.px > 0)
        def _():
            self.x_copy(j).wait_recv()

        self.a[j] = self.own[self.c * CHUNKS + j] + self.exch[j] + self.xin[j]

        @pl.when(self.px < self.nx - 1)
        def _():
            self.x_copy(j).start()

        @pl.when(self.pz == 0)
        def _():
            self.up_copy(self.a, j).start()

        @pl.when((self.pz == self.nz - 1) & (self.px > 0))
        def _():
            self.dn_copy(self.xin, j).start()

    def up(self, j):
        self.up_copy(self.upout, j).wait_recv()

        @pl.when(self.pz < self.nz - 1)
        def _():
            self.upout[j] = self.upin[j] + self.a[j]
            self.up_copy(self.upout, j).start()

    def down(self, j):
        self.dn_copy(self.dnout, j).wait_recv()

        @pl.when(self.pz > 0)
        def _():
            self.dnout[j] = self.dnin[j] + self.xin[j]
            self.dn_copy(self.dnout, j).start()

    def forward(self, t):
        jx = t - HOP * self.px
        ju = jx - HOP * self.pz
        jd = jx - HOP * (self.nz - 1 - self.pz)

        @pl.when((jx >= 0) & (jx < CHUNKS))
        def _():
            self.along_x(jx)

        @pl.when((ju >= 0) & (ju < CHUNKS) & (self.pz > 0))
        def _():
            self.up(ju)

        @pl.when((jd >= 0) & (jd < CHUNKS) & (self.pz < self.nz - 1) & (self.px > 0))
        def _():
            self.down(jd)

    def finish(self, m):
        part = pl.ds(m * CH, CH)
        before = (self.upin[part] + self.xin[part] + self.dnin[part]).reshape(DIM, DIM)
        first = self.own[pl.ds(self.c * CHUNKS + m * CH, CH)].reshape(DIM, DIM)
        second = self.exch[part].reshape(DIM, DIM)
        self.bkout[part] = jnp.where(self.pc == 0, before + first, before).reshape(CH, ROWS, DIM)
        self.bk_copy(m).start()
        return jnp.where(self.pc == 1, before + second, before)

    def finished(self, m):
        self.bk_copy(m).wait_recv()
        return self.bkin[pl.ds(m * CH, CH)].reshape(DIM, DIM)

    def drain(self):
        whole = self.exch
        self.remote(whole, whole, 0, self.re.at[0], self.partner()).wait_send()
        self.remote(whole, whole, 4, self.rb.at[0], self.partner()).wait_send()

        @pl.when(self.px < self.nx - 1)
        def _():
            self.remote(whole, whole, 1, self.rx.at[0], self.partner()).wait_send()

        @pl.when(self.pz < self.nz - 1)
        def _():
            self.remote(whole, whole, 2, self.ru.at[0], self.partner()).wait_send()

        @pl.when((self.pz > 0) & (self.px > 0))
        def _():
            self.remote(whole, whole, 3, self.rd.at[0], self.partner()).wait_send()


def kernel(
    sizes,
    q_hbm,
    k_hbm,
    v_hbm,
    g_hbm,
    gain_ref,
    dq_hbm,
    dk_hbm,
    dv_hbm,
    dgain_ref,
    *scratch,
):
    ny, nx, nz = sizes
    scratch = list(scratch)

    def take(n):
        out = scratch[:n]
        del scratch[:n]
        return out

    q, k, v, g = take(4)
    dq, dk, dv = take(3)
    scores, d_out, prior = take(3)
    out_loc, dk_loc, dv_loc = take(3)
    gtile, gin1, acc1, gin2, acc2, gin3, acc3, gin4 = take(8)
    bufs1, sems1 = take(10), take(6)
    bufs2, sems2 = take(10), take(6)
    in_sem, out_sem, gsend, g1r, g2r, g3r, g4r = take(7)

    y = lax.axis_index("dp")
    ctx = lax.axis_index("ctx")
    x = ctx // (2 * nz)
    z = (ctx // 2) % nz
    c = ctx % 2
    pos = (y, x, z, c)

    def device(y_, x_, z_, c_):
        return (y_, (x_ * nz + z_) * 2 + c_)

    loads = [pltpu.make_async_copy(src.at[0], dst, in_sem.at[i]) for i, (src, dst) in enumerate(((k_hbm, k), (v_hbm, v), (q_hbm, q), (g_hbm, g)))]
    for load in loads:
        load.start()

    def y_peer(i):
        return device((y + i) % ny, x, z, c)

    def x_peer(i):
        return device(y, (x + i) % nx, z, c)

    def z_peer(i):
        return device(y, x, (z + i) % nz, c)

    partner = device(y, x, z, 1 - c)
    barrier = pltpu.get_barrier_semaphore()
    pl.semaphore_signal(barrier, inc=1, device_id=partner, device_id_type=MESH)
    for count, peer in ((ny, y_peer), (nx, x_peer), (nz, z_peer)):
        for i in range(1, count):
            pl.semaphore_signal(barrier, inc=1, device_id=peer(i), device_id_type=MESH)

    one = Scan((nx, nz), pos, 1, bufs1, sems1)
    two = Scan((nx, nz), pos, -1, bufs2, sems2)
    one.clear()
    two.clear()

    def col(h):
        return pl.ds(pl.multiple_of(h * DIM, DIM), DIM)

    mine, other = c * HALF, (1 - c) * HALF

    def columns(ref, heads):
        return [ref[:, col(h)] for h in heads]

    def local_states(heads):
        ks, vs = columns(k, heads), columns(v, heads)
        states = [dot(kh, vh, 0, 0) for kh, vh in zip(ks, vs)]
        for h, state in zip(heads, states):
            one.own[pl.ds(h * CH, CH)] = state.reshape(CH, ROWS, DIM)

    loads[0].wait()
    loads[1].wait()

    for i in range(0, HALF, 4):
        local_states([other + i + u for u in range(4)])
        if i == 0:
            pl.semaphore_wait(barrier, ny + nx + nz - 2)
        for u in range(4):
            one.exch_copy(i + u).start()

    @pl.loop(0, HALF // 4)
    def _(i):
        local_states([mine + i * 4 + u for u in range(4)])

    loads[2].wait()
    loads[3].wait()

    keep = lax.broadcasted_iota(jnp.int32, (DIM, DIM), 0) >= lax.broadcasted_iota(jnp.int32, (DIM, DIM), 1)

    def before_one(heads):
        qs, ks, vs = columns(q, heads), columns(k, heads), columns(v, heads)
        raw = [dot(qh, kh, 1, 1) for qh, kh in zip(qs, ks)]
        lows = [jnp.where(keep, r, 0.0).astype(BF16) for r in raw]
        outs = [dot(low, vh, 1, 0) for low, vh in zip(lows, vs)]
        for h, low, out in zip(heads, lows, outs):
            scores[h] = low
            out_loc[h] = out

    def pass_one(heads, states):
        qs = columns(q, heads)
        gfs = [gh.astype(F32) for gh in columns(g, heads)]
        gains = columns(gain_ref, heads)
        locs = [out_loc[h] for h in heads]
        lows = [state.astype(BF16) for state in states]
        outs = [loc + dot(qh, low, 1, 0) for loc, qh, low in zip(locs, qs, lows)]
        invs = [lax.rsqrt(jnp.mean(out * out, axis=1, keepdims=True) + EPSILON) for out in outs]
        normeds = [out * inv for out, inv in zip(outs, invs)]
        gns = [gf * gain for gf, gain in zip(gfs, gains)]
        means = [jnp.mean(gn * normed, axis=1, keepdims=True) for gn, normed in zip(gns, normeds)]
        ds = [((gn - normed * mean) * inv).astype(BF16) for gn, normed, mean, inv in zip(gns, normeds, means, invs)]
        grads = [dot(qh, d, 0, 0) for qh, d in zip(qs, ds)]
        terms = [jnp.sum((gf * normed).reshape(DIM // 8, 8, DIM), axis=0) for gf, normed in zip(gfs, normeds)]
        for h, low, d, grad, term in zip(heads, lows, ds, grads, terms):
            prior[h] = low
            d_out[h] = d
            two.own[pl.ds(h * CH, CH)] = grad.reshape(CH, ROWS, DIM)
            gtile[h] = term

    def between(heads):
        ds, lows, scs = [d_out[h] for h in heads], [prior[h] for h in heads], [scores[h] for h in heads]
        qs, ks, vs = columns(q, heads), columns(k, heads), columns(v, heads)
        raw = [dot(d, vh, 1, 1) for d, vh in zip(ds, vs)]
        dvs = [dot(sc, d, 0, 0) for sc, d in zip(scs, ds)]
        pqs = [dot(d, low, 1, 1) for d, low in zip(ds, lows)]
        gss = [jnp.where(keep, r, 0.0).astype(BF16) for r in raw]
        dqs = [(dot(gs, kh, 1, 0) + pq).astype(BF16) for gs, kh, pq in zip(gss, ks, pqs)]
        dks = [dot(gs, qh, 0, 0) for gs, qh in zip(gss, qs)]
        for h, dqh, dkh, dvh in zip(heads, dqs, dks, dvs):
            dq[:, col(h)] = dqh
            dk_loc[h] = dkh
            dv_loc[h] = dvh

    def store(ref, hbm, i, h):
        return pltpu.make_async_copy(ref.at[:, col(h)], hbm.at[0, :, col(h)], out_sem.at[i])

    def pass_two(heads, states):
        ks, vs = columns(k, heads), columns(v, heads)
        dks, dvs = [dk_loc[h] for h in heads], [dv_loc[h] for h in heads]
        lows = [state.astype(BF16) for state in states]
        dks = [(part + dot(vh, low, 1, 1)).astype(BF16) for part, vh, low in zip(dks, vs, lows)]
        dvs = [(part + dot(kh, low, 1, 0)).astype(BF16) for part, kh, low in zip(dvs, ks, lows)]
        for h, dkh, dvh in zip(heads, dks, dvs):
            dk[:, col(h)] = dkh
            dv[:, col(h)] = dvh
        for h in heads:
            store(dk, dk_hbm, 1, h).start()
            store(dv, dv_hbm, 2, h).start()

    ry, rx = HEADS // ny, HEADS // ny // nx

    def g1_copy(i):
        src = gtile.at[pl.ds(((y + i) % ny) * ry, ry)]
        return pltpu.make_async_remote_copy(
            src_ref=src, dst_ref=gin1.at[i - 1], send_sem=gsend.at[0], recv_sem=g1r.at[i - 1], device_id=y_peer(i), device_id_type=MESH
        )

    def g2_copy(i):
        src = acc1.at[pl.ds(((x + i) % nx) * rx, rx)]
        return pltpu.make_async_remote_copy(
            src_ref=src, dst_ref=gin2.at[i - 1], send_sem=gsend.at[1], recv_sem=g2r.at[i - 1], device_id=x_peer(i), device_id_type=MESH
        )

    def g3_copy(i):
        return pltpu.make_async_remote_copy(
            src_ref=acc2, dst_ref=gin3.at[i - 1], send_sem=gsend.at[2], recv_sem=g3r.at[i - 1], device_id=z_peer(i), device_id_type=MESH
        )

    def g4_copy():
        return pltpu.make_async_remote_copy(
            src_ref=acc3, dst_ref=gin4, send_sem=gsend.at[3], recv_sem=g4r, device_id=partner, device_id_type=MESH
        )

    def gain_step(stage):
        if stage == 0:
            for i in range(1, ny):
                g1_copy(i).start()
        elif stage == 1:
            total = gtile[pl.ds(y * ry, ry)]
            for i in range(1, ny):
                g1_copy(i).wait_recv()
                total = total + gin1[i - 1]
            acc1[...] = total
            for i in range(1, nx):
                g2_copy(i).start()
        elif stage == 2:
            total = acc1[pl.ds(x * rx, rx)]
            for i in range(1, nx):
                g2_copy(i).wait_recv()
                total = total + gin2[i - 1]
            acc2[...] = total
            for i in range(1, nz):
                g3_copy(i).start()
        elif stage == 3:
            total = acc2[...]
            for i in range(1, nz):
                g3_copy(i).wait_recv()
                total = total + gin3[i - 1]
            acc3[...] = total
            g4_copy().start()
        else:
            g4_copy().wait_recv()
            scale = 1.0 / math.sqrt(ny * nx * nz * 2 * DIM)
            dgain_ref[...] = jnp.sum(acc3[...] + gin4[...], axis=1) * scale

    span = HOP * (nz - 1)
    row1 = HOP * x + span + CH - 1
    begin2 = HOP * (nx - 1) + span + CH - 1 + CH * LAG + HOP
    row2 = begin2 + HOP * (nx - 1 - x) + span + CH - 1
    gain_begin = HOP * (nx - 1) + span + CHUNKS + CH * LAG
    steps = begin2 + HOP * (nx - 1) + span + CHUNKS + CH * LAG

    def finishing(first, s, scan, work, after):
        f = s - first
        m = f // CH

        @pl.when((f >= 0) & (f % CH == 0) & (m < LAG))
        def _():
            work([mine + m], [scan.finish(m)])

        @pl.when((f % CH == 0) & (m >= LAG) & (m < HALF))
        def _():
            state = scan.finish(m)
            work([mine + m, other + m - LAG], [state, scan.finished(m - LAG)])
            after(m - LAG)

        @pl.when((f % CH == 0) & (m >= HALF) & (m < HALF + LAG))
        def _():
            work([other + m - LAG], [scan.finished(m - LAG)])
            after(m - LAG)

    def swap_two(m):
        two.exch_copy(m).start()

    def nothing(m):
        pass

    @pl.loop(0, steps)
    def _(s):
        one.forward(s)
        two.forward(s - begin2)
        finishing(row1, s, one, pass_one, swap_two)
        finishing(row2, s, two, pass_two, nothing)

        @pl.when((s < CHUNKS) & (s % CH == 0))
        def _():
            m = s // CH
            before_one([mine + m, other + m])

        mid = s - (row1 + CHUNKS + CH * LAG)

        @pl.when((mid >= 0) & (mid < CHUNKS) & (mid % CH == 0))
        def _():
            m = mid // CH
            between([mine + m, other + m])

        @pl.when(mid == CHUNKS)
        def _():
            pltpu.make_async_copy(dq, dq_hbm.at[0], out_sem.at[0]).start()

        for stage in range(5):

            @pl.when(s == gain_begin + 4 * stage)
            def _(stage=stage):
                gain_step(stage)

    one.drain()
    two.drain()
    for i in range(1, ny):
        g1_copy(i).wait_send()
    for i in range(1, nx):
        g2_copy(i).wait_send()
    for i in range(1, nz):
        g3_copy(i).wait_send()
    g4_copy().wait_send()
    for i, (ref, hbm) in enumerate(((dq, dq_hbm), (dk, dk_hbm), (dv, dv_hbm))):
        pltpu.make_async_copy(ref, hbm.at[0], out_sem.at[i]).wait()


def build(mesh, nx, nz):
    ny = mesh.shape["dp"]
    width = HEADS * DIM
    ry, rx = HEADS // ny, HEADS // ny // nx

    def scan_scratch():
        state = pltpu.VMEM((CHUNKS, ROWS, DIM), F32)
        return [
            pltpu.VMEM((2 * CHUNKS, ROWS, DIM), F32),
            *[state] * 9,
            pltpu.SemaphoreType.DMA((HALF,)),
            *[pltpu.SemaphoreType.DMA((CHUNKS,))] * 3,
            pltpu.SemaphoreType.DMA((HALF,)),
            pltpu.SemaphoreType.DMA((5,)),
        ]

    scratch = [
        *[pltpu.VMEM((DIM, width), BF16)] * 7,
        *[pltpu.VMEM((HEADS, DIM, DIM), BF16)] * 3,
        *[pltpu.VMEM((HEADS, DIM, DIM), F32)] * 3,
        pltpu.VMEM((HEADS, 8, DIM), F32),
        pltpu.VMEM((ny - 1, ry, 8, DIM), F32),
        pltpu.VMEM((ry, 8, DIM), F32),
        pltpu.VMEM((nx - 1, rx, 8, DIM), F32),
        pltpu.VMEM((rx, 8, DIM), F32),
        pltpu.VMEM((nz - 1, rx, 8, DIM), F32),
        pltpu.VMEM((rx, 8, DIM), F32),
        pltpu.VMEM((rx, 8, DIM), F32),
        *scan_scratch(),
        *scan_scratch(),
        pltpu.SemaphoreType.DMA((4,)),
        pltpu.SemaphoreType.DMA((3,)),
        pltpu.SemaphoreType.DMA((4,)),
        pltpu.SemaphoreType.DMA((ny - 1,)),
        pltpu.SemaphoreType.DMA((nx - 1,)),
        pltpu.SemaphoreType.DMA((nz - 1,)),
        pltpu.SemaphoreType.DMA,
    ]

    def body(queries, key_rows, value_rows, out_grad, norm_gain):
        rows = jax.ShapeDtypeStruct(queries.shape, BF16)
        dq, dk, dv, dgain = pl.pallas_call(
            functools.partial(kernel, (ny, nx, nz)),
            out_shape=(rows, rows, rows, jax.ShapeDtypeStruct((rx, DIM), F32)),
            in_specs=[pl.BlockSpec(memory_space=pl.ANY)] * 4 + [pl.BlockSpec(memory_space=pltpu.VMEM)],
            out_specs=[pl.BlockSpec(memory_space=pl.ANY)] * 3 + [pl.BlockSpec(memory_space=pltpu.VMEM)],
            scratch_shapes=scratch,
            compiler_params=pltpu.CompilerParams(
                collective_id=0, has_side_effects=True, vmem_limit_bytes=62 * 1024 * 1024
            ),
        )(queries, key_rows, value_rows, out_grad, norm_gain.reshape(1, width))
        share = rx * DIM // (2 * nz)
        place = lax.rem(lax.axis_index("ctx"), 2 * nz) * share
        return dq, dk, dv, lax.dynamic_slice(dgain.reshape(rx * DIM), (place,), (share,))

    placed = P("dp", "ctx", None)
    return jax.shard_map(
        body,
        mesh=mesh,
        in_specs=(placed, placed, placed, placed, P()),
        out_specs=(placed, placed, placed, P(("dp", "ctx"))),
        check_vma=False,
    )


def solution(mesh):
    return build(mesh, 4, 8)
```

```python
import functools
import math

import jax
import jax.numpy as jnp
from jax import lax
from jax.experimental import pallas as pl
from jax.experimental.pallas import tpu as pltpu
from jax.sharding import PartitionSpec as P

HEADS = 16
HALF = 8
DIM = 128
EPSILON = 1e-05
MESH = pl.DeviceIdType.MESH
F32 = jnp.float32
BF16 = jnp.bfloat16

CH = 2
HOP = 2
LAG = 2
ROWS = DIM // CH
CHUNKS = HALF * CH


def dot(a, b, ca, cb):
    return lax.dot_general(a, b, (((ca,), (cb,)), ((), ())), preferred_element_type=F32)


class Scan:
    def __init__(self, sizes, pos, order, bufs, sems):
        self.nx, self.nz = sizes
        self.y, self.x, self.z, self.c = pos
        self.order = order
        if order > 0:
            self.px, self.pz, self.pc = self.x, self.z, self.c
        else:
            self.px, self.pz, self.pc = self.nx - 1 - self.x, self.nz - 1 - self.z, 1 - self.c
        (self.own, self.exch, self.xin, self.a, self.upin, self.upout, self.dnin, self.dnout, self.bkin, self.bkout) = bufs
        self.re, self.rx, self.ru, self.rd, self.rb, self.sends = sems

    def device(self, x, z, c):
        return (self.y, (x * self.nz + z) * 2 + c)

    def partner(self):
        return self.device(self.x, self.z, 1 - self.c)

    def remote(self, src, dst, which, recv, to):
        return pltpu.make_async_remote_copy(
            src_ref=src, dst_ref=dst, send_sem=self.sends.at[which], recv_sem=recv, device_id=to, device_id_type=MESH
        )

    def exch_copy(self, m):
        src = self.own.at[pl.ds(((1 - self.c) * HALF + m) * CH, CH)]
        return self.remote(src, self.exch.at[pl.ds(m * CH, CH)], 0, self.re.at[m], self.partner())

    def x_copy(self, j):
        return self.remote(
            self.a.at[j], self.xin.at[j], 1, self.rx.at[j], self.device(self.x + self.order, self.z, self.c)
        )

    def up_copy(self, src, j):
        return self.remote(
            src.at[j], self.upin.at[j], 2, self.ru.at[j], self.device(self.x, self.z + self.order, self.c)
        )

    def dn_copy(self, src, j):
        return self.remote(
            src.at[j], self.dnin.at[j], 3, self.rd.at[j], self.device(self.x, self.z - self.order, self.c)
        )

    def bk_copy(self, m):
        part = pl.ds(m * CH, CH)
        return self.remote(self.bkout.at[part], self.bkin.at[part], 4, self.rb.at[m], self.partner())

    def clear(self):
        @pl.when(self.px == 0)
        def _():
            self.xin[...] = jnp.zeros(self.xin.shape, F32)

        @pl.when(self.pz == 0)
        def _():
            self.upin[...] = jnp.zeros(self.upin.shape, F32)

        @pl.when((self.px == 0) | (self.pz == self.nz - 1))
        def _():
            self.dnin[...] = jnp.zeros(self.dnin.shape, F32)

    def along_x(self, j):
        @pl.when(j % CH == 0)
        def _():
            self.exch_copy(j // CH).wait_recv()

        @pl.when(self.px > 0)
        def _():
            self.x_copy(j).wait_recv()

        self.a[j] = self.own[self.c * CHUNKS + j] + self.exch[j] + self.xin[j]

        @pl.when(self.px < self.nx - 1)
        def _():
            self.x_copy(j).start()

        @pl.when(self.pz == 0)
        def _():
            self.up_copy(self.a, j).start()

        @pl.when((self.pz == self.nz - 1) & (self.px > 0))
        def _():
            self.dn_copy(self.xin, j).start()

    def up(self, j):
        self.up_copy(self.upout, j).wait_recv()

        @pl.when(self.pz < self.nz - 1)
        def _():
            self.upout[j] = self.upin[j] + self.a[j]
            self.up_copy(self.upout, j).start()

    def down(self, j):
        self.dn_copy(self.dnout, j).wait_recv()

        @pl.when(self.pz > 0)
        def _():
            self.dnout[j] = self.dnin[j] + self.xin[j]
            self.dn_copy(self.dnout, j).start()

    def forward(self, t):
        jx = t - HOP * self.px
        ju = jx - HOP * self.pz
        jd = jx - HOP * (self.nz - 1 - self.pz)

        @pl.when((jx >= 0) & (jx < CHUNKS))
        def _():
            self.along_x(jx)

        @pl.when((ju >= 0) & (ju < CHUNKS) & (self.pz > 0))
        def _():
            self.up(ju)

        @pl.when((jd >= 0) & (jd < CHUNKS) & (self.pz < self.nz - 1) & (self.px > 0))
        def _():
            self.down(jd)

    def finish(self, m):
        part = pl.ds(m * CH, CH)
        before = (self.upin[part] + self.xin[part] + self.dnin[part]).reshape(DIM, DIM)
        first = self.own[pl.ds(self.c * CHUNKS + m * CH, CH)].reshape(DIM, DIM)
        second = self.exch[part].reshape(DIM, DIM)
        self.bkout[part] = jnp.where(self.pc == 0, before + first, before).reshape(CH, ROWS, DIM)
        self.bk_copy(m).start()
        return jnp.where(self.pc == 1, before + second, before)

    def finished(self, m):
        self.bk_copy(m).wait_recv()
        return self.bkin[pl.ds(m * CH, CH)].reshape(DIM, DIM)

    def drain(self):
        whole = self.exch
        self.remote(whole, whole, 0, self.re.at[0], self.partner()).wait_send()
        self.remote(whole, whole, 4, self.rb.at[0], self.partner()).wait_send()

        @pl.when(self.px < self.nx - 1)
        def _():
            self.remote(whole, whole, 1, self.rx.at[0], self.partner()).wait_send()

        @pl.when(self.pz < self.nz - 1)
        def _():
            self.remote(whole, whole, 2, self.ru.at[0], self.partner()).wait_send()

        @pl.when((self.pz > 0) & (self.px > 0))
        def _():
            self.remote(whole, whole, 3, self.rd.at[0], self.partner()).wait_send()


def kernel(
    sizes,
    q_hbm,
    k_hbm,
    v_hbm,
    g_hbm,
    gain_ref,
    dq_hbm,
    dk_hbm,
    dv_hbm,
    dgain_ref,
    *scratch,
):
    ny, nx, nz = sizes
    scratch = list(scratch)

    def take(n):
        out = scratch[:n]
        del scratch[:n]
        return out

    q, k, v, g = take(4)
    dq, dk, dv = take(3)
    scores, d_out, prior = take(3)
    out_loc, dk_loc, dv_loc = take(3)
    gtile, gin1, acc1, gin2, acc2, gin3, acc3, gin4 = take(8)
    bufs1, sems1 = take(10), take(6)
    bufs2, sems2 = take(10), take(6)
    in_sem, out_sem, gsend, g1r, g2r, g3r, g4r = take(7)

    y = lax.axis_index("dp")
    ctx = lax.axis_index("ctx")
    x = ctx // (2 * nz)
    z = (ctx // 2) % nz
    c = ctx % 2
    pos = (y, x, z, c)

    def device(y_, x_, z_, c_):
        return (y_, (x_ * nz + z_) * 2 + c_)

    loads = [pltpu.make_async_copy(src.at[0], dst, in_sem.at[i]) for i, (src, dst) in enumerate(((k_hbm, k), (v_hbm, v), (q_hbm, q), (g_hbm, g)))]
    for load in loads:
        load.start()

    def y_peer(i):
        return device((y + i) % ny, x, z, c)

    def x_peer(i):
        return device(y, (x + i) % nx, z, c)

    def z_peer(i):
        return device(y, x, (z + i) % nz, c)

    partner = device(y, x, z, 1 - c)
    barrier = pltpu.get_barrier_semaphore()
    pl.semaphore_signal(barrier, inc=1, device_id=partner, device_id_type=MESH)
    for count, peer in ((ny, y_peer), (nx, x_peer), (nz, z_peer)):
        for i in range(1, count):
            pl.semaphore_signal(barrier, inc=1, device_id=peer(i), device_id_type=MESH)

    one = Scan((nx, nz), pos, 1, bufs1, sems1)
    two = Scan((nx, nz), pos, -1, bufs2, sems2)
    one.clear()
    two.clear()

    def col(h):
        return pl.ds(pl.multiple_of(h * DIM, DIM), DIM)

    mine, other = c * HALF, (1 - c) * HALF

    def columns(ref, heads):
        return [ref[:, col(h)] for h in heads]

    def local_states(heads):
        ks, vs = columns(k, heads), columns(v, heads)
        states = [dot(kh, vh, 0, 0) for kh, vh in zip(ks, vs)]
        for h, state in zip(heads, states):
            one.own[pl.ds(h * CH, CH)] = state.reshape(CH, ROWS, DIM)

    loads[0].wait()
    loads[1].wait()

    for i in range(0, HALF, 4):
        local_states([other + i + u for u in range(4)])
        if i == 0:
            pl.semaphore_wait(barrier, ny + nx + nz - 2)
        for u in range(4):
            one.exch_copy(i + u).start()

    @pl.loop(0, HALF // 4)
    def _(i):
        local_states([mine + i * 4 + u for u in range(4)])

    loads[2].wait()
    loads[3].wait()

    keep = lax.broadcasted_iota(jnp.int32, (DIM, DIM), 0) >= lax.broadcasted_iota(jnp.int32, (DIM, DIM), 1)

    def before_one(heads):
        qs, ks, vs = columns(q, heads), columns(k, heads), columns(v, heads)
        raw = [dot(qh, kh, 1, 1) for qh, kh in zip(qs, ks)]
        lows = [jnp.where(keep, r, 0.0).astype(BF16) for r in raw]
        outs = [dot(low, vh, 1, 0) for low, vh in zip(lows, vs)]
        for h, low, out in zip(heads, lows, outs):
            scores[h] = low
            out_loc[h] = out

    def pass_one(heads, states):
        qs = columns(q, heads)
        gfs = [gh.astype(F32) for gh in columns(g, heads)]
        gains = columns(gain_ref, heads)
        locs = [out_loc[h] for h in heads]
        lows = [state.astype(BF16) for state in states]
        outs = [loc + dot(qh, low, 1, 0) for loc, qh, low in zip(locs, qs, lows)]
        invs = [lax.rsqrt(jnp.mean(out * out, axis=1, keepdims=True) + EPSILON) for out in outs]
        normeds = [out * inv for out, inv in zip(outs, invs)]
        gns = [gf * gain for gf, gain in zip(gfs, gains)]
        means = [jnp.mean(gn * normed, axis=1, keepdims=True) for gn, normed in zip(gns, normeds)]
        ds = [((gn - normed * mean) * inv).astype(BF16) for gn, normed, mean, inv in zip(gns, normeds, means, invs)]
        grads = [dot(qh, d, 0, 0) for qh, d in zip(qs, ds)]
        terms = [jnp.sum((gf * normed).reshape(DIM // 8, 8, DIM), axis=0) for gf, normed in zip(gfs, normeds)]
        for h, low, d, grad, term in zip(heads, lows, ds, grads, terms):
            prior[h] = low
            d_out[h] = d
            two.own[pl.ds(h * CH, CH)] = grad.reshape(CH, ROWS, DIM)
            gtile[h] = term

    def between(heads):
        ds, lows, scs = [d_out[h] for h in heads], [prior[h] for h in heads], [scores[h] for h in heads]
        qs, ks, vs = columns(q, heads), columns(k, heads), columns(v, heads)
        raw = [dot(d, vh, 1, 1) for d, vh in zip(ds, vs)]
        dvs = [dot(sc, d, 0, 0) for sc, d in zip(scs, ds)]
        pqs = [dot(d, low, 1, 1) for d, low in zip(ds, lows)]
        gss = [jnp.where(keep, r, 0.0).astype(BF16) for r in raw]
        dqs = [(dot(gs, kh, 1, 0) + pq).astype(BF16) for gs, kh, pq in zip(gss, ks, pqs)]
        dks = [dot(gs, qh, 0, 0) for gs, qh in zip(gss, qs)]
        for h, dqh, dkh, dvh in zip(heads, dqs, dks, dvs):
            dq[:, col(h)] = dqh
            dk_loc[h] = dkh
            dv_loc[h] = dvh

    def store(ref, hbm, i, h):
        return pltpu.make_async_copy(ref.at[:, col(h)], hbm.at[0, :, col(h)], out_sem.at[i])

    def pass_two(heads, states):
        ks, vs = columns(k, heads), columns(v, heads)
        dks, dvs = [dk_loc[h] for h in heads], [dv_loc[h] for h in heads]
        lows = [state.astype(BF16) for state in states]
        dks = [(part + dot(vh, low, 1, 1)).astype(BF16) for part, vh, low in zip(dks, vs, lows)]
        dvs = [(part + dot(kh, low, 1, 0)).astype(BF16) for part, kh, low in zip(dvs, ks, lows)]
        for h, dkh, dvh in zip(heads, dks, dvs):
            dk[:, col(h)] = dkh
            dv[:, col(h)] = dvh
        for h in heads:
            store(dk, dk_hbm, 1, h).start()
            store(dv, dv_hbm, 2, h).start()

    ry, rx = HEADS // ny, HEADS // ny // nx

    def g1_copy(i):
        src = gtile.at[pl.ds(((y + i) % ny) * ry, ry)]
        return pltpu.make_async_remote_copy(
            src_ref=src, dst_ref=gin1.at[i - 1], send_sem=gsend.at[0], recv_sem=g1r.at[i - 1], device_id=y_peer(i), device_id_type=MESH
        )

    def g2_copy(i):
        src = acc1.at[pl.ds(((x + i) % nx) * rx, rx)]
        return pltpu.make_async_remote_copy(
            src_ref=src, dst_ref=gin2.at[i - 1], send_sem=gsend.at[1], recv_sem=g2r.at[i - 1], device_id=x_peer(i), device_id_type=MESH
        )

    def g3_copy(i):
        return pltpu.make_async_remote_copy(
            src_ref=acc2, dst_ref=gin3.at[i - 1], send_sem=gsend.at[2], recv_sem=g3r.at[i - 1], device_id=z_peer(i), device_id_type=MESH
        )

    def g4_copy():
        return pltpu.make_async_remote_copy(
            src_ref=acc3, dst_ref=gin4, send_sem=gsend.at[3], recv_sem=g4r, device_id=partner, device_id_type=MESH
        )

    def gain_step(stage):
        if stage == 0:
            for i in range(1, ny):
                g1_copy(i).start()
        elif stage == 1:
            total = gtile[pl.ds(y * ry, ry)]
            for i in range(1, ny):
                g1_copy(i).wait_recv()
                total = total + gin1[i - 1]
            acc1[...] = total
            for i in range(1, nx):
                g2_copy(i).start()
        elif stage == 2:
            total = acc1[pl.ds(x * rx, rx)]
            for i in range(1, nx):
                g2_copy(i).wait_recv()
                total = total + gin2[i - 1]
            acc2[...] = total
            for i in range(1, nz):
                g3_copy(i).start()
        elif stage == 3:
            total = acc2[...]
            for i in range(1, nz):
                g3_copy(i).wait_recv()
                total = total + gin3[i - 1]
            acc3[...] = total
            g4_copy().start()
        else:
            g4_copy().wait_recv()
            scale = 1.0 / math.sqrt(ny * nx * nz * 2 * DIM)
            dgain_ref[...] = jnp.sum(acc3[...] + gin4[...], axis=1) * scale

    span = HOP * (nz - 1)
    row1 = HOP * x + span + CH - 1
    begin2 = HOP * (nx - 1) + span + CH - 1 + CH * LAG + HOP
    row2 = begin2 + HOP * (nx - 1 - x) + span + CH - 1
    gain_begin = HOP * (nx - 1) + span + CHUNKS + CH * LAG
    steps = begin2 + HOP * (nx - 1) + span + CHUNKS + CH * LAG

    def finishing(first, s, scan, work, after):
        f = s - first
        m = f // CH

        @pl.when((f >= 0) & (f % CH == 0) & (m < LAG))
        def _():
            work([mine + m], [scan.finish(m)])

        @pl.when((f % CH == 0) & (m >= LAG) & (m < HALF))
        def _():
            state = scan.finish(m)
            work([mine + m, other + m - LAG], [state, scan.finished(m - LAG)])
            after(m - LAG)

        @pl.when((f % CH == 0) & (m >= HALF) & (m < HALF + LAG))
        def _():
            work([other + m - LAG], [scan.finished(m - LAG)])
            after(m - LAG)

    def swap_two(m):
        two.exch_copy(m).start()

    def nothing(m):
        pass

    @pl.loop(0, steps)
    def _(s):
        one.forward(s)
        two.forward(s - begin2)
        finishing(row1, s, one, pass_one, swap_two)
        finishing(row2, s, two, pass_two, nothing)

        @pl.when((s < CHUNKS) & (s % CH == 0))
        def _():
            m = s // CH
            before_one([mine + m, other + m])

        mid = s - (row1 + CHUNKS + CH * LAG)

        @pl.when((mid >= 0) & (mid < CHUNKS) & (mid % CH == 0))
        def _():
            m = mid // CH
            between([mine + m, other + m])

        @pl.when(mid == CHUNKS)
        def _():
            pltpu.make_async_copy(dq, dq_hbm.at[0], out_sem.at[0]).start()

        for stage in range(5):

            @pl.when(s == gain_begin + 4 * stage)
            def _(stage=stage):
                gain_step(stage)

    one.drain()
    two.drain()
    for i in range(1, ny):
        g1_copy(i).wait_send()
    for i in range(1, nx):
        g2_copy(i).wait_send()
    for i in range(1, nz):
        g3_copy(i).wait_send()
    g4_copy().wait_send()
    for i, (ref, hbm) in enumerate(((dq, dq_hbm), (dk, dk_hbm), (dv, dv_hbm))):
        pltpu.make_async_copy(ref, hbm.at[0], out_sem.at[i]).wait()


def hand_over(a, b, c, a_out, b_out, c_out, sems):
    copies = [pltpu.make_async_copy(src, dst, sems.at[i]) for i, (src, dst) in enumerate(((a, a_out), (b, b_out), (c, c_out)))]
    for copy in copies:
        copy.start()
    for copy in copies:
        copy.wait()


def build(mesh, nx, nz):
    ny = mesh.shape["dp"]
    width = HEADS * DIM
    ry, rx = HEADS // ny, HEADS // ny // nx

    def scan_scratch():
        state = pltpu.VMEM((CHUNKS, ROWS, DIM), F32)
        return [
            pltpu.VMEM((2 * CHUNKS, ROWS, DIM), F32),
            *[state] * 9,
            pltpu.SemaphoreType.DMA((HALF,)),
            *[pltpu.SemaphoreType.DMA((CHUNKS,))] * 3,
            pltpu.SemaphoreType.DMA((HALF,)),
            pltpu.SemaphoreType.DMA((5,)),
        ]

    scratch = [
        *[pltpu.VMEM((DIM, width), BF16)] * 7,
        *[pltpu.VMEM((HEADS, DIM, DIM), BF16)] * 3,
        *[pltpu.VMEM((HEADS, DIM, DIM), F32)] * 3,
        pltpu.VMEM((HEADS, 8, DIM), F32),
        pltpu.VMEM((ny - 1, ry, 8, DIM), F32),
        pltpu.VMEM((ry, 8, DIM), F32),
        pltpu.VMEM((nx - 1, rx, 8, DIM), F32),
        pltpu.VMEM((rx, 8, DIM), F32),
        pltpu.VMEM((nz - 1, rx, 8, DIM), F32),
        pltpu.VMEM((rx, 8, DIM), F32),
        pltpu.VMEM((rx, 8, DIM), F32),
        *scan_scratch(),
        *scan_scratch(),
        pltpu.SemaphoreType.DMA((4,)),
        pltpu.SemaphoreType.DMA((3,)),
        pltpu.SemaphoreType.DMA((4,)),
        pltpu.SemaphoreType.DMA((ny - 1,)),
        pltpu.SemaphoreType.DMA((nx - 1,)),
        pltpu.SemaphoreType.DMA((nz - 1,)),
        pltpu.SemaphoreType.DMA,
    ]

    def body(queries, key_rows, value_rows, out_grad, norm_gain):
        rows = jax.ShapeDtypeStruct(queries.shape, BF16)
        dq, dk, dv, dgain = pl.pallas_call(
            functools.partial(kernel, (ny, nx, nz)),
            out_shape=(rows, rows, rows, jax.ShapeDtypeStruct((rx, DIM), F32)),
            in_specs=[pl.BlockSpec(memory_space=pl.ANY)] * 4 + [pl.BlockSpec(memory_space=pltpu.VMEM)],
            out_specs=[pl.BlockSpec(memory_space=pl.ANY)] * 3 + [pl.BlockSpec(memory_space=pltpu.VMEM)],
            scratch_shapes=scratch,
            compiler_params=pltpu.CompilerParams(
                collective_id=0, has_side_effects=True, vmem_limit_bytes=62 * 1024 * 1024
            ),
        )(queries, key_rows, value_rows, out_grad, norm_gain.reshape(1, width))
        dq, dk, dv = pl.pallas_call(
            hand_over,
            out_shape=(rows, rows, rows),
            in_specs=[pl.BlockSpec(memory_space=pl.ANY)] * 3,
            out_specs=[pl.BlockSpec(memory_space=pl.ANY)] * 3,
            scratch_shapes=[pltpu.SemaphoreType.DMA((3,))],
            compiler_params=pltpu.CompilerParams(vmem_limit_bytes=62 * 1024 * 1024),
        )(dq, dk, dv)
        share = rx * DIM // (2 * nz)
        place = lax.rem(lax.axis_index("ctx"), 2 * nz) * share
        return dq, dk, dv, lax.dynamic_slice(dgain.reshape(rx * DIM), (place,), (share,))

    placed = P("dp", "ctx", None)
    return jax.shard_map(
        body,
        mesh=mesh,
        in_specs=(placed, placed, placed, placed, P()),
        out_specs=(placed, placed, placed, P(("dp", "ctx"))),
        check_vma=False,
    )


def solution(mesh):
    return build(mesh, 4, 8)
```

```python
import functools
import math

import jax
import jax.numpy as jnp
from jax import lax
from jax.experimental import pallas as pl
from jax.experimental.pallas import tpu as pltpu
from jax.sharding import PartitionSpec as P

HEADS = 16
HALF = 8
DIM = 128
EPSILON = 1e-05
MESH = pl.DeviceIdType.MESH
F32 = jnp.float32
BF16 = jnp.bfloat16

LAG = 2
SUM_LAG = 2


def dot(a, b, ca, cb):
    return lax.dot_general(a, b, (((ca,), (cb,)), ((), ())), preferred_element_type=F32)


def turn(e):
    return 4 - e // 2 + (e % 2) * (e // 2 + (e + 1) // 2)


class Scan:
    def __init__(self, sizes, pos, order, bufs, sems):
        self.nx, self.nz = sizes
        self.y, self.x, self.z, self.c = pos
        self.order = order
        if order > 0:
            self.px, self.pc = self.x, self.c
        else:
            self.px, self.pc = self.nx - 1 - self.x, 1 - self.c
        self.own, self.exch, self.s, self.gin, self.r, self.rin, self.pout, self.pin, self.bkin, self.bkout = bufs
        self.re, self.ri, self.rx, self.ro, self.rb, self.sends = sems

    def device(self, x, z, c):
        return (self.y, (x * self.nz + z) * 2 + c)

    def partner(self):
        return self.device(self.x, self.z, 1 - self.c)

    def remote(self, src, dst, which, recv, to):
        return pltpu.make_async_remote_copy(
            src_ref=src, dst_ref=dst, send_sem=self.sends.at[which], recv_sem=recv, device_id=to, device_id_type=MESH
        )

    def exch_copy(self, m):
        return self.remote(self.own.at[(1 - self.c) * HALF + m], self.exch.at[m], 0, self.re.at[m], self.partner())

    def in_copy(self, m, slot):
        return self.remote(self.s.at[m], self.gin.at[slot], 1, self.ri.at[slot], self.device(self.x, m, self.c))

    def out_copy(self, m, slot):
        return self.remote(self.pout.at[m], self.pin.at[slot], 2, self.ro.at[slot], self.device(self.x, m, self.c))

    def bk_copy(self, m):
        return self.remote(self.bkout.at[m], self.bkin.at[m], 3, self.rb.at[m], self.partner())

    def x_copy(self, i):
        to = self.device(self.x + i * self.order, self.z, self.c)
        return self.remote(self.r, self.rin.at[i - 1], 3 + i, self.rx.at[i - 1], to)

    def add_chip(self, m):
        self.exch_copy(m).wait_recv()
        total = self.own[self.c * HALF + m] + self.exch[m]

        @pl.when(m == self.z)
        def _():
            self.gin[m] = total

        @pl.when(m != self.z)
        def _():
            self.s[m] = total
            self.in_copy(m, self.z).start()

    def add_row(self):
        for e in range(self.nz - 1):
            source = (self.z + self.nz - turn(e)) % self.nz
            self.in_copy(source, source).wait_recv()
        total = self.gin[0]
        for m in range(1, self.nz):
            total = total + self.gin[m]
        self.r[...] = total
        for i in range(1, self.nx):

            @pl.when(self.px + i < self.nx)
            def _(i=i):
                self.x_copy(i).start()

    def spread(self):
        self.pout[0] = jnp.zeros((DIM, DIM), F32)
        for i in range(1, self.nx):

            @pl.when(self.px >= i)
            def _(i=i):
                self.x_copy(i).wait_recv()
                self.pout[0] = self.pout[0] + self.rin[i - 1]

        total = self.pout[0]
        for m in range(self.nz):
            place = m if self.order > 0 else self.nz - 1 - m
            self.pout[place] = total
            total = total + self.gin[place]
        self.pin[self.z] = self.pout[self.z]

        @pl.loop(0, self.nz - 1)
        def _(e):
            self.out_copy((self.z + turn(e)) % self.nz, self.z).start()

    def finish(self, m):
        @pl.when(m != self.z)
        def _():
            self.out_copy(m, m).wait_recv()

        before = self.pin[m]
        self.bkout[m] = jnp.where(self.pc == 0, before + self.own[self.c * HALF + m], before)
        self.bk_copy(m).start()
        return jnp.where(self.pc == 1, before + self.exch[m], before)

    def finished(self, m):
        self.bk_copy(m).wait_recv()
        return self.bkin[m]

    def drain(self):
        some = pl.ds(0, self.nz - 1)
        self.remote(self.exch, self.exch, 0, self.re.at[0], self.partner()).wait_send()
        self.remote(self.s.at[some], self.gin.at[some], 1, self.ri.at[0], self.partner()).wait_send()
        self.remote(self.pout.at[some], self.pin.at[some], 2, self.ro.at[0], self.partner()).wait_send()
        self.remote(self.bkout, self.bkin, 3, self.rb.at[0], self.partner()).wait_send()
        for i in range(1, self.nx):

            @pl.when(self.px + i < self.nx)
            def _(i=i):
                self.x_copy(i).wait_send()


def kernel(
    sizes,
    q_hbm,
    k_hbm,
    v_hbm,
    g_hbm,
    gain_ref,
    dq_hbm,
    dk_hbm,
    dv_hbm,
    dgain_ref,
    *scratch,
):
    ny, nx, nz = sizes
    scratch = list(scratch)

    def take(n):
        out = scratch[:n]
        del scratch[:n]
        return out

    q, k, v, g = take(4)
    dq, dk, dv = take(3)
    scores, d_out, prior = take(3)
    out_loc, dk_loc, dv_loc = take(3)
    gtile, gin1, acc1, gin2, acc2, gin3, acc3, gin4 = take(8)
    bufs1, sems1 = take(10), take(6)
    bufs2, sems2 = take(10), take(6)
    in_sem, out_sem, gsend, g1r, g2r, g3r, g4r = take(7)

    y = lax.axis_index("dp")
    ctx = lax.axis_index("ctx")
    x = ctx // (2 * nz)
    z = (ctx // 2) % nz
    c = ctx % 2
    pos = (y, x, z, c)

    def device(y_, x_, z_, c_):
        return (y_, (x_ * nz + z_) * 2 + c_)

    loads = [pltpu.make_async_copy(src.at[0], dst, in_sem.at[i]) for i, (src, dst) in enumerate(((k_hbm, k), (v_hbm, v), (q_hbm, q), (g_hbm, g)))]
    for load in loads:
        load.start()

    def y_peer(i):
        return device((y + i) % ny, x, z, c)

    def x_peer(i):
        return device(y, (x + i) % nx, z, c)

    def z_peer(i):
        return device(y, x, (z + i) % nz, c)

    partner = device(y, x, z, 1 - c)
    barrier = pltpu.get_barrier_semaphore()
    pl.semaphore_signal(barrier, inc=1, device_id=partner, device_id_type=MESH)
    for count, peer in ((ny, y_peer), (nx, x_peer), (nz, z_peer)):
        for i in range(1, count):
            pl.semaphore_signal(barrier, inc=1, device_id=peer(i), device_id_type=MESH)

    one = Scan((nx, nz), pos, 1, bufs1, sems1)
    two = Scan((nx, nz), pos, -1, bufs2, sems2)

    def col(h):
        return pl.ds(pl.multiple_of(h * DIM, DIM), DIM)

    mine, other = c * HALF, (1 - c) * HALF

    def columns(ref, heads):
        return [ref[:, col(h)] for h in heads]

    def local_states(heads):
        ks, vs = columns(k, heads), columns(v, heads)
        states = [dot(kh, vh, 0, 0) for kh, vh in zip(ks, vs)]
        for h, state in zip(heads, states):
            one.own[h] = state

    loads[0].wait()
    loads[1].wait()

    def place(e):
        return (z + turn(e)) % nz

    for i in range(0, HALF, 4):
        local_states([other + place(i + u) for u in range(4)])
        if i == 0:
            pl.semaphore_wait(barrier, ny + nx + nz - 2)
        for u in range(4):
            one.exch_copy(place(i + u)).start()

    for i in range(0, HALF, 4):
        local_states([mine + place(i + u) for u in range(4)])
        for u in range(4):
            one.add_chip(place(i + u))

    loads[2].wait()
    loads[3].wait()

    keep = lax.broadcasted_iota(jnp.int32, (DIM, DIM), 0) >= lax.broadcasted_iota(jnp.int32, (DIM, DIM), 1)

    def before_one(heads):
        qs, ks, vs = columns(q, heads), columns(k, heads), columns(v, heads)
        raw = [dot(qh, kh, 1, 1) for qh, kh in zip(qs, ks)]
        lows = [jnp.where(keep, r, 0.0).astype(BF16) for r in raw]
        outs = [dot(low, vh, 1, 0) for low, vh in zip(lows, vs)]
        for h, low, out in zip(heads, lows, outs):
            scores[h] = low
            out_loc[h] = out

    def pass_one(heads, states):
        qs = columns(q, heads)
        gfs = [gh.astype(F32) for gh in columns(g, heads)]
        gains = columns(gain_ref, heads)
        locs = [out_loc[h] for h in heads]
        lows = [state.astype(BF16) for state in states]
        outs = [loc + dot(qh, low, 1, 0) for loc, qh, low in zip(locs, qs, lows)]
        invs = [lax.rsqrt(jnp.mean(out * out, axis=1, keepdims=True) + EPSILON) for out in outs]
        normeds = [out * inv for out, inv in zip(outs, invs)]
        gns = [gf * gain for gf, gain in zip(gfs, gains)]
        means = [jnp.mean(gn * normed, axis=1, keepdims=True) for gn, normed in zip(gns, normeds)]
        ds = [((gn - normed * mean) * inv).astype(BF16) for gn, normed, mean, inv in zip(gns, normeds, means, invs)]
        grads = [dot(qh, d, 0, 0) for qh, d in zip(qs, ds)]
        terms = [jnp.sum((gf * normed).reshape(DIM // 8, 8, DIM), axis=0) for gf, normed in zip(gfs, normeds)]
        for h, low, d, grad, term in zip(heads, lows, ds, grads, terms):
            prior[h] = low
            d_out[h] = d
            two.own[h] = grad
            gtile[h] = term

    def between(heads):
        ds, lows, scs = [d_out[h] for h in heads], [prior[h] for h in heads], [scores[h] for h in heads]
        qs, ks, vs = columns(q, heads), columns(k, heads), columns(v, heads)
        raw = [dot(d, vh, 1, 1) for d, vh in zip(ds, vs)]
        dvs = [dot(sc, d, 0, 0) for sc, d in zip(scs, ds)]
        pqs = [dot(d, low, 1, 1) for d, low in zip(ds, lows)]
        gss = [jnp.where(keep, r, 0.0).astype(BF16) for r in raw]
        dqs = [(dot(gs, kh, 1, 0) + pq).astype(BF16) for gs, kh, pq in zip(gss, ks, pqs)]
        dks = [dot(gs, qh, 0, 0) for gs, qh in zip(gss, qs)]
        for h, dqh, dkh, dvh in zip(heads, dqs, dks, dvs):
            dq[:, col(h)] = dqh
            dk_loc[h] = dkh
            dv_loc[h] = dvh

    def store(ref, hbm, i, h):
        return pltpu.make_async_copy(ref.at[:, col(h)], hbm.at[0, :, col(h)], out_sem.at[i])

    def pass_two(heads, states):
        ks, vs = columns(k, heads), columns(v, heads)
        dks, dvs = [dk_loc[h] for h in heads], [dv_loc[h] for h in heads]
        lows = [state.astype(BF16) for state in states]
        dks = [(part + dot(vh, low, 1, 1)).astype(BF16) for part, vh, low in zip(dks, vs, lows)]
        dvs = [(part + dot(kh, low, 1, 0)).astype(BF16) for part, kh, low in zip(dvs, ks, lows)]
        for h, dkh, dvh in zip(heads, dks, dvs):
            dk[:, col(h)] = dkh
            dv[:, col(h)] = dvh
        for h in heads:
            store(dk, dk_hbm, 1, h).start()
            store(dv, dv_hbm, 2, h).start()

    ry, rx = HEADS // ny, HEADS // ny // nx

    def g1_copy(i):
        src = gtile.at[pl.ds(((y + i) % ny) * ry, ry)]
        return pltpu.make_async_remote_copy(
            src_ref=src, dst_ref=gin1.at[i - 1], send_sem=gsend.at[0], recv_sem=g1r.at[i - 1], device_id=y_peer(i), device_id_type=MESH
        )

    def g2_copy(i):
        src = acc1.at[pl.ds(((x + i) % nx) * rx, rx)]
        return pltpu.make_async_remote_copy(
            src_ref=src, dst_ref=gin2.at[i - 1], send_sem=gsend.at[1], recv_sem=g2r.at[i - 1], device_id=x_peer(i), device_id_type=MESH
        )

    def g3_copy(i):
        return pltpu.make_async_remote_copy(
            src_ref=acc2, dst_ref=gin3.at[i - 1], send_sem=gsend.at[2], recv_sem=g3r.at[i - 1], device_id=z_peer(i), device_id_type=MESH
        )

    def g4_copy():
        return pltpu.make_async_remote_copy(
            src_ref=acc3, dst_ref=gin4, send_sem=gsend.at[3], recv_sem=g4r, device_id=partner, device_id_type=MESH
        )

    def gain_step(stage):
        if stage == 0:
            for i in range(1, ny):
                g1_copy(i).start()
        elif stage == 1:
            total = gtile[pl.ds(y * ry, ry)]
            for i in range(1, ny):
                g1_copy(i).wait_recv()
                total = total + gin1[i - 1]
            acc1[...] = total
            for i in range(1, nx):
                g2_copy(i).start()
        elif stage == 2:
            total = acc1[pl.ds(x * rx, rx)]
            for i in range(1, nx):
                g2_copy(i).wait_recv()
                total = total + gin2[i - 1]
            acc2[...] = total
            for i in range(1, nz):
                g3_copy(i).start()
        elif stage == 3:
            total = acc2[...]
            for i in range(1, nz):
                g3_copy(i).wait_recv()
                total = total + gin3[i - 1]
            acc3[...] = total
            g4_copy().start()
        else:
            g4_copy().wait_recv()
            scale = 1.0 / math.sqrt(ny * nx * nz * 2 * DIM)
            dgain_ref[...] = jnp.sum(acc3[...] + gin4[...], axis=1) * scale

    def arrival(e):
        return (z + nz - turn((e + nz - 1) % nz)) % nz

    def finishing(scan, work, after, last):
        @pl.loop(0, HALF + LAG + SUM_LAG)
        def _(e):
            @pl.when(e >= LAG + SUM_LAG)
            def _():
                last(arrival(e - LAG - SUM_LAG))

            @pl.when(e < LAG)
            def _():
                m = arrival(e)
                work([mine + m], [scan.finish(m)])

            @pl.when((e >= LAG) & (e < HALF))
            def _():
                m, n = arrival(e), arrival(e - LAG)
                state = scan.finish(m)
                work([mine + m, other + n], [state, scan.finished(n)])
                after(n)

            @pl.when((e >= HALF) & (e < HALF + LAG))
            def _():
                n = arrival(e - LAG)
                work([other + n], [scan.finished(n)])
                after(n)

    def nothing(m):
        pass

    @pl.loop(0, HALF)
    def _(m):
        before_one([mine + m, other + m])

    one.add_row()
    one.spread()
    finishing(one, pass_one, lambda m: two.exch_copy(m).start(), two.add_chip)
    gain_step(0)

    @pl.loop(0, HALF)
    def _(m):
        between([mine + m, other + m])

        @pl.when(m == HALF // 2)
        def _():
            gain_step(1)

    pltpu.make_async_copy(dq, dq_hbm.at[0], out_sem.at[0]).start()
    gain_step(2)
    two.add_row()
    two.spread()
    gain_step(3)
    finishing(two, pass_two, nothing, nothing)
    gain_step(4)

    one.drain()
    two.drain()
    for i in range(1, ny):
        g1_copy(i).wait_send()
    for i in range(1, nx):
        g2_copy(i).wait_send()
    for i in range(1, nz):
        g3_copy(i).wait_send()
    g4_copy().wait_send()
    for i, (ref, hbm) in enumerate(((dq, dq_hbm), (dk, dk_hbm), (dv, dv_hbm))):
        pltpu.make_async_copy(ref, hbm.at[0], out_sem.at[i]).wait()


def hand_over(a, b, c, a_out, b_out, c_out, a_buf, b_buf, c_buf, sems):
    trips = ((a, a_buf, a_out), (b, b_buf, b_out), (c, c_buf, c_out))
    loads = [pltpu.make_async_copy(src.at[0], buf, sems.at[0, i]) for i, (src, buf, _) in enumerate(trips)]
    stores = [pltpu.make_async_copy(buf, dst.at[0], sems.at[1, i]) for i, (_, buf, dst) in enumerate(trips)]
    for load in loads:
        load.start()
    for load, store in zip(loads, stores):
        load.wait()
        store.start()
    for store in stores:
        store.wait()


def build(mesh, nx, nz):
    ny = mesh.shape["dp"]
    width = HEADS * DIM
    ry, rx = HEADS // ny, HEADS // ny // nx

    def scan_scratch():
        state = pltpu.VMEM((HALF, DIM, DIM), F32)
        return [
            pltpu.VMEM((HEADS, DIM, DIM), F32),
            *[state] * 3,
            pltpu.VMEM((DIM, DIM), F32),
            pltpu.VMEM((nx - 1, DIM, DIM), F32),
            *[state] * 4,
            *[pltpu.SemaphoreType.DMA((HALF,))] * 2,
            pltpu.SemaphoreType.DMA((nx - 1,)),
            *[pltpu.SemaphoreType.DMA((HALF,))] * 2,
            pltpu.SemaphoreType.DMA((3 + nx,)),
        ]

    scratch = [
        *[pltpu.VMEM((DIM, width), BF16)] * 7,
        *[pltpu.VMEM((HEADS, DIM, DIM), BF16)] * 3,
        *[pltpu.VMEM((HEADS, DIM, DIM), F32)] * 3,
        pltpu.VMEM((HEADS, 8, DIM), F32),
        pltpu.VMEM((ny - 1, ry, 8, DIM), F32),
        pltpu.VMEM((ry, 8, DIM), F32),
        pltpu.VMEM((nx - 1, rx, 8, DIM), F32),
        pltpu.VMEM((rx, 8, DIM), F32),
        pltpu.VMEM((nz - 1, rx, 8, DIM), F32),
        pltpu.VMEM((rx, 8, DIM), F32),
        pltpu.VMEM((rx, 8, DIM), F32),
        *scan_scratch(),
        *scan_scratch(),
        pltpu.SemaphoreType.DMA((4,)),
        pltpu.SemaphoreType.DMA((3,)),
        pltpu.SemaphoreType.DMA((4,)),
        pltpu.SemaphoreType.DMA((ny - 1,)),
        pltpu.SemaphoreType.DMA((nx - 1,)),
        pltpu.SemaphoreType.DMA((nz - 1,)),
        pltpu.SemaphoreType.DMA,
    ]

    def body(queries, key_rows, value_rows, out_grad, norm_gain):
        rows = jax.ShapeDtypeStruct(queries.shape, BF16)
        dq, dk, dv, dgain = pl.pallas_call(
            functools.partial(kernel, (ny, nx, nz)),
            out_shape=(rows, rows, rows, jax.ShapeDtypeStruct((rx, DIM), F32)),
            in_specs=[pl.BlockSpec(memory_space=pl.ANY)] * 4 + [pl.BlockSpec(memory_space=pltpu.VMEM)],
            out_specs=[pl.BlockSpec(memory_space=pl.ANY)] * 3 + [pl.BlockSpec(memory_space=pltpu.VMEM)],
            scratch_shapes=scratch,
            compiler_params=pltpu.CompilerParams(
                collective_id=0, has_side_effects=True, vmem_limit_bytes=62 * 1024 * 1024
            ),
        )(queries, key_rows, value_rows, out_grad, norm_gain.reshape(1, width))
        dq, dk, dv = pl.pallas_call(
            hand_over,
            out_shape=(rows, rows, rows),
            in_specs=[pl.BlockSpec(memory_space=pl.ANY)] * 3,
            out_specs=[pl.BlockSpec(memory_space=pl.ANY)] * 3,
            scratch_shapes=[*[pltpu.VMEM((DIM, width), BF16)] * 3, pltpu.SemaphoreType.DMA((2, 3))],
            compiler_params=pltpu.CompilerParams(vmem_limit_bytes=62 * 1024 * 1024),
        )(dq, dk, dv)
        share = rx * DIM // (2 * nz)
        place = lax.rem(lax.axis_index("ctx"), 2 * nz) * share
        return dq, dk, dv, lax.dynamic_slice(dgain.reshape(rx * DIM), (place,), (share,))

    placed = P("dp", "ctx", None)
    return jax.shard_map(
        body,
        mesh=mesh,
        in_specs=(placed, placed, placed, placed, P()),
        out_specs=(placed, placed, placed, P(("dp", "ctx"))),
        check_vma=False,
    )


def solution(mesh):
    return build(mesh, 4, 8)
```

```python
import functools
import math

import jax
import jax.numpy as jnp
from jax import lax
from jax.experimental import pallas as pl
from jax.experimental.pallas import tpu as pltpu
from jax.sharding import PartitionSpec as P

HEADS = 16
HALF = 8
DIM = 128
EPSILON = 1e-05
MESH = pl.DeviceIdType.MESH
F32 = jnp.float32
BF16 = jnp.bfloat16

LAG = 2
SUM_LAG = 2
BLOCK = 32


def dot(a, b, ca, cb):
    return lax.dot_general(a, b, (((ca,), (cb,)), ((), ())), preferred_element_type=F32)


def listed(places, e):
    packed = sum(place << (3 * i) for i, place in enumerate(places))
    return lax.shift_right_logical(jnp.int32(packed), jnp.int32(3) * e) % 8


MAKE = (4, 5, 3, 6, 2, 7, 1, 0)
SEND = (5, 3, 6, 2, 7, 1)
WORK = (5, 0, 3, 4, 6, 2, 7, 1)


def ring(places, e, z, nz):
    away = listed(places, e)
    return (z + away + (z % 2) * (nz - 2 * away)) % nz


class Scan:
    def __init__(self, sizes, pos, order, bufs, sems):
        self.nx, self.nz = sizes
        self.y, self.x, self.z, self.c = pos
        self.order = order
        self.pc = self.c if order > 0 else 1 - self.c
        self.slot = self.x * self.nz + self.z
        self.mate = self.z + 1 - 2 * (self.z % 2)
        self.first = self.z % 2 == (0 if order > 0 else 1)
        self.far = (self.z + self.nz // 2) % self.nz
        self.passed = (self.mate + self.nz // 2) % self.nz
        (self.own, self.exch, self.s, self.gin, self.pout, self.pin, self.bkin, self.bkout, self.given, self.both, self.on) = bufs
        self.re, self.ri, self.ro, self.rb, self.rg, self.sends = sems

    def device(self, x, z, c):
        return (self.y, (x * self.nz + z) * 2 + c)

    def partner(self):
        return self.device(self.x, self.z, 1 - self.c)

    def remote(self, src, dst, which, recv, to):
        return pltpu.make_async_remote_copy(
            src_ref=src, dst_ref=dst, send_sem=self.sends.at[which], recv_sem=recv, device_id=to, device_id_type=MESH
        )

    def exch_copy(self, m):
        return self.remote(self.own.at[(1 - self.c) * HALF + m], self.exch.at[m], 0, self.re.at[m], self.partner())

    def clear(self):
        for x in range(self.nx):
            self.gin[x * self.nz + self.far] = jnp.zeros((DIM // self.nx, DIM), F32)

    def give_copy(self):
        to = self.device(self.x, self.mate, self.c)
        return self.remote(self.s.at[self.far], self.given, 4, self.rg, to)

    def on_copy(self):
        to = self.device(self.x, self.mate, self.c)
        return self.remote(self.on, self.pin.at[self.passed], 5, self.ro.at[self.passed], to)

    def in_copy(self, src, m, r):
        return self.remote(src.at[r], self.gin.at[self.slot], 1, self.ri, self.device(r, m, self.c))

    def out_copy(self, x, z):
        to = self.device(x, z, self.c)
        return self.remote(self.pout.at[x * self.nz + z], self.pin.at[self.z, self.x], 2, self.ro.at[self.z], to)

    def bk_copy(self, m):
        return self.remote(self.bkout.at[m], self.bkin.at[m], 3, self.rb.at[m], self.partner())

    def add_chip(self, m):
        self.exch_copy(m).wait_recv()
        parts = (self.nx, DIM // self.nx, DIM)
        self.s[m] = (self.own[self.c * HALF + m] + self.exch[m]).reshape(parts)

        @pl.when(m == self.far)
        def _():
            self.give_copy().start()

        @pl.when((m != self.far) & (m != self.passed))
        def _():
            for i in range(1, self.nx):
                self.in_copy(self.s.at[m], m, (self.x + i) % self.nx).start()

            @pl.when(m == self.z)
            def _():
                self.gin[self.slot] = self.s[m, self.x]

            @pl.when(m != self.z)
            def _():
                self.in_copy(self.s.at[m], m, self.x).start()

    def pass_in(self):
        self.give_copy().wait_recv()
        self.both[...] = self.s[self.passed] + self.given[...]
        for r in range(self.nx):
            self.in_copy(self.both, self.passed, r).start()

    def scan(self):
        slots = self.nx * self.nz
        some = pl.ds(0, slots - self.nx - 1)
        self.remote(self.gin.at[some], self.gin.at[some], 1, self.ri, self.partner()).wait_recv()
        total = jnp.zeros((DIM // self.nx, DIM), F32)
        for i in range(slots):
            slot = i if self.order > 0 else slots - 1 - i
            self.pout[slot] = total
            total = total + self.gin[slot]
        self.pin[self.z, self.x] = self.pout[self.slot]

        @pl.loop(0, self.nz - 2)
        def _(e):
            for i in range(self.nx):
                self.out_copy((self.x + i) % self.nx, ring(SEND, e, self.z, self.nz)).start()

        for i in range(1, self.nx):
            self.out_copy((self.x + i) % self.nx, self.z).start()

    def arrived(self, m, parts):
        part = self.pin.at[m, pl.ds(0, parts)]
        self.remote(part, part, 2, self.ro.at[m], self.partner()).wait_recv()

    def finish(self, m):
        @pl.when(m == self.z)
        def _():
            self.arrived(m, self.nx - 1)

        @pl.when(m != self.z)
        def _():
            self.arrived(m, self.nx)

        @pl.when(m == self.passed)
        def _():
            before = self.pin[m]
            self.on[...] = jnp.where(self.first, before + self.s[m], before)
            self.on_copy().start()
            self.pin[m] = jnp.where(self.first, before, before + self.given[...])

        before = self.pin[m].reshape(DIM, DIM)
        self.bkout[m] = jnp.where(self.pc == 0, before + self.own[self.c * HALF + m], before)
        self.bk_copy(m).start()
        return jnp.where(self.pc == 1, before + self.exch[m], before)

    def finished(self, m):
        self.bk_copy(m).wait_recv()
        return self.bkin[m]

    def drain(self):
        some = pl.ds(0, self.nx * (self.nz - 1) - 1)
        self.remote(self.exch, self.exch, 0, self.re.at[0], self.partner()).wait_send()
        self.remote(self.gin.at[some], self.gin.at[some], 1, self.ri, self.partner()).wait_send()
        self.remote(self.pout.at[some], self.pout.at[some], 2, self.ro.at[0], self.partner()).wait_send()
        self.remote(self.bkout, self.bkin, 3, self.rb.at[0], self.partner()).wait_send()
        self.give_copy().wait_send()
        self.on_copy().wait_send()


def kernel(
    sizes,
    q_hbm,
    k_hbm,
    v_hbm,
    g_hbm,
    gain_ref,
    dq_hbm,
    dk_hbm,
    dv_hbm,
    dgain_ref,
    *scratch,
):
    ny, nx, nz = sizes
    scratch = list(scratch)

    def take(n):
        out = scratch[:n]
        del scratch[:n]
        return out

    q, k, v, g = take(4)
    dq, dk, dv = take(3)
    scores, d_out, prior = take(3)
    out_loc, dk_loc, dv_loc = take(3)
    gtile, gin1, acc1, gin2, acc2, gin3, acc3, gin4 = take(8)
    bufs1, sems1 = take(11), take(6)
    bufs2, sems2 = take(11), take(6)
    in_sem, out_sem, gsend, g1r, g2r, g3r, g4r = take(7)

    y = lax.axis_index("dp")
    ctx = lax.axis_index("ctx")
    x = ctx // (2 * nz)
    z = (ctx // 2) % nz
    c = ctx % 2
    pos = (y, x, z, c)

    def device(y_, x_, z_, c_):
        return (y_, (x_ * nz + z_) * 2 + c_)

    loads = [pltpu.make_async_copy(src.at[0], dst, in_sem.at[i]) for i, (src, dst) in enumerate(((k_hbm, k), (v_hbm, v), (q_hbm, q), (g_hbm, g)))]
    for load in loads:
        load.start()

    def y_peer(i):
        return device((y + i) % ny, x, z, c)

    def x_peer(i):
        return device(y, (x + i) % nx, z, c)

    def z_peer(i):
        return device(y, x, (z + i) % nz, c)

    partner = device(y, x, z, 1 - c)
    barrier = pltpu.get_barrier_semaphore()
    pl.semaphore_signal(barrier, inc=1, device_id=partner, device_id_type=MESH)
    for i in range(1, ny):
        pl.semaphore_signal(barrier, inc=1, device_id=y_peer(i), device_id_type=MESH)

    @pl.loop(1, nx * nz)
    def _(i):
        to = (x * nz + z + i) % (nx * nz)
        pl.semaphore_signal(barrier, inc=1, device_id=(y, to * 2 + c), device_id_type=MESH)

    one = Scan((nx, nz), pos, 1, bufs1, sems1)
    two = Scan((nx, nz), pos, -1, bufs2, sems2)
    one.clear()
    two.clear()

    def col(h):
        return pl.ds(pl.multiple_of(h * DIM, DIM), DIM)

    mine, other = c * HALF, (1 - c) * HALF

    def columns(ref, heads):
        return [ref[:, col(h)] for h in heads]

    def local_states(heads):
        ks, vs = columns(k, heads), columns(v, heads)
        states = [dot(kh, vh, 0, 0) for kh, vh in zip(ks, vs)]
        for h, state in zip(heads, states):
            one.own[h] = state

    loads[0].wait()
    loads[1].wait()

    def place(e):
        return ring(MAKE, jnp.int32(e), z, nz)

    for i in range(0, HALF, 4):
        local_states([other + place(i + u) for u in range(4)])
        if i == 0:
            pl.semaphore_wait(barrier, nx * nz + ny - 1)
        for u in range(4):
            one.exch_copy(place(i + u)).start()

    for i in range(0, HALF, 4):
        local_states([mine + place(i + u) for u in range(4)])
        for u in range(4):
            one.add_chip(place(i + u))
    one.pass_in()

    loads[2].wait()
    loads[3].wait()

    keep = lax.broadcasted_iota(jnp.int32, (DIM, DIM), 0) >= lax.broadcasted_iota(jnp.int32, (DIM, DIM), 1)

    def before_one(heads):
        qs, ks, vs = columns(q, heads), columns(k, heads), columns(v, heads)
        raw = [dot(qh, kh, 1, 1) for qh, kh in zip(qs, ks)]
        lows = [jnp.where(keep, r, 0.0).astype(BF16) for r in raw]
        outs = [dot(low, vh, 1, 0) for low, vh in zip(lows, vs)]
        for h, low, out in zip(heads, lows, outs):
            scores[h] = low
            out_loc[h] = out

    def pass_one(heads, states):
        qs = columns(q, heads)
        gfs = [gh.astype(F32) for gh in columns(g, heads)]
        gains = columns(gain_ref, heads)
        locs = [out_loc[h] for h in heads]
        lows = [state.astype(BF16) for state in states]
        outs = [loc + dot(qh, low, 1, 0) for loc, qh, low in zip(locs, qs, lows)]
        invs = [lax.rsqrt(jnp.mean(out * out, axis=1, keepdims=True) + EPSILON) for out in outs]
        normeds = [out * inv for out, inv in zip(outs, invs)]
        gns = [gf * gain for gf, gain in zip(gfs, gains)]
        means = [jnp.mean(gn * normed, axis=1, keepdims=True) for gn, normed in zip(gns, normeds)]
        ds = [((gn - normed * mean) * inv).astype(BF16) for gn, normed, mean, inv in zip(gns, normeds, means, invs)]
        grads = [dot(qh, d, 0, 0) for qh, d in zip(qs, ds)]
        terms = [jnp.sum((gf * normed).reshape(DIM // 8, 8, DIM), axis=0) for gf, normed in zip(gfs, normeds)]
        for h, low, d, grad, term in zip(heads, lows, ds, grads, terms):
            prior[h] = low
            d_out[h] = d
            two.own[h] = grad
            gtile[h] = term

    def between(heads):
        ds, lows, scs = [d_out[h] for h in heads], [prior[h] for h in heads], [scores[h] for h in heads]
        qs, ks, vs = columns(q, heads), columns(k, heads), columns(v, heads)
        raw = [dot(d, vh, 1, 1) for d, vh in zip(ds, vs)]
        dvs = [dot(sc, d, 0, 0) for sc, d in zip(scs, ds)]
        pqs = [dot(d, low, 1, 1) for d, low in zip(ds, lows)]
        gss = [jnp.where(keep, r, 0.0).astype(BF16) for r in raw]
        dqs = [(dot(gs, kh, 1, 0) + pq).astype(BF16) for gs, kh, pq in zip(gss, ks, pqs)]
        dks = [dot(gs, qh, 0, 0) for gs, qh in zip(gss, qs)]
        for h, dqh, dkh, dvh in zip(heads, dqs, dks, dvs):
            dq[:, col(h)] = dqh
            dk_loc[h] = dkh
            dv_loc[h] = dvh

    def store(ref, hbm, i, h):
        return pltpu.make_async_copy(ref.at[:, col(h)], hbm.at[0, :, col(h)], out_sem.at[i])

    def pass_two(heads, states):
        ks, vs = columns(k, heads), columns(v, heads)
        dks, dvs = [dk_loc[h] for h in heads], [dv_loc[h] for h in heads]
        lows = [state.astype(BF16) for state in states]
        dks = [(part + dot(vh, low, 1, 1)).astype(BF16) for part, vh, low in zip(dks, vs, lows)]
        dvs = [(part + dot(kh, low, 1, 0)).astype(BF16) for part, kh, low in zip(dvs, ks, lows)]
        for h, dkh, dvh in zip(heads, dks, dvs):
            dk[:, col(h)] = dkh
            dv[:, col(h)] = dvh
        for h in heads:
            store(dk, dk_hbm, 1, h).start()
            store(dv, dv_hbm, 2, h).start()

    ry, rx = HEADS // ny, HEADS // ny // nx

    def g1_copy(i):
        src = gtile.at[pl.ds(((y + i) % ny) * ry, ry)]
        return pltpu.make_async_remote_copy(
            src_ref=src, dst_ref=gin1.at[i - 1], send_sem=gsend.at[0], recv_sem=g1r.at[i - 1], device_id=y_peer(i), device_id_type=MESH
        )

    def g2_copy(i):
        src = acc1.at[pl.ds(((x + i) % nx) * rx, rx)]
        return pltpu.make_async_remote_copy(
            src_ref=src, dst_ref=gin2.at[i - 1], send_sem=gsend.at[1], recv_sem=g2r.at[i - 1], device_id=x_peer(i), device_id_type=MESH
        )

    def g3_copy(i):
        return pltpu.make_async_remote_copy(
            src_ref=acc2, dst_ref=gin3.at[i - 1], send_sem=gsend.at[2], recv_sem=g3r.at[i - 1], device_id=z_peer(i), device_id_type=MESH
        )

    def g4_copy():
        return pltpu.make_async_remote_copy(
            src_ref=acc3, dst_ref=gin4, send_sem=gsend.at[3], recv_sem=g4r, device_id=partner, device_id_type=MESH
        )

    def gain_step(stage):
        if stage == 0:
            for i in range(1, ny):
                g1_copy(i).start()
        elif stage == 1:
            total = gtile[pl.ds(y * ry, ry)]
            for i in range(1, ny):
                g1_copy(i).wait_recv()
                total = total + gin1[i - 1]
            acc1[...] = total
            for i in range(1, nx):
                g2_copy(i).start()
        elif stage == 2:
            total = acc1[pl.ds(x * rx, rx)]
            for i in range(1, nx):
                g2_copy(i).wait_recv()
                total = total + gin2[i - 1]
            acc2[...] = total
            for i in range(1, nz):
                g3_copy(i).start()
        elif stage == 3:
            total = acc2[...]
            for i in range(1, nz):
                g3_copy(i).wait_recv()
                total = total + gin3[i - 1]
            acc3[...] = total
            g4_copy().start()
        else:
            g4_copy().wait_recv()
            scale = 1.0 / math.sqrt(ny * nx * nz * 2 * DIM)
            total = jnp.sum(acc3[...] + gin4[...], axis=1, keepdims=True) * scale
            dgain_ref[...] = jnp.broadcast_to(total, dgain_ref.shape)

    def arrival(e):
        return ring(WORK, e, z, nz)

    def finishing(scan, work, after, last, final):
        @pl.loop(0, HALF + LAG + SUM_LAG)
        def _(e):
            @pl.when(e >= LAG + SUM_LAG)
            def _():
                last(arrival(e - LAG - SUM_LAG))

            @pl.when(e == HALF + LAG)
            def _():
                final()

            @pl.when(e < LAG)
            def _():
                m = arrival(e)
                work([mine + m], [scan.finish(m)])

            @pl.when((e >= LAG) & (e < HALF))
            def _():
                m, n = arrival(e), arrival(e - LAG)
                state = scan.finish(m)
                work([mine + m, other + n], [state, scan.finished(n)])
                after(n)

            @pl.when((e >= HALF) & (e < HALF + LAG))
            def _():
                n = arrival(e - LAG)
                work([other + n], [scan.finished(n)])
                after(n)

    def nothing(*_):
        pass

    @pl.loop(0, HALF)
    def _(m):
        before_one([mine + m, other + m])

    one.scan()
    finishing(one, pass_one, lambda m: two.exch_copy(m).start(), two.add_chip, two.pass_in)
    gain_step(0)

    @pl.loop(0, HALF)
    def _(m):
        between([mine + m, other + m])

        @pl.when(m == HALF // 2)
        def _():
            gain_step(1)

    pltpu.make_async_copy(dq, dq_hbm.at[0], out_sem.at[0]).start()
    gain_step(2)
    two.scan()
    gain_step(3)
    finishing(two, pass_two, nothing, nothing, nothing)
    gain_step(4)

    one.drain()
    two.drain()
    for i in range(1, ny):
        g1_copy(i).wait_send()
    for i in range(1, nx):
        g2_copy(i).wait_send()
    for i in range(1, nz):
        g3_copy(i).wait_send()
    g4_copy().wait_send()
    for i, (ref, hbm) in enumerate(((dq, dq_hbm), (dk, dk_hbm), (dv, dv_hbm))):
        pltpu.make_async_copy(ref, hbm.at[0], out_sem.at[i]).wait()


def hand_over(nz, a, b, c, gain, a_out, b_out, c_out, gain_out, a_buf, b_buf, c_buf, gain_buf, sems):
    trips = ((a, a_buf, a_out), (b, b_buf, b_out), (c, c_buf, c_out))
    loads, stores = [], []
    for row in range(0, DIM, BLOCK):
        for src, buf, dst in trips:
            part, i = pl.ds(row, BLOCK), len(loads)
            loads.append(pltpu.make_async_copy(src.at[0, part], buf.at[part], sems.at[0, i]))
            stores.append(pltpu.make_async_copy(buf.at[part], dst.at[0, part], sems.at[1, i]))
    load_gain = pltpu.make_async_copy(gain, gain_buf, sems.at[0, len(loads)])
    load_gain.start()
    for load in loads:
        load.start()
    load_gain.wait()
    share = gain_out.shape[1]
    place = lax.rem(lax.axis_index("ctx"), 2 * nz) * share
    turned = pltpu.roll(gain_buf[place // DIM], (DIM - place % DIM) % DIM, 1)
    gain_out[...] = turned[0:1, :share]
    for load, store in zip(loads, stores):
        load.wait()
        store.start()
    for store in stores:
        store.wait()


def build(mesh, nx, nz):
    ny = mesh.shape["dp"]
    width = HEADS * DIM
    ry, rx = HEADS // ny, HEADS // ny // nx

    def scan_scratch():
        state = pltpu.VMEM((HALF, DIM, DIM), F32)
        parts = pltpu.VMEM((HALF, nx, DIM // nx, DIM), F32)
        slots = pltpu.VMEM((nx * nz, DIM // nx, DIM), F32)
        return [
            pltpu.VMEM((HEADS, DIM, DIM), F32),
            state,
            parts,
            slots,
            slots,
            parts,
            state,
            state,
            *[pltpu.VMEM((nx, DIM // nx, DIM), F32)] * 3,
            pltpu.SemaphoreType.DMA((HALF,)),
            pltpu.SemaphoreType.DMA,
            *[pltpu.SemaphoreType.DMA((HALF,))] * 2,
            pltpu.SemaphoreType.DMA,
            pltpu.SemaphoreType.DMA((6,)),
        ]

    scratch = [
        *[pltpu.VMEM((DIM, width), BF16)] * 7,
        *[pltpu.VMEM((HEADS, DIM, DIM), BF16)] * 3,
        *[pltpu.VMEM((HEADS, DIM, DIM), F32)] * 3,
        pltpu.VMEM((HEADS, 8, DIM), F32),
        pltpu.VMEM((ny - 1, ry, 8, DIM), F32),
        pltpu.VMEM((ry, 8, DIM), F32),
        pltpu.VMEM((nx - 1, rx, 8, DIM), F32),
        pltpu.VMEM((rx, 8, DIM), F32),
        pltpu.VMEM((nz - 1, rx, 8, DIM), F32),
        pltpu.VMEM((rx, 8, DIM), F32),
        pltpu.VMEM((rx, 8, DIM), F32),
        *scan_scratch(),
        *scan_scratch(),
        pltpu.SemaphoreType.DMA((4,)),
        pltpu.SemaphoreType.DMA((3,)),
        pltpu.SemaphoreType.DMA((4,)),
        pltpu.SemaphoreType.DMA((ny - 1,)),
        pltpu.SemaphoreType.DMA((nx - 1,)),
        pltpu.SemaphoreType.DMA((nz - 1,)),
        pltpu.SemaphoreType.DMA,
    ]

    def body(queries, key_rows, value_rows, out_grad, norm_gain):
        rows = jax.ShapeDtypeStruct(queries.shape, BF16)
        dq, dk, dv, dgain = pl.pallas_call(
            functools.partial(kernel, (ny, nx, nz)),
            out_shape=(rows, rows, rows, jax.ShapeDtypeStruct((rx, 8, DIM), F32)),
            in_specs=[pl.BlockSpec(memory_space=pl.ANY)] * 4 + [pl.BlockSpec(memory_space=pltpu.VMEM)],
            out_specs=[pl.BlockSpec(memory_space=pl.ANY)] * 3 + [pl.BlockSpec(memory_space=pltpu.VMEM)],
            scratch_shapes=scratch,
            compiler_params=pltpu.CompilerParams(
                collective_id=0, has_side_effects=True, vmem_limit_bytes=62 * 1024 * 1024
            ),
        )(queries, key_rows, value_rows, out_grad, norm_gain.reshape(1, width))
        share = rx * DIM // (2 * nz)
        dq, dk, dv, dgain = pl.pallas_call(
            functools.partial(hand_over, nz),
            out_shape=(rows, rows, rows, jax.ShapeDtypeStruct((1, share), F32)),
            in_specs=[pl.BlockSpec(memory_space=pl.ANY)] * 4,
            out_specs=[pl.BlockSpec(memory_space=pl.ANY)] * 3 + [pl.BlockSpec(memory_space=pltpu.VMEM)],
            scratch_shapes=[
                *[pltpu.VMEM((DIM, width), BF16)] * 3,
                pltpu.VMEM((rx, 8, DIM), F32),
                pltpu.SemaphoreType.DMA((2, 3 * (DIM // BLOCK) + 1)),
            ],
            compiler_params=pltpu.CompilerParams(vmem_limit_bytes=62 * 1024 * 1024),
        )(dq, dk, dv, dgain)
        return dq, dk, dv, dgain.reshape(share)

    placed = P("dp", "ctx", None)
    return jax.shard_map(
        body,
        mesh=mesh,
        in_specs=(placed, placed, placed, placed, P()),
        out_specs=(placed, placed, placed, P(("dp", "ctx"))),
        check_vma=False,
    )


def solution(mesh):
    return build(mesh, 4, 8)
```

```python
import functools
import math

import jax
import jax.numpy as jnp
from jax import lax
from jax.experimental import pallas as pl
from jax.experimental.pallas import tpu as pltpu
from jax.sharding import PartitionSpec as P

HEADS = 16
HALF = 8
DIM = 128
EPSILON = 1e-05
MESH = pl.DeviceIdType.MESH
F32 = jnp.float32
BF16 = jnp.bfloat16

LAG = 2
SUM_LAG = 2
EARLY_ONE = 5
EARLY_TWO = 4
BLOCK = 32


def dot(a, b, ca, cb):
    return lax.dot_general(a, b, (((ca,), (cb,)), ((), ())), preferred_element_type=F32)


def listed(places, e):
    packed = sum(place << (3 * i) for i, place in enumerate(places))
    return lax.shift_right_logical(jnp.int32(packed), jnp.int32(3) * e) % 8


MAKE = (4, 5, 3, 6, 2, 7, 1, 0)
SEND = (5, 3, 6, 2, 7, 1)
WORK = (5, 0, 3, 4, 6, 2, 7, 1)


def ring(places, e, z, nz):
    away = listed(places, e)
    return (z + away + (z % 2) * (nz - 2 * away)) % nz


class Scan:
    def __init__(self, sizes, pos, order, bufs, sems):
        self.nx, self.nz = sizes
        self.y, self.x, self.z, self.c = pos
        self.order = order
        self.pc = self.c if order > 0 else 1 - self.c
        self.slot = self.x * self.nz + self.z
        self.mate = self.z + 1 - 2 * (self.z % 2)
        self.first = self.z % 2 == (0 if order > 0 else 1)
        self.far = (self.z + self.nz // 2) % self.nz
        self.passed = (self.mate + self.nz // 2) % self.nz
        (self.own, self.exch, self.s, self.gin, self.pout, self.pin, self.bkin, self.bkout, self.given, self.both, self.on) = bufs
        self.re, self.ri, self.ro, self.rb, self.rg, self.sends = sems

    def device(self, x, z, c):
        return (self.y, (x * self.nz + z) * 2 + c)

    def partner(self):
        return self.device(self.x, self.z, 1 - self.c)

    def remote(self, src, dst, which, recv, to):
        return pltpu.make_async_remote_copy(
            src_ref=src, dst_ref=dst, send_sem=self.sends.at[which], recv_sem=recv, device_id=to, device_id_type=MESH
        )

    def exch_copy(self, m):
        return self.remote(self.own.at[(1 - self.c) * HALF + m], self.exch.at[m], 0, self.re.at[m], self.partner())

    def clear(self):
        for x in range(self.nx):
            self.gin[x * self.nz + self.far] = jnp.zeros((DIM // self.nx, DIM), F32)

    def give_copy(self):
        to = self.device(self.x, self.mate, self.c)
        return self.remote(self.s.at[self.far], self.given, 4, self.rg, to)

    def on_copy(self):
        to = self.device(self.x, self.mate, self.c)
        return self.remote(self.on, self.pin.at[self.passed], 5, self.ro.at[self.passed], to)

    def in_copy(self, src, m, r):
        return self.remote(src.at[r], self.gin.at[self.slot], 1, self.ri, self.device(r, m, self.c))

    def out_copy(self, x, z):
        to = self.device(x, z, self.c)
        return self.remote(self.pout.at[x * self.nz + z], self.pin.at[self.z, self.x], 2, self.ro.at[self.z], to)

    def bk_copy(self, m):
        return self.remote(self.bkout.at[m], self.bkin.at[m], 3, self.rb.at[m], self.partner())

    def add_chip(self, m):
        self.exch_copy(m).wait_recv()
        parts = (self.nx, DIM // self.nx, DIM)
        self.s[m] = (self.own[self.c * HALF + m] + self.exch[m]).reshape(parts)

        @pl.when(m == self.far)
        def _():
            self.give_copy().start()

        @pl.when((m != self.far) & (m != self.passed))
        def _():
            for i in range(1, self.nx):
                self.in_copy(self.s.at[m], m, (self.x + i) % self.nx).start()

            @pl.when(m == self.z)
            def _():
                self.gin[self.slot] = self.s[m, self.x]

            @pl.when(m != self.z)
            def _():
                self.in_copy(self.s.at[m], m, self.x).start()

    def pass_in(self):
        self.give_copy().wait_recv()
        self.both[...] = self.s[self.passed] + self.given[...]
        for r in range(self.nx):
            self.in_copy(self.both, self.passed, r).start()

    def scan(self):
        slots = self.nx * self.nz
        some = pl.ds(0, slots - self.nx - 1)
        self.remote(self.gin.at[some], self.gin.at[some], 1, self.ri, self.partner()).wait_recv()
        total = jnp.zeros((DIM // self.nx, DIM), F32)
        for i in range(slots):
            slot = i if self.order > 0 else slots - 1 - i
            self.pout[slot] = total
            total = total + self.gin[slot]
        self.pin[self.z, self.x] = self.pout[self.slot]

        @pl.loop(0, self.nz - 2)
        def _(e):
            for i in range(self.nx):
                self.out_copy((self.x + i) % self.nx, ring(SEND, e, self.z, self.nz)).start()

        for i in range(1, self.nx):
            self.out_copy((self.x + i) % self.nx, self.z).start()

    def arrived(self, m, parts):
        part = self.pin.at[m, pl.ds(0, parts)]
        self.remote(part, part, 2, self.ro.at[m], self.partner()).wait_recv()

    def finish(self, m):
        @pl.when(m == self.z)
        def _():
            self.arrived(m, self.nx - 1)

        @pl.when(m != self.z)
        def _():
            self.arrived(m, self.nx)

        @pl.when(m == self.passed)
        def _():
            before = self.pin[m]
            self.on[...] = jnp.where(self.first, before + self.s[m], before)
            self.on_copy().start()
            self.pin[m] = jnp.where(self.first, before, before + self.given[...])

        before = self.pin[m].reshape(DIM, DIM)
        self.bkout[m] = jnp.where(self.pc == 0, before + self.own[self.c * HALF + m], before)
        self.bk_copy(m).start()
        return jnp.where(self.pc == 1, before + self.exch[m], before)

    def finished(self, m):
        self.bk_copy(m).wait_recv()
        return self.bkin[m]

    def drain(self):
        some = pl.ds(0, self.nx * (self.nz - 1) - 1)
        self.remote(self.exch, self.exch, 0, self.re.at[0], self.partner()).wait_send()
        self.remote(self.gin.at[some], self.gin.at[some], 1, self.ri, self.partner()).wait_send()
        self.remote(self.pout.at[some], self.pout.at[some], 2, self.ro.at[0], self.partner()).wait_send()
        self.remote(self.bkout, self.bkin, 3, self.rb.at[0], self.partner()).wait_send()
        self.give_copy().wait_send()
        self.on_copy().wait_send()


def kernel(
    sizes,
    q_hbm,
    k_hbm,
    v_hbm,
    g_hbm,
    gain_ref,
    dq_hbm,
    dk_hbm,
    dv_hbm,
    dgain_ref,
    *scratch,
):
    ny, nx, nz = sizes
    scratch = list(scratch)

    def take(n):
        out = scratch[:n]
        del scratch[:n]
        return out

    q, k, v, g = take(4)
    dq, dk, dv = take(3)
    scores, d_out, prior = take(3)
    out_loc, dk_loc, dv_loc = take(3)
    gtile, gin1, acc1, gin2, acc2, gin3, acc3, gin4 = take(8)
    bufs1, sems1 = take(11), take(6)
    bufs2, sems2 = take(11), take(6)
    in_sem, out_sem, gsend, g1r, g2r, g3r, g4r = take(7)

    y = lax.axis_index("dp")
    ctx = lax.axis_index("ctx")
    x = ctx // (2 * nz)
    z = (ctx // 2) % nz
    c = ctx % 2
    pos = (y, x, z, c)

    def device(y_, x_, z_, c_):
        return (y_, (x_ * nz + z_) * 2 + c_)

    loads = [pltpu.make_async_copy(src.at[0], dst, in_sem.at[i]) for i, (src, dst) in enumerate(((k_hbm, k), (v_hbm, v), (q_hbm, q), (g_hbm, g)))]
    for load in loads:
        load.start()

    def y_peer(i):
        return device((y + i) % ny, x, z, c)

    def x_peer(i):
        return device(y, (x + i) % nx, z, c)

    def z_peer(i):
        return device(y, x, (z + i) % nz, c)

    partner = device(y, x, z, 1 - c)
    barrier = pltpu.get_barrier_semaphore()
    pl.semaphore_signal(barrier, inc=1, device_id=partner, device_id_type=MESH)
    for i in range(1, ny):
        pl.semaphore_signal(barrier, inc=1, device_id=y_peer(i), device_id_type=MESH)

    @pl.loop(1, nx * nz)
    def _(i):
        to = (x * nz + z + i) % (nx * nz)
        pl.semaphore_signal(barrier, inc=1, device_id=(y, to * 2 + c), device_id_type=MESH)

    one = Scan((nx, nz), pos, 1, bufs1, sems1)
    two = Scan((nx, nz), pos, -1, bufs2, sems2)
    one.clear()
    two.clear()

    def col(h):
        return pl.ds(pl.multiple_of(h * DIM, DIM), DIM)

    mine, other = c * HALF, (1 - c) * HALF

    def columns(ref, heads):
        return [ref[:, col(h)] for h in heads]

    def local_states(heads):
        ks, vs = columns(k, heads), columns(v, heads)
        states = [dot(kh, vh, 0, 0) for kh, vh in zip(ks, vs)]
        for h, state in zip(heads, states):
            one.own[h] = state

    loads[0].wait()
    loads[1].wait()

    def place(e):
        return ring(MAKE, jnp.int32(e), z, nz)

    for i in range(0, HALF, 4):
        local_states([other + place(i + u) for u in range(4)])
        if i == 0:
            pl.semaphore_wait(barrier, nx * nz + ny - 1)
        for u in range(4):
            one.exch_copy(place(i + u)).start()

    for i in range(0, HALF, 4):
        local_states([mine + place(i + u) for u in range(4)])
        for u in range(4):
            one.add_chip(place(i + u))
    one.pass_in()

    loads[2].wait()
    loads[3].wait()

    keep = lax.broadcasted_iota(jnp.int32, (DIM, DIM), 0) >= lax.broadcasted_iota(jnp.int32, (DIM, DIM), 1)

    def before_one(heads):
        qs, ks, vs = columns(q, heads), columns(k, heads), columns(v, heads)
        raw = [dot(qh, kh, 1, 1) for qh, kh in zip(qs, ks)]
        lows = [jnp.where(keep, r, 0.0).astype(BF16) for r in raw]
        outs = [dot(low, vh, 1, 0) for low, vh in zip(lows, vs)]
        for h, low, out in zip(heads, lows, outs):
            scores[h] = low
            out_loc[h] = out

    def pass_one(heads, states):
        qs = columns(q, heads)
        gfs = [gh.astype(F32) for gh in columns(g, heads)]
        gains = columns(gain_ref, heads)
        locs = [out_loc[h] for h in heads]
        lows = [state.astype(BF16) for state in states]
        outs = [loc + dot(qh, low, 1, 0) for loc, qh, low in zip(locs, qs, lows)]
        invs = [lax.rsqrt(jnp.mean(out * out, axis=1, keepdims=True) + EPSILON) for out in outs]
        normeds = [out * inv for out, inv in zip(outs, invs)]
        gns = [gf * gain for gf, gain in zip(gfs, gains)]
        means = [jnp.mean(gn * normed, axis=1, keepdims=True) for gn, normed in zip(gns, normeds)]
        ds = [((gn - normed * mean) * inv).astype(BF16) for gn, normed, mean, inv in zip(gns, normeds, means, invs)]
        grads = [dot(qh, d, 0, 0) for qh, d in zip(qs, ds)]
        terms = [jnp.sum((gf * normed).reshape(DIM // 8, 8, DIM), axis=0) for gf, normed in zip(gfs, normeds)]
        for h, low, d, grad, term in zip(heads, lows, ds, grads, terms):
            prior[h] = low
            d_out[h] = d
            two.own[h] = grad
            gtile[h] = term

    def between(heads):
        ds, lows, scs = [d_out[h] for h in heads], [prior[h] for h in heads], [scores[h] for h in heads]
        qs, ks, vs = columns(q, heads), columns(k, heads), columns(v, heads)
        raw = [dot(d, vh, 1, 1) for d, vh in zip(ds, vs)]
        dvs = [dot(sc, d, 0, 0) for sc, d in zip(scs, ds)]
        pqs = [dot(d, low, 1, 1) for d, low in zip(ds, lows)]
        gss = [jnp.where(keep, r, 0.0).astype(BF16) for r in raw]
        dqs = [(dot(gs, kh, 1, 0) + pq).astype(BF16) for gs, kh, pq in zip(gss, ks, pqs)]
        dks = [dot(gs, qh, 0, 0) for gs, qh in zip(gss, qs)]
        for h, dqh, dkh, dvh in zip(heads, dqs, dks, dvs):
            dq[:, col(h)] = dqh
            dk_loc[h] = dkh
            dv_loc[h] = dvh

    def store(ref, hbm, i, h):
        return pltpu.make_async_copy(ref.at[:, col(h)], hbm.at[0, :, col(h)], out_sem.at[i])

    def pass_two(heads, states):
        ks, vs = columns(k, heads), columns(v, heads)
        dks, dvs = [dk_loc[h] for h in heads], [dv_loc[h] for h in heads]
        lows = [state.astype(BF16) for state in states]
        dks = [(part + dot(vh, low, 1, 1)).astype(BF16) for part, vh, low in zip(dks, vs, lows)]
        dvs = [(part + dot(kh, low, 1, 0)).astype(BF16) for part, kh, low in zip(dvs, ks, lows)]
        for h, dkh, dvh in zip(heads, dks, dvs):
            dk[:, col(h)] = dkh
            dv[:, col(h)] = dvh
        for h in heads:
            store(dk, dk_hbm, 1, h).start()
            store(dv, dv_hbm, 2, h).start()

    ry, rx = HEADS // ny, HEADS // ny // nx

    def g1_copy(i):
        src = gtile.at[pl.ds(((y + i) % ny) * ry, ry)]
        return pltpu.make_async_remote_copy(
            src_ref=src, dst_ref=gin1.at[i - 1], send_sem=gsend.at[0], recv_sem=g1r.at[i - 1], device_id=y_peer(i), device_id_type=MESH
        )

    def g2_copy(i):
        src = acc1.at[pl.ds(((x + i) % nx) * rx, rx)]
        return pltpu.make_async_remote_copy(
            src_ref=src, dst_ref=gin2.at[i - 1], send_sem=gsend.at[1], recv_sem=g2r.at[i - 1], device_id=x_peer(i), device_id_type=MESH
        )

    def g3_copy(i):
        return pltpu.make_async_remote_copy(
            src_ref=acc2, dst_ref=gin3.at[i - 1], send_sem=gsend.at[2], recv_sem=g3r.at[i - 1], device_id=z_peer(i), device_id_type=MESH
        )

    def g4_copy():
        return pltpu.make_async_remote_copy(
            src_ref=acc3, dst_ref=gin4, send_sem=gsend.at[3], recv_sem=g4r, device_id=partner, device_id_type=MESH
        )

    def gain_step(stage):
        if stage == 0:
            for i in range(1, ny):
                g1_copy(i).start()
        elif stage == 1:
            total = gtile[pl.ds(y * ry, ry)]
            for i in range(1, ny):
                g1_copy(i).wait_recv()
                total = total + gin1[i - 1]
            acc1[...] = total
            for i in range(1, nx):
                g2_copy(i).start()
        elif stage == 2:
            total = acc1[pl.ds(x * rx, rx)]
            for i in range(1, nx):
                g2_copy(i).wait_recv()
                total = total + gin2[i - 1]
            acc2[...] = total
            for i in range(1, nz):
                g3_copy(i).start()
        elif stage == 3:
            total = acc2[...]
            for i in range(1, nz):
                g3_copy(i).wait_recv()
                total = total + gin3[i - 1]
            acc3[...] = total
            g4_copy().start()
        else:
            g4_copy().wait_recv()
            scale = 1.0 / math.sqrt(ny * nx * nz * 2 * DIM)
            total = jnp.sum(acc3[...] + gin4[...], axis=1, keepdims=True) * scale
            dgain_ref[...] = jnp.broadcast_to(total, dgain_ref.shape)

    def arrival(e):
        return ring(WORK, e, z, nz)

    def finishing(scan, work, after, last, final, fill):
        @pl.loop(0, HALF + LAG + SUM_LAG)
        def _(e):
            fill(e)

            @pl.when(e >= LAG + SUM_LAG)
            def _():
                last(arrival(e - LAG - SUM_LAG))

            @pl.when(e == HALF + LAG)
            def _():
                final()

            @pl.when(e < LAG)
            def _():
                m = arrival(e)
                work([mine + m], [scan.finish(m)])

            @pl.when((e >= LAG) & (e < HALF))
            def _():
                m, n = arrival(e), arrival(e - LAG)
                state = scan.finish(m)
                work([mine + m, other + n], [state, scan.finished(n)])
                after(n)

            @pl.when((e >= HALF) & (e < HALF + LAG))
            def _():
                n = arrival(e - LAG)
                work([other + n], [scan.finished(n)])
                after(n)

    def nothing(*_):
        pass

    def pair(work, e):
        m = arrival(e)
        work([mine + m, other + m])

    @pl.loop(0, EARLY_ONE)
    def _(e):
        pair(before_one, e)

    one.scan()

    def fill_one(e):
        @pl.when(e < HALF - EARLY_ONE)
        def _():
            pair(before_one, e + EARLY_ONE)

    finishing(one, pass_one, lambda m: two.exch_copy(m).start(), two.add_chip, two.pass_in, fill_one)
    gain_step(0)

    @pl.loop(0, EARLY_TWO)
    def _(e):
        pair(between, e)

    two.scan()
    gain_step(1)

    def fill_two(e):
        @pl.when(e < HALF - EARLY_TWO)
        def _():
            pair(between, e + EARLY_TWO)

        @pl.when(e == HALF - EARLY_TWO)
        def _():
            gain_step(2)
            pltpu.make_async_copy(dq, dq_hbm.at[0], out_sem.at[0]).start()

        @pl.when(e == HALF)
        def _():
            gain_step(3)

    finishing(two, pass_two, nothing, nothing, nothing, fill_two)
    gain_step(4)

    one.drain()
    two.drain()
    for i in range(1, ny):
        g1_copy(i).wait_send()
    for i in range(1, nx):
        g2_copy(i).wait_send()
    for i in range(1, nz):
        g3_copy(i).wait_send()
    g4_copy().wait_send()
    for i, (ref, hbm) in enumerate(((dq, dq_hbm), (dk, dk_hbm), (dv, dv_hbm))):
        pltpu.make_async_copy(ref, hbm.at[0], out_sem.at[i]).wait()


def hand_over(nz, a, b, c, gain, a_out, b_out, c_out, gain_out, a_buf, b_buf, c_buf, gain_buf, sems):
    trips = ((a, a_buf, a_out), (b, b_buf, b_out), (c, c_buf, c_out))
    loads, stores = [], []
    for row in range(0, DIM, BLOCK):
        for src, buf, dst in trips:
            part, i = pl.ds(row, BLOCK), len(loads)
            loads.append(pltpu.make_async_copy(src.at[0, part], buf.at[part], sems.at[0, i]))
            stores.append(pltpu.make_async_copy(buf.at[part], dst.at[0, part], sems.at[1, i]))
    load_gain = pltpu.make_async_copy(gain, gain_buf, sems.at[0, len(loads)])
    load_gain.start()
    for load in loads:
        load.start()
    load_gain.wait()
    share = gain_out.shape[1]
    place = lax.rem(lax.axis_index("ctx"), 2 * nz) * share
    turned = pltpu.roll(gain_buf[place // DIM], (DIM - place % DIM) % DIM, 1)
    gain_out[...] = turned[0:1, :share]
    for load, store in zip(loads, stores):
        load.wait()
        store.start()
    for store in stores:
        store.wait()


def build(mesh, nx, nz):
    ny = mesh.shape["dp"]
    width = HEADS * DIM
    ry, rx = HEADS // ny, HEADS // ny // nx

    def scan_scratch():
        state = pltpu.VMEM((HALF, DIM, DIM), F32)
        parts = pltpu.VMEM((HALF, nx, DIM // nx, DIM), F32)
        slots = pltpu.VMEM((nx * nz, DIM // nx, DIM), F32)
        return [
            pltpu.VMEM((HEADS, DIM, DIM), F32),
            state,
            parts,
            slots,
            slots,
            parts,
            state,
            state,
            *[pltpu.VMEM((nx, DIM // nx, DIM), F32)] * 3,
            pltpu.SemaphoreType.DMA((HALF,)),
            pltpu.SemaphoreType.DMA,
            *[pltpu.SemaphoreType.DMA((HALF,))] * 2,
            pltpu.SemaphoreType.DMA,
            pltpu.SemaphoreType.DMA((6,)),
        ]

    scratch = [
        *[pltpu.VMEM((DIM, width), BF16)] * 7,
        *[pltpu.VMEM((HEADS, DIM, DIM), BF16)] * 3,
        *[pltpu.VMEM((HEADS, DIM, DIM), F32)] * 3,
        pltpu.VMEM((HEADS, 8, DIM), F32),
        pltpu.VMEM((ny - 1, ry, 8, DIM), F32),
        pltpu.VMEM((ry, 8, DIM), F32),
        pltpu.VMEM((nx - 1, rx, 8, DIM), F32),
        pltpu.VMEM((rx, 8, DIM), F32),
        pltpu.VMEM((nz - 1, rx, 8, DIM), F32),
        pltpu.VMEM((rx, 8, DIM), F32),
        pltpu.VMEM((rx, 8, DIM), F32),
        *scan_scratch(),
        *scan_scratch(),
        pltpu.SemaphoreType.DMA((4,)),
        pltpu.SemaphoreType.DMA((3,)),
        pltpu.SemaphoreType.DMA((4,)),
        pltpu.SemaphoreType.DMA((ny - 1,)),
        pltpu.SemaphoreType.DMA((nx - 1,)),
        pltpu.SemaphoreType.DMA((nz - 1,)),
        pltpu.SemaphoreType.DMA,
    ]

    def body(queries, key_rows, value_rows, out_grad, norm_gain):
        rows = jax.ShapeDtypeStruct(queries.shape, BF16)
        dq, dk, dv, dgain = pl.pallas_call(
            functools.partial(kernel, (ny, nx, nz)),
            out_shape=(rows, rows, rows, jax.ShapeDtypeStruct((rx, 8, DIM), F32)),
            in_specs=[pl.BlockSpec(memory_space=pl.ANY)] * 4 + [pl.BlockSpec(memory_space=pltpu.VMEM)],
            out_specs=[pl.BlockSpec(memory_space=pl.ANY)] * 3 + [pl.BlockSpec(memory_space=pltpu.VMEM)],
            scratch_shapes=scratch,
            compiler_params=pltpu.CompilerParams(
                collective_id=0, has_side_effects=True, vmem_limit_bytes=62 * 1024 * 1024
            ),
        )(queries, key_rows, value_rows, out_grad, norm_gain.reshape(1, width))
        share = rx * DIM // (2 * nz)
        dq, dk, dv, dgain = pl.pallas_call(
            functools.partial(hand_over, nz),
            out_shape=(rows, rows, rows, jax.ShapeDtypeStruct((1, share), F32)),
            in_specs=[pl.BlockSpec(memory_space=pl.ANY)] * 4,
            out_specs=[pl.BlockSpec(memory_space=pl.ANY)] * 3 + [pl.BlockSpec(memory_space=pltpu.VMEM)],
            scratch_shapes=[
                *[pltpu.VMEM((DIM, width), BF16)] * 3,
                pltpu.VMEM((rx, 8, DIM), F32),
                pltpu.SemaphoreType.DMA((2, 3 * (DIM // BLOCK) + 1)),
            ],
            compiler_params=pltpu.CompilerParams(vmem_limit_bytes=62 * 1024 * 1024),
        )(dq, dk, dv, dgain)
        return dq, dk, dv, dgain.reshape(share)

    placed = P("dp", "ctx", None)
    return jax.shard_map(
        body,
        mesh=mesh,
        in_specs=(placed, placed, placed, placed, P()),
        out_specs=(placed, placed, placed, P(("dp", "ctx"))),
        check_vma=False,
    )


def solution(mesh):
    return build(mesh, 4, 8)
```

```python
import functools
import math

import jax
import jax.numpy as jnp
from jax import lax
from jax.experimental import pallas as pl
from jax.experimental.pallas import tpu as pltpu
from jax.sharding import PartitionSpec as P

HEADS = 16
HALF = 8
DIM = 128
EPSILON = 1e-05
MESH = pl.DeviceIdType.MESH
F32 = jnp.float32
BF16 = jnp.bfloat16

LAG = 2
SUM_LAG = 2
BLOCK = 32


def dot(a, b, ca, cb):
    return lax.dot_general(a, b, (((ca,), (cb,)), ((), ())), preferred_element_type=F32)


def listed(places, e):
    packed = sum(place << (3 * i) for i, place in enumerate(places))
    return lax.shift_right_logical(jnp.int32(packed), jnp.int32(3) * e) % 8


MAKE = (4, 5, 3, 6, 2, 7, 1, 0)
SEND = (5, 3, 6, 2, 7, 1)
WORK = (5, 0, 3, 4, 6, 2, 7, 1)


def ring(places, e, z, nz):
    away = listed(places, e)
    return (z + away + (z % 2) * (nz - 2 * away)) % nz


class Scan:
    def __init__(self, sizes, pos, order, bufs, sems):
        self.nx, self.nz = sizes
        self.y, self.x, self.z, self.c = pos
        self.order = order
        self.pc = self.c if order > 0 else 1 - self.c
        self.slot = self.x * self.nz + self.z
        self.mate = self.z + 1 - 2 * (self.z % 2)
        self.first = self.z % 2 == (0 if order > 0 else 1)
        self.far = (self.z + self.nz // 2) % self.nz
        self.passed = (self.mate + self.nz // 2) % self.nz
        (self.own, self.exch, self.s, self.gin, self.pout, self.pin, self.bkin, self.bkout, self.given, self.both, self.on) = bufs
        self.re, self.ri, self.ro, self.rb, self.rg, self.sends = sems

    def device(self, x, z, c):
        return (self.y, (x * self.nz + z) * 2 + c)

    def partner(self):
        return self.device(self.x, self.z, 1 - self.c)

    def remote(self, src, dst, which, recv, to):
        return pltpu.make_async_remote_copy(
            src_ref=src, dst_ref=dst, send_sem=self.sends.at[which], recv_sem=recv, device_id=to, device_id_type=MESH
        )

    def exch_copy(self, m):
        return self.remote(self.own.at[(1 - self.c) * HALF + m], self.exch.at[m], 0, self.re.at[m], self.partner())

    def clear(self):
        for x in range(self.nx):
            self.gin[x * self.nz + self.far] = jnp.zeros((DIM // self.nx, DIM), F32)

    def give_copy(self):
        to = self.device(self.x, self.mate, self.c)
        return self.remote(self.s.at[self.far], self.given, 4, self.rg, to)

    def on_copy(self):
        to = self.device(self.x, self.mate, self.c)
        return self.remote(self.on, self.pin.at[self.passed], 5, self.ro.at[self.passed], to)

    def in_copy(self, src, m, r):
        return self.remote(src.at[r], self.gin.at[self.slot], 1, self.ri, self.device(r, m, self.c))

    def out_copy(self, x, z):
        to = self.device(x, z, self.c)
        return self.remote(self.pout.at[x * self.nz + z], self.pin.at[self.z, self.x], 2, self.ro.at[self.z], to)

    def bk_copy(self, m):
        return self.remote(self.bkout.at[m], self.bkin.at[m], 3, self.rb.at[m], self.partner())

    def add_chip(self, m):
        self.exch_copy(m).wait_recv()
        parts = (self.nx, DIM // self.nx, DIM)
        self.s[m] = (self.own[self.c * HALF + m] + self.exch[m]).reshape(parts)

        @pl.when(m == self.far)
        def _():
            self.give_copy().start()

        @pl.when((m != self.far) & (m != self.passed))
        def _():
            for i in range(1, self.nx):
                self.in_copy(self.s.at[m], m, (self.x + i) % self.nx).start()

            @pl.when(m == self.z)
            def _():
                self.gin[self.slot] = self.s[m, self.x]

            @pl.when(m != self.z)
            def _():
                self.in_copy(self.s.at[m], m, self.x).start()

    def pass_in(self):
        self.give_copy().wait_recv()
        self.both[...] = self.s[self.passed] + self.given[...]
        for r in range(self.nx):
            self.in_copy(self.both, self.passed, r).start()

    def scan(self):
        slots = self.nx * self.nz
        some = pl.ds(0, slots - self.nx - 1)
        self.remote(self.gin.at[some], self.gin.at[some], 1, self.ri, self.partner()).wait_recv()
        total = jnp.zeros((DIM // self.nx, DIM), F32)
        for i in range(slots):
            slot = i if self.order > 0 else slots - 1 - i
            self.pout[slot] = total
            total = total + self.gin[slot]
        self.pin[self.z, self.x] = self.pout[self.slot]

        @pl.loop(0, self.nz - 2)
        def _(e):
            for i in range(self.nx):
                self.out_copy((self.x + i) % self.nx, ring(SEND, e, self.z, self.nz)).start()

        for i in range(1, self.nx):
            self.out_copy((self.x + i) % self.nx, self.z).start()

    def arrived(self, m, parts):
        part = self.pin.at[m, pl.ds(0, parts)]
        self.remote(part, part, 2, self.ro.at[m], self.partner()).wait_recv()

    def finish(self, m):
        @pl.when(m == self.z)
        def _():
            self.arrived(m, self.nx - 1)

        @pl.when(m != self.z)
        def _():
            self.arrived(m, self.nx)

        @pl.when(m == self.passed)
        def _():
            before = self.pin[m]
            self.on[...] = jnp.where(self.first, before + self.s[m], before)
            self.on_copy().start()
            self.pin[m] = jnp.where(self.first, before, before + self.given[...])

        before = self.pin[m].reshape(DIM, DIM)
        self.bkout[m] = jnp.where(self.pc == 0, before + self.own[self.c * HALF + m], before)
        self.bk_copy(m).start()
        return jnp.where(self.pc == 1, before + self.exch[m], before)

    def finished(self, m):
        self.bk_copy(m).wait_recv()
        return self.bkin[m]

    def drain(self):
        some = pl.ds(0, self.nx * (self.nz - 1) - 1)
        self.remote(self.exch, self.exch, 0, self.re.at[0], self.partner()).wait_send()
        self.remote(self.gin.at[some], self.gin.at[some], 1, self.ri, self.partner()).wait_send()
        self.remote(self.pout.at[some], self.pout.at[some], 2, self.ro.at[0], self.partner()).wait_send()
        self.remote(self.bkout, self.bkin, 3, self.rb.at[0], self.partner()).wait_send()
        self.give_copy().wait_send()
        self.on_copy().wait_send()


def kernel(
    sizes,
    q_hbm,
    k_hbm,
    v_hbm,
    g_hbm,
    gain_ref,
    dq_hbm,
    dk_hbm,
    dv_hbm,
    dgain_ref,
    *scratch,
):
    ny, nx, nz = sizes
    scratch = list(scratch)

    def take(n):
        out = scratch[:n]
        del scratch[:n]
        return out

    q, k, v, g = take(4)
    dq, dk, dv = take(3)
    scores, d_out, prior = take(3)
    out_loc, dk_loc, dv_loc = take(3)
    gtile, gin1, acc1, gin2, acc2, gin3, acc3, gin4 = take(8)
    bufs1, sems1 = take(11), take(6)
    bufs2, sems2 = take(11), take(6)
    in_sem, out_sem, gsend, g1r, g2r, g3r, g4r = take(7)

    y = lax.axis_index("dp")
    ctx = lax.axis_index("ctx")
    x = ctx // (2 * nz)
    z = (ctx // 2) % nz
    c = ctx % 2
    pos = (y, x, z, c)

    def device(y_, x_, z_, c_):
        return (y_, (x_ * nz + z_) * 2 + c_)

    loads = [pltpu.make_async_copy(src.at[0], dst, in_sem.at[i]) for i, (src, dst) in enumerate(((k_hbm, k), (v_hbm, v), (q_hbm, q), (g_hbm, g)))]
    for load in loads:
        load.start()

    def y_peer(i):
        return device((y + i) % ny, x, z, c)

    def x_peer(i):
        return device(y, (x + i) % nx, z, c)

    def z_peer(i):
        return device(y, x, (z + i) % nz, c)

    partner = device(y, x, z, 1 - c)
    barrier = pltpu.get_barrier_semaphore()
    pl.semaphore_signal(barrier, inc=1, device_id=partner, device_id_type=MESH)
    for i in range(1, ny):
        pl.semaphore_signal(barrier, inc=1, device_id=y_peer(i), device_id_type=MESH)

    @pl.loop(1, nx * nz)
    def _(i):
        to = (x * nz + z + i) % (nx * nz)
        pl.semaphore_signal(barrier, inc=1, device_id=(y, to * 2 + c), device_id_type=MESH)

    one = Scan((nx, nz), pos, 1, bufs1, sems1)
    two = Scan((nx, nz), pos, -1, bufs2, sems2)
    one.clear()
    two.clear()

    def col(h):
        return pl.ds(pl.multiple_of(h * DIM, DIM), DIM)

    mine, other = c * HALF, (1 - c) * HALF

    def columns(ref, heads):
        return [ref[:, col(h)] for h in heads]

    def local_states(heads):
        ks, vs = columns(k, heads), columns(v, heads)
        states = [dot(kh, vh, 0, 0) for kh, vh in zip(ks, vs)]
        for h, state in zip(heads, states):
            one.own[h] = state

    loads[0].wait()
    loads[1].wait()

    def place(e):
        return ring(MAKE, jnp.int32(e), z, nz)

    for i in range(0, HALF, 4):
        local_states([other + place(i + u) for u in range(4)])
        if i == 0:
            pl.semaphore_wait(barrier, nx * nz + ny - 1)
        for u in range(4):
            one.exch_copy(place(i + u)).start()

    for i in range(0, HALF, 4):
        local_states([mine + place(i + u) for u in range(4)])
        for u in range(4):
            one.add_chip(place(i + u))
    one.pass_in()

    loads[2].wait()
    loads[3].wait()

    keep = lax.broadcasted_iota(jnp.int32, (DIM, DIM), 0) >= lax.broadcasted_iota(jnp.int32, (DIM, DIM), 1)

    def before_one(heads):
        qs, ks, vs = columns(q, heads), columns(k, heads), columns(v, heads)
        raw = [dot(qh, kh, 1, 1) for qh, kh in zip(qs, ks)]
        lows = [jnp.where(keep, r, 0.0).astype(BF16) for r in raw]
        outs = [dot(low, vh, 1, 0) for low, vh in zip(lows, vs)]
        for h, low, out in zip(heads, lows, outs):
            scores[h] = low
            out_loc[h] = out

    def pass_one(heads, states):
        qs = columns(q, heads)
        gfs = [gh.astype(F32) for gh in columns(g, heads)]
        gains = columns(gain_ref, heads)
        locs = [out_loc[h] for h in heads]
        lows = [state.astype(BF16) for state in states]
        outs = [loc + dot(qh, low, 1, 0) for loc, qh, low in zip(locs, qs, lows)]
        invs = [lax.rsqrt(jnp.mean(out * out, axis=1, keepdims=True) + EPSILON) for out in outs]
        normeds = [out * inv for out, inv in zip(outs, invs)]
        gns = [gf * gain for gf, gain in zip(gfs, gains)]
        means = [jnp.mean(gn * normed, axis=1, keepdims=True) for gn, normed in zip(gns, normeds)]
        ds = [((gn - normed * mean) * inv).astype(BF16) for gn, normed, mean, inv in zip(gns, normeds, means, invs)]
        grads = [dot(qh, d, 0, 0) for qh, d in zip(qs, ds)]
        terms = [jnp.sum((gf * normed).reshape(DIM // 8, 8, DIM), axis=0) for gf, normed in zip(gfs, normeds)]
        for h, low, d, grad, term in zip(heads, lows, ds, grads, terms):
            prior[h] = low
            d_out[h] = d
            two.own[h] = grad
            gtile[h] = term

    def between(heads):
        ds, lows, scs = [d_out[h] for h in heads], [prior[h] for h in heads], [scores[h] for h in heads]
        qs, ks, vs = columns(q, heads), columns(k, heads), columns(v, heads)
        raw = [dot(d, vh, 1, 1) for d, vh in zip(ds, vs)]
        dvs = [dot(sc, d, 0, 0) for sc, d in zip(scs, ds)]
        pqs = [dot(d, low, 1, 1) for d, low in zip(ds, lows)]
        gss = [jnp.where(keep, r, 0.0).astype(BF16) for r in raw]
        dqs = [(dot(gs, kh, 1, 0) + pq).astype(BF16) for gs, kh, pq in zip(gss, ks, pqs)]
        dks = [dot(gs, qh, 0, 0) for gs, qh in zip(gss, qs)]
        for h, dqh, dkh, dvh in zip(heads, dqs, dks, dvs):
            dq[:, col(h)] = dqh
            dk_loc[h] = dkh
            dv_loc[h] = dvh

    def store(ref, hbm, i, h):
        return pltpu.make_async_copy(ref.at[:, col(h)], hbm.at[0, :, col(h)], out_sem.at[i])

    def pass_two(heads, states):
        ks, vs = columns(k, heads), columns(v, heads)
        dks, dvs = [dk_loc[h] for h in heads], [dv_loc[h] for h in heads]
        lows = [state.astype(BF16) for state in states]
        dks = [(part + dot(vh, low, 1, 1)).astype(BF16) for part, vh, low in zip(dks, vs, lows)]
        dvs = [(part + dot(kh, low, 1, 0)).astype(BF16) for part, kh, low in zip(dvs, ks, lows)]
        for h, dkh, dvh in zip(heads, dks, dvs):
            dk[:, col(h)] = dkh
            dv[:, col(h)] = dvh
        for h in heads:
            store(dk, dk_hbm, 1, h).start()
            store(dv, dv_hbm, 2, h).start()

    ry, rx = HEADS // ny, HEADS // ny // nx

    def g1_copy(i):
        src = gtile.at[pl.ds(((y + i) % ny) * ry, ry)]
        return pltpu.make_async_remote_copy(
            src_ref=src, dst_ref=gin1.at[i - 1], send_sem=gsend.at[0], recv_sem=g1r.at[i - 1], device_id=y_peer(i), device_id_type=MESH
        )

    def g2_copy(i):
        src = acc1.at[pl.ds(((x + i) % nx) * rx, rx)]
        return pltpu.make_async_remote_copy(
            src_ref=src, dst_ref=gin2.at[i - 1], send_sem=gsend.at[1], recv_sem=g2r.at[i - 1], device_id=x_peer(i), device_id_type=MESH
        )

    def g3_copy(i):
        return pltpu.make_async_remote_copy(
            src_ref=acc2, dst_ref=gin3.at[i - 1], send_sem=gsend.at[2], recv_sem=g3r.at[i - 1], device_id=z_peer(i), device_id_type=MESH
        )

    def g4_copy():
        return pltpu.make_async_remote_copy(
            src_ref=acc3, dst_ref=gin4, send_sem=gsend.at[3], recv_sem=g4r, device_id=partner, device_id_type=MESH
        )

    def gain_step(stage):
        if stage == 0:
            for i in range(1, ny):
                g1_copy(i).start()
        elif stage == 1:
            total = gtile[pl.ds(y * ry, ry)]
            for i in range(1, ny):
                g1_copy(i).wait_recv()
                total = total + gin1[i - 1]
            acc1[...] = total
            for i in range(1, nx):
                g2_copy(i).start()
        elif stage == 2:
            total = acc1[pl.ds(x * rx, rx)]
            for i in range(1, nx):
                g2_copy(i).wait_recv()
                total = total + gin2[i - 1]
            acc2[...] = total
            for i in range(1, nz):
                g3_copy(i).start()
        elif stage == 3:
            total = acc2[...]
            for i in range(1, nz):
                g3_copy(i).wait_recv()
                total = total + gin3[i - 1]
            acc3[...] = total
            g4_copy().start()
        else:
            g4_copy().wait_recv()
            scale = 1.0 / math.sqrt(ny * nx * nz * 2 * DIM)
            total = jnp.sum(acc3[...] + gin4[...], axis=1, keepdims=True) * scale
            dgain_ref[...] = jnp.broadcast_to(total, dgain_ref.shape)

    def arrival(e):
        return ring(WORK, e, z, nz)

    def finishing(scan, work, after, last, final):
        @pl.loop(0, HALF + LAG + SUM_LAG)
        def _(e):
            @pl.when(e >= LAG + SUM_LAG)
            def _():
                last(arrival(e - LAG - SUM_LAG))

            @pl.when(e == HALF + LAG)
            def _():
                final()

            @pl.when(e < LAG)
            def _():
                m = arrival(e)
                work([mine + m], [scan.finish(m)])

            @pl.when((e >= LAG) & (e < HALF))
            def _():
                m, n = arrival(e), arrival(e - LAG)
                state = scan.finish(m)
                work([mine + m, other + n], [state, scan.finished(n)])
                after(n)

            @pl.when((e >= HALF) & (e < HALF + LAG))
            def _():
                n = arrival(e - LAG)
                work([other + n], [scan.finished(n)])
                after(n)

    def nothing(*_):
        pass

    @pl.loop(0, HALF)
    def _(m):
        before_one([mine + m, other + m])

    one.scan()
    finishing(one, pass_one, lambda m: two.exch_copy(m).start(), two.add_chip, two.pass_in)
    gain_step(0)

    @pl.loop(0, HALF)
    def _(m):
        between([mine + m, other + m])

        @pl.when(m == HALF // 2)
        def _():
            gain_step(1)

    pltpu.make_async_copy(dq, dq_hbm.at[0], out_sem.at[0]).start()
    gain_step(2)
    two.scan()
    gain_step(3)
    finishing(two, pass_two, nothing, nothing, nothing)
    gain_step(4)

    one.drain()
    two.drain()
    for i in range(1, ny):
        g1_copy(i).wait_send()
    for i in range(1, nx):
        g2_copy(i).wait_send()
    for i in range(1, nz):
        g3_copy(i).wait_send()
    g4_copy().wait_send()
    for i, (ref, hbm) in enumerate(((dq, dq_hbm), (dk, dk_hbm), (dv, dv_hbm))):
        pltpu.make_async_copy(ref, hbm.at[0], out_sem.at[i]).wait()


def hand_over(nz, a, b, c, gain, a_out, b_out, c_out, gain_out, gain_buf, sems):
    stores = []
    for row in range(0, DIM, BLOCK):
        for src, dst in ((a, a_out), (b, b_out), (c, c_out)):
            part = pl.ds(row, BLOCK)
            stores.append(pltpu.make_async_copy(src.at[0, part], dst.at[0, part], sems.at[len(stores)]))
    load_gain = pltpu.make_async_copy(gain, gain_buf, sems.at[len(stores)])
    load_gain.start()
    for store in stores:
        store.start()
    load_gain.wait()
    share = gain_out.shape[1]
    place = lax.rem(lax.axis_index("ctx"), 2 * nz) * share
    turned = pltpu.roll(gain_buf[place // DIM], (DIM - place % DIM) % DIM, 1)
    gain_out[...] = turned[0:1, :share]
    for store in stores:
        store.wait()


def build(mesh, nx, nz):
    ny = mesh.shape["dp"]
    width = HEADS * DIM
    ry, rx = HEADS // ny, HEADS // ny // nx

    def scan_scratch():
        state = pltpu.VMEM((HALF, DIM, DIM), F32)
        parts = pltpu.VMEM((HALF, nx, DIM // nx, DIM), F32)
        slots = pltpu.VMEM((nx * nz, DIM // nx, DIM), F32)
        return [
            pltpu.VMEM((HEADS, DIM, DIM), F32),
            state,
            parts,
            slots,
            slots,
            parts,
            state,
            state,
            *[pltpu.VMEM((nx, DIM // nx, DIM), F32)] * 3,
            pltpu.SemaphoreType.DMA((HALF,)),
            pltpu.SemaphoreType.DMA,
            *[pltpu.SemaphoreType.DMA((HALF,))] * 2,
            pltpu.SemaphoreType.DMA,
            pltpu.SemaphoreType.DMA((6,)),
        ]

    scratch = [
        *[pltpu.VMEM((DIM, width), BF16)] * 7,
        *[pltpu.VMEM((HEADS, DIM, DIM), BF16)] * 3,
        *[pltpu.VMEM((HEADS, DIM, DIM), F32)] * 3,
        pltpu.VMEM((HEADS, 8, DIM), F32),
        pltpu.VMEM((ny - 1, ry, 8, DIM), F32),
        pltpu.VMEM((ry, 8, DIM), F32),
        pltpu.VMEM((nx - 1, rx, 8, DIM), F32),
        pltpu.VMEM((rx, 8, DIM), F32),
        pltpu.VMEM((nz - 1, rx, 8, DIM), F32),
        pltpu.VMEM((rx, 8, DIM), F32),
        pltpu.VMEM((rx, 8, DIM), F32),
        *scan_scratch(),
        *scan_scratch(),
        pltpu.SemaphoreType.DMA((4,)),
        pltpu.SemaphoreType.DMA((3,)),
        pltpu.SemaphoreType.DMA((4,)),
        pltpu.SemaphoreType.DMA((ny - 1,)),
        pltpu.SemaphoreType.DMA((nx - 1,)),
        pltpu.SemaphoreType.DMA((nz - 1,)),
        pltpu.SemaphoreType.DMA,
    ]

    def body(queries, key_rows, value_rows, out_grad, norm_gain):
        rows = jax.ShapeDtypeStruct(queries.shape, BF16)
        dq, dk, dv, dgain = pl.pallas_call(
            functools.partial(kernel, (ny, nx, nz)),
            out_shape=(*[pltpu.VMEM(queries.shape, BF16)] * 3, pltpu.VMEM((rx, 8, DIM), F32)),
            in_specs=[pl.BlockSpec(memory_space=pl.ANY)] * 4 + [pl.BlockSpec(memory_space=pltpu.VMEM)],
            out_specs=[pl.BlockSpec(memory_space=pl.ANY)] * 3 + [pl.BlockSpec(memory_space=pltpu.VMEM)],
            scratch_shapes=scratch,
            compiler_params=pltpu.CompilerParams(
                collective_id=0, has_side_effects=True, vmem_limit_bytes=62 * 1024 * 1024
            ),
        )(queries, key_rows, value_rows, out_grad, norm_gain.reshape(1, width))
        share = rx * DIM // (2 * nz)
        dq, dk, dv, dgain = pl.pallas_call(
            functools.partial(hand_over, nz),
            out_shape=(rows, rows, rows, jax.ShapeDtypeStruct((1, share), F32)),
            in_specs=[pl.BlockSpec(memory_space=pl.ANY)] * 4,
            out_specs=[pl.BlockSpec(memory_space=pl.ANY)] * 3 + [pl.BlockSpec(memory_space=pltpu.VMEM)],
            scratch_shapes=[pltpu.VMEM((rx, 8, DIM), F32), pltpu.SemaphoreType.DMA((3 * (DIM // BLOCK) + 1,))],
            compiler_params=pltpu.CompilerParams(vmem_limit_bytes=8 * 1024 * 1024),
        )(dq, dk, dv, dgain)
        return dq, dk, dv, dgain.reshape(share)

    placed = P("dp", "ctx", None)
    return jax.shard_map(
        body,
        mesh=mesh,
        in_specs=(placed, placed, placed, placed, P()),
        out_specs=(placed, placed, placed, P(("dp", "ctx"))),
        check_vma=False,
    )


def solution(mesh):
    return build(mesh, 4, 8)
```

```python
import functools
import math

import jax
import jax.numpy as jnp
from jax import lax
from jax.experimental import pallas as pl
from jax.experimental.pallas import tpu as pltpu
from jax.sharding import PartitionSpec as P

HEADS = 16
HALF = 8
DIM = 128
EPSILON = 1e-05
MESH = pl.DeviceIdType.MESH
F32 = jnp.float32
BF16 = jnp.bfloat16

LAG = 2
SUM_LAG = 2
BLOCK = 32


def dot(a, b, ca, cb):
    return lax.dot_general(a, b, (((ca,), (cb,)), ((), ())), preferred_element_type=F32)


def listed(places, e):
    packed = sum(place << (3 * i) for i, place in enumerate(places))
    return lax.shift_right_logical(jnp.int32(packed), jnp.int32(3) * e) % 8


MAKE = (4, 5, 3, 6, 2, 7, 1, 0)
SEND = (5, 3, 6, 2, 7, 1)
WORK = (5, 0, 3, 4, 6, 2, 7, 1)


def ring(places, e, z, nz):
    away = listed(places, e)
    return (z + away + (z % 2) * (nz - 2 * away)) % nz


class Scan:
    def __init__(self, sizes, pos, order, bufs, sems):
        self.nx, self.nz = sizes
        self.y, self.x, self.z, self.c = pos
        self.order = order
        self.pc = self.c if order > 0 else 1 - self.c
        self.slot = self.x * self.nz + self.z
        self.parts = self.nx // 2
        self.scans = self.x % 2 == self.c
        self.xs = [(self.x + i) % self.nx for i in range(self.nx)]
        self.base = [(2 * p + self.c) * 2 * self.nz + self.c for p in range(self.parts)]
        self.mate = self.z + 1 - 2 * (self.z % 2)
        self.first = self.z % 2 == (0 if order > 0 else 1)
        self.far = (self.z + self.nz // 2) % self.nz
        self.passed = (self.mate + self.nz // 2) % self.nz
        (self.own, self.exch, self.s, self.gin, self.pout, self.pin, self.bkin, self.bkout, self.given, self.both, self.on) = bufs
        self.re, self.ri, self.ro, self.rb, self.rg, self.sends = sems

    def device(self, x, z, c):
        return (self.y, (x * self.nz + z) * 2 + c)

    def partner(self):
        return self.device(self.x, self.z, 1 - self.c)

    def remote(self, src, dst, which, recv, to):
        return pltpu.make_async_remote_copy(
            src_ref=src, dst_ref=dst, send_sem=self.sends.at[which], recv_sem=recv, device_id=to, device_id_type=MESH
        )

    def exch_copy(self, m):
        return self.remote(self.own.at[(1 - self.c) * HALF + m], self.exch.at[m], 0, self.re.at[m], self.partner())

    def clear(self):
        for x in range(self.nx):
            self.gin[x * self.nz + self.far] = jnp.zeros((DIM // self.parts, DIM), F32)

    def give_copy(self):
        to = self.device(self.x, self.mate, self.c)
        return self.remote(self.s.at[self.far], self.given, 4, self.rg, to)

    def on_copy(self):
        to = self.device(self.x, self.mate, self.c)
        return self.remote(self.on, self.pin.at[self.passed], 5, self.ro.at[self.passed], to)

    def in_copy(self, src, m, p):
        return self.remote(src.at[p], self.gin.at[self.slot], 1, self.ri, (self.y, self.base[p] + 2 * m))

    def out_copy(self, x, z):
        to = self.device(x, z, self.c)
        return self.remote(self.pout.at[x * self.nz + z], self.pin.at[self.z, self.x // 2], 2, self.ro.at[self.z], to)

    def bk_copy(self, m):
        return self.remote(self.bkout.at[m], self.bkin.at[m], 3, self.rb.at[m], self.partner())

    def add_chip(self, m):
        self.exch_copy(m).wait_recv()
        parts = (self.parts, DIM // self.parts, DIM)
        self.s[m] = (self.own[self.c * HALF + m] + self.exch[m]).reshape(parts)

        @pl.when(m == self.far)
        def _():
            self.give_copy().start()

        @pl.when((m != self.far) & (m != self.passed))
        def _():
            for p in range(self.parts):
                here = (m == self.z) & (self.x == 2 * p + self.c)

                @pl.when(here)
                def _(p=p):
                    self.gin[self.slot] = self.s[m, p]

                @pl.when(jnp.logical_not(here))
                def _(p=p):
                    self.in_copy(self.s.at[m], m, p).start()

    def pass_in(self):
        self.give_copy().wait_recv()
        self.both[...] = self.s[self.passed] + self.given[...]
        for p in range(self.parts):
            self.in_copy(self.both, self.passed, p).start()

    def scan(self):
        pl.when(self.scans)(self.scan_part)

    def scan_part(self):
        slots = self.nx * self.nz
        some = pl.ds(0, slots - self.nx - 1)
        self.remote(self.gin.at[some], self.gin.at[some], 1, self.ri, self.partner()).wait_recv()
        total = jnp.zeros((DIM // self.parts, DIM), F32)
        for i in range(slots):
            slot = i if self.order > 0 else slots - 1 - i
            self.pout[slot] = total
            total = total + self.gin[slot]
        self.pin[self.z, self.x // 2] = self.pout[self.slot]

        @pl.loop(0, self.nz - 2)
        def _(e):
            to = ring(SEND, e, self.z, self.nz)
            for x in self.xs:
                self.out_copy(x, to).start()

        for x in self.xs[1:]:
            self.out_copy(x, self.z).start()

    def arrived(self, m, parts):
        part = self.pin.at[m, pl.ds(0, parts)]
        self.remote(part, part, 2, self.ro.at[m], self.partner()).wait_recv()

    def finish(self, m):
        here = (m == self.z) & self.scans
        if self.parts > 1:

            @pl.when(here)
            def _():
                self.arrived(m, self.parts - 1)

        @pl.when(jnp.logical_not(here))
        def _():
            self.arrived(m, self.parts)

        @pl.when(m == self.passed)
        def _():
            before = self.pin[m]
            self.on[...] = jnp.where(self.first, before + self.s[m], before)
            self.on_copy().start()
            self.pin[m] = jnp.where(self.first, before, before + self.given[...])

        before = self.pin[m].reshape(DIM, DIM)
        self.bkout[m] = jnp.where(self.pc == 0, before + self.own[self.c * HALF + m], before)
        self.bk_copy(m).start()
        return jnp.where(self.pc == 1, before + self.exch[m], before)

    def finished(self, m):
        self.bk_copy(m).wait_recv()
        return self.bkin[m]

    def drain(self):
        sent = self.parts * (HALF - 1)
        some = pl.ds(0, self.nx * (self.nz - 1) - 1)
        self.remote(self.exch, self.exch, 0, self.re.at[0], self.partner()).wait_send()

        @pl.when(self.scans)
        def _():
            own = self.gin.at[pl.ds(0, sent - 1)]
            self.remote(own, own, 1, self.ri, self.partner()).wait_send()
            self.remote(self.pout.at[some], self.pout.at[some], 2, self.ro.at[0], self.partner()).wait_send()

        @pl.when(jnp.logical_not(self.scans))
        def _():
            all_parts = self.gin.at[pl.ds(0, sent)]
            self.remote(all_parts, all_parts, 1, self.ri, self.partner()).wait_send()

        self.remote(self.bkout, self.bkin, 3, self.rb.at[0], self.partner()).wait_send()
        self.give_copy().wait_send()
        self.on_copy().wait_send()


def kernel(
    sizes,
    q_hbm,
    k_hbm,
    v_hbm,
    g_hbm,
    gain_ref,
    dq_hbm,
    dk_hbm,
    dv_hbm,
    dgain_ref,
    *scratch,
):
    ny, nx, nz = sizes
    scratch = list(scratch)

    def take(n):
        out = scratch[:n]
        del scratch[:n]
        return out

    q, k, v, g = take(4)
    dq, dk, dv = take(3)
    scores, d_out, prior = take(3)
    out_loc, dk_loc, dv_loc = take(3)
    gtile, gin1, acc1, gin2, acc2, gin3, acc3, gin4 = take(8)
    bufs1, sems1 = take(11), take(6)
    bufs2, sems2 = take(11), take(6)
    in_sem, out_sem, gsend, g1r, g2r, g3r, g4r = take(7)

    y = lax.axis_index("dp")
    ctx = lax.axis_index("ctx")
    x = ctx // (2 * nz)
    z = (ctx // 2) % nz
    c = ctx % 2
    pos = (y, x, z, c)

    def device(y_, x_, z_, c_):
        return (y_, (x_ * nz + z_) * 2 + c_)

    loads = [pltpu.make_async_copy(src.at[0], dst, in_sem.at[i]) for i, (src, dst) in enumerate(((k_hbm, k), (v_hbm, v), (q_hbm, q), (g_hbm, g)))]
    for load in loads:
        load.start()

    def y_peer(i):
        return device((y + i) % ny, x, z, c)

    def x_peer(i):
        return device(y, (x + i) % nx, z, c)

    def z_peer(i):
        return device(y, x, (z + i) % nz, c)

    partner = device(y, x, z, 1 - c)
    barrier = pltpu.get_barrier_semaphore()
    pl.semaphore_signal(barrier, inc=1, device_id=partner, device_id_type=MESH)
    for i in range(1, ny):
        pl.semaphore_signal(barrier, inc=1, device_id=y_peer(i), device_id_type=MESH)

    @pl.loop(1, nx * nz)
    def _(i):
        to = (x * nz + z + i) % (nx * nz)
        pl.semaphore_signal(barrier, inc=1, device_id=(y, to * 2 + c), device_id_type=MESH)

    one = Scan((nx, nz), pos, 1, bufs1, sems1)
    two = Scan((nx, nz), pos, -1, bufs2, sems2)
    one.clear()
    two.clear()

    def col(h):
        return pl.ds(pl.multiple_of(h * DIM, DIM), DIM)

    mine, other = c * HALF, (1 - c) * HALF

    def columns(ref, heads):
        return [ref[:, col(h)] for h in heads]

    def local_states(heads):
        ks, vs = columns(k, heads), columns(v, heads)
        states = [dot(kh, vh, 0, 0) for kh, vh in zip(ks, vs)]
        for h, state in zip(heads, states):
            one.own[h] = state

    loads[0].wait()
    loads[1].wait()

    def place(e):
        return ring(MAKE, jnp.int32(e), z, nz)

    for i in range(0, HALF, 4):
        local_states([other + place(i + u) for u in range(4)])
        if i == 0:
            pl.semaphore_wait(barrier, nx * nz + ny - 1)
        for u in range(4):
            one.exch_copy(place(i + u)).start()

    for i in range(0, HALF, 4):
        local_states([mine + place(i + u) for u in range(4)])
        for u in range(4):
            one.add_chip(place(i + u))
    one.pass_in()

    loads[2].wait()
    loads[3].wait()

    keep = lax.broadcasted_iota(jnp.int32, (DIM, DIM), 0) >= lax.broadcasted_iota(jnp.int32, (DIM, DIM), 1)

    def before_one(heads):
        qs, ks, vs = columns(q, heads), columns(k, heads), columns(v, heads)
        raw = [dot(qh, kh, 1, 1) for qh, kh in zip(qs, ks)]
        lows = [jnp.where(keep, r, 0.0).astype(BF16) for r in raw]
        outs = [dot(low, vh, 1, 0) for low, vh in zip(lows, vs)]
        for h, low, out in zip(heads, lows, outs):
            scores[h] = low
            out_loc[h] = out

    def pass_one(heads, states):
        qs = columns(q, heads)
        gfs = [gh.astype(F32) for gh in columns(g, heads)]
        gains = columns(gain_ref, heads)
        locs = [out_loc[h] for h in heads]
        lows = [state.astype(BF16) for state in states]
        outs = [loc + dot(qh, low, 1, 0) for loc, qh, low in zip(locs, qs, lows)]
        invs = [lax.rsqrt(jnp.mean(out * out, axis=1, keepdims=True) + EPSILON) for out in outs]
        normeds = [out * inv for out, inv in zip(outs, invs)]
        gns = [gf * gain for gf, gain in zip(gfs, gains)]
        means = [jnp.mean(gn * normed, axis=1, keepdims=True) for gn, normed in zip(gns, normeds)]
        ds = [((gn - normed * mean) * inv).astype(BF16) for gn, normed, mean, inv in zip(gns, normeds, means, invs)]
        grads = [dot(qh, d, 0, 0) for qh, d in zip(qs, ds)]
        terms = [jnp.sum((gf * normed).reshape(DIM // 8, 8, DIM), axis=0) for gf, normed in zip(gfs, normeds)]
        for h, low, d, grad, term in zip(heads, lows, ds, grads, terms):
            prior[h] = low
            d_out[h] = d
            two.own[h] = grad
            gtile[h] = term

    def between(heads):
        ds, lows, scs = [d_out[h] for h in heads], [prior[h] for h in heads], [scores[h] for h in heads]
        qs, ks, vs = columns(q, heads), columns(k, heads), columns(v, heads)
        raw = [dot(d, vh, 1, 1) for d, vh in zip(ds, vs)]
        dvs = [dot(sc, d, 0, 0) for sc, d in zip(scs, ds)]
        pqs = [dot(d, low, 1, 1) for d, low in zip(ds, lows)]
        gss = [jnp.where(keep, r, 0.0).astype(BF16) for r in raw]
        dqs = [(dot(gs, kh, 1, 0) + pq).astype(BF16) for gs, kh, pq in zip(gss, ks, pqs)]
        dks = [dot(gs, qh, 0, 0) for gs, qh in zip(gss, qs)]
        for h, dqh, dkh, dvh in zip(heads, dqs, dks, dvs):
            dq[:, col(h)] = dqh
            dk_loc[h] = dkh
            dv_loc[h] = dvh

    def store(ref, hbm, i, h):
        return pltpu.make_async_copy(ref.at[:, col(h)], hbm.at[0, :, col(h)], out_sem.at[i])

    def pass_two(heads, states):
        ks, vs = columns(k, heads), columns(v, heads)
        dks, dvs = [dk_loc[h] for h in heads], [dv_loc[h] for h in heads]
        lows = [state.astype(BF16) for state in states]
        dks = [(part + dot(vh, low, 1, 1)).astype(BF16) for part, vh, low in zip(dks, vs, lows)]
        dvs = [(part + dot(kh, low, 1, 0)).astype(BF16) for part, kh, low in zip(dvs, ks, lows)]
        for h, dkh, dvh in zip(heads, dks, dvs):
            dk[:, col(h)] = dkh
            dv[:, col(h)] = dvh
        for h in heads:
            store(dk, dk_hbm, 1, h).start()
            store(dv, dv_hbm, 2, h).start()

    ry, rx = HEADS // ny, HEADS // ny // nx

    def g1_copy(i):
        src = gtile.at[pl.ds(((y + i) % ny) * ry, ry)]
        return pltpu.make_async_remote_copy(
            src_ref=src, dst_ref=gin1.at[i - 1], send_sem=gsend.at[0], recv_sem=g1r.at[i - 1], device_id=y_peer(i), device_id_type=MESH
        )

    def g2_copy(i):
        src = acc1.at[pl.ds(((x + i) % nx) * rx, rx)]
        return pltpu.make_async_remote_copy(
            src_ref=src, dst_ref=gin2.at[i - 1], send_sem=gsend.at[1], recv_sem=g2r.at[i - 1], device_id=x_peer(i), device_id_type=MESH
        )

    def g3_copy(i):
        return pltpu.make_async_remote_copy(
            src_ref=acc2, dst_ref=gin3.at[i - 1], send_sem=gsend.at[2], recv_sem=g3r.at[i - 1], device_id=z_peer(i), device_id_type=MESH
        )

    def g4_copy():
        return pltpu.make_async_remote_copy(
            src_ref=acc3, dst_ref=gin4, send_sem=gsend.at[3], recv_sem=g4r, device_id=partner, device_id_type=MESH
        )

    def gain_step(stage):
        if stage == 0:
            for i in range(1, ny):
                g1_copy(i).start()
        elif stage == 1:
            total = gtile[pl.ds(y * ry, ry)]
            for i in range(1, ny):
                g1_copy(i).wait_recv()
                total = total + gin1[i - 1]
            acc1[...] = total
            for i in range(1, nx):
                g2_copy(i).start()
        elif stage == 2:
            total = acc1[pl.ds(x * rx, rx)]
            for i in range(1, nx):
                g2_copy(i).wait_recv()
                total = total + gin2[i - 1]
            acc2[...] = total
            for i in range(1, nz):
                g3_copy(i).start()
        elif stage == 3:
            total = acc2[...]
            for i in range(1, nz):
                g3_copy(i).wait_recv()
                total = total + gin3[i - 1]
            acc3[...] = total
            g4_copy().start()
        else:
            g4_copy().wait_recv()
            scale = 1.0 / math.sqrt(ny * nx * nz * 2 * DIM)
            total = jnp.sum(acc3[...] + gin4[...], axis=1, keepdims=True) * scale
            dgain_ref[...] = jnp.broadcast_to(total, dgain_ref.shape)

    def arrival(e):
        return ring(WORK, e, z, nz)

    def finishing(scan, work, after, last, final):
        @pl.loop(0, HALF + LAG + SUM_LAG)
        def _(e):
            @pl.when(e >= LAG + SUM_LAG)
            def _():
                last(arrival(e - LAG - SUM_LAG))

            @pl.when(e == HALF + LAG)
            def _():
                final()

            @pl.when(e < LAG)
            def _():
                m = arrival(e)
                work([mine + m], [scan.finish(m)])

            @pl.when((e >= LAG) & (e < HALF))
            def _():
                m, n = arrival(e), arrival(e - LAG)
                state = scan.finish(m)
                work([mine + m, other + n], [state, scan.finished(n)])
                after(n)

            @pl.when((e >= HALF) & (e < HALF + LAG))
            def _():
                n = arrival(e - LAG)
                work([other + n], [scan.finished(n)])
                after(n)

    def nothing(*_):
        pass

    @pl.loop(0, HALF)
    def _(m):
        before_one([mine + m, other + m])

    one.scan()
    finishing(one, pass_one, lambda m: two.exch_copy(m).start(), two.add_chip, two.pass_in)
    gain_step(0)

    @pl.loop(0, HALF)
    def _(m):
        between([mine + m, other + m])

        @pl.when(m == HALF // 2)
        def _():
            gain_step(1)

    pltpu.make_async_copy(dq, dq_hbm.at[0], out_sem.at[0]).start()
    gain_step(2)
    two.scan()
    gain_step(3)
    finishing(two, pass_two, nothing, nothing, nothing)
    gain_step(4)

    one.drain()
    two.drain()
    for i in range(1, ny):
        g1_copy(i).wait_send()
    for i in range(1, nx):
        g2_copy(i).wait_send()
    for i in range(1, nz):
        g3_copy(i).wait_send()
    g4_copy().wait_send()
    for i, (ref, hbm) in enumerate(((dq, dq_hbm), (dk, dk_hbm), (dv, dv_hbm))):
        pltpu.make_async_copy(ref, hbm.at[0], out_sem.at[i]).wait()


def hand_over(nz, a, b, c, gain, a_out, b_out, c_out, gain_out, gain_buf, sems):
    stores = []
    for row in range(0, DIM, BLOCK):
        for src, dst in ((a, a_out), (b, b_out), (c, c_out)):
            part = pl.ds(row, BLOCK)
            stores.append(pltpu.make_async_copy(src.at[0, part], dst.at[0, part], sems.at[len(stores)]))
    load_gain = pltpu.make_async_copy(gain, gain_buf, sems.at[len(stores)])
    load_gain.start()
    for store in stores:
        store.start()
    load_gain.wait()
    share = gain_out.shape[1]
    place = lax.rem(lax.axis_index("ctx"), 2 * nz) * share
    turned = pltpu.roll(gain_buf[place // DIM], (DIM - place % DIM) % DIM, 1)
    gain_out[...] = turned[0:1, :share]
    for store in stores:
        store.wait()


def build(mesh, nx, nz):
    ny = mesh.shape["dp"]
    width = HEADS * DIM
    ry, rx = HEADS // ny, HEADS // ny // nx

    def scan_scratch():
        state = pltpu.VMEM((HALF, DIM, DIM), F32)
        count = nx // 2
        parts = pltpu.VMEM((HALF, count, DIM // count, DIM), F32)
        slots = pltpu.VMEM((nx * nz, DIM // count, DIM), F32)
        return [
            pltpu.VMEM((HEADS, DIM, DIM), F32),
            state,
            parts,
            slots,
            slots,
            parts,
            state,
            state,
            *[pltpu.VMEM((count, DIM // count, DIM), F32)] * 3,
            pltpu.SemaphoreType.DMA((HALF,)),
            pltpu.SemaphoreType.DMA,
            *[pltpu.SemaphoreType.DMA((HALF,))] * 2,
            pltpu.SemaphoreType.DMA,
            pltpu.SemaphoreType.DMA((6,)),
        ]

    scratch = [
        *[pltpu.VMEM((DIM, width), BF16)] * 7,
        *[pltpu.VMEM((HEADS, DIM, DIM), BF16)] * 3,
        *[pltpu.VMEM((HEADS, DIM, DIM), F32)] * 3,
        pltpu.VMEM((HEADS, 8, DIM), F32),
        pltpu.VMEM((ny - 1, ry, 8, DIM), F32),
        pltpu.VMEM((ry, 8, DIM), F32),
        pltpu.VMEM((nx - 1, rx, 8, DIM), F32),
        pltpu.VMEM((rx, 8, DIM), F32),
        pltpu.VMEM((nz - 1, rx, 8, DIM), F32),
        pltpu.VMEM((rx, 8, DIM), F32),
        pltpu.VMEM((rx, 8, DIM), F32),
        *scan_scratch(),
        *scan_scratch(),
        pltpu.SemaphoreType.DMA((4,)),
        pltpu.SemaphoreType.DMA((3,)),
        pltpu.SemaphoreType.DMA((4,)),
        pltpu.SemaphoreType.DMA((ny - 1,)),
        pltpu.SemaphoreType.DMA((nx - 1,)),
        pltpu.SemaphoreType.DMA((nz - 1,)),
        pltpu.SemaphoreType.DMA,
    ]

    def body(queries, key_rows, value_rows, out_grad, norm_gain):
        rows = jax.ShapeDtypeStruct(queries.shape, BF16)
        dq, dk, dv, dgain = pl.pallas_call(
            functools.partial(kernel, (ny, nx, nz)),
            out_shape=(*[pltpu.VMEM(queries.shape, BF16)] * 3, pltpu.VMEM((rx, 8, DIM), F32)),
            in_specs=[pl.BlockSpec(memory_space=pl.ANY)] * 4 + [pl.BlockSpec(memory_space=pltpu.VMEM)],
            out_specs=[pl.BlockSpec(memory_space=pl.ANY)] * 3 + [pl.BlockSpec(memory_space=pltpu.VMEM)],
            scratch_shapes=scratch,
            compiler_params=pltpu.CompilerParams(
                collective_id=0, has_side_effects=True, vmem_limit_bytes=62 * 1024 * 1024
            ),
        )(queries, key_rows, value_rows, out_grad, norm_gain.reshape(1, width))
        share = rx * DIM // (2 * nz)
        dq, dk, dv, dgain = pl.pallas_call(
            functools.partial(hand_over, nz),
            out_shape=(rows, rows, rows, jax.ShapeDtypeStruct((1, share), F32)),
            in_specs=[pl.BlockSpec(memory_space=pl.ANY)] * 4,
            out_specs=[pl.BlockSpec(memory_space=pl.ANY)] * 3 + [pl.BlockSpec(memory_space=pltpu.VMEM)],
            scratch_shapes=[pltpu.VMEM((rx, 8, DIM), F32), pltpu.SemaphoreType.DMA((3 * (DIM // BLOCK) + 1,))],
            compiler_params=pltpu.CompilerParams(vmem_limit_bytes=8 * 1024 * 1024),
        )(dq, dk, dv, dgain)
        return dq, dk, dv, dgain.reshape(share)

    placed = P("dp", "ctx", None)
    return jax.shard_map(
        body,
        mesh=mesh,
        in_specs=(placed, placed, placed, placed, P()),
        out_specs=(placed, placed, placed, P(("dp", "ctx"))),
        check_vma=False,
    )


def solution(mesh):
    return build(mesh, 4, 8)
```

```python
import functools
import math

import jax
import jax.numpy as jnp
from jax import lax
from jax.experimental import pallas as pl
from jax.experimental.pallas import tpu as pltpu
from jax.sharding import PartitionSpec as P

HEADS = 16
HALF = 8
DIM = 128
EPSILON = 1e-05
MESH = pl.DeviceIdType.MESH
F32 = jnp.float32
BF16 = jnp.bfloat16

LAG = 2
SUM_LAG = 2
BLOCK = 32


def dot(a, b, ca, cb):
    return lax.dot_general(a, b, (((ca,), (cb,)), ((), ())), preferred_element_type=F32)


def listed(places, e):
    packed = sum(place << (3 * i) for i, place in enumerate(places))
    return lax.shift_right_logical(jnp.int32(packed), jnp.int32(3) * e) % 8


MAKE = (4, 5, 3, 6, 2, 7, 1, 0)
SEND = (5, 3, 6, 2, 7, 1)
WORK = (5, 0, 3, 4, 6, 2, 7, 1)


def ring(places, e, z, nz):
    away = listed(places, e)
    return (z + away + (z % 2) * (nz - 2 * away)) % nz


class Scan:
    def __init__(self, sizes, pos, order, bufs, sems):
        self.nx, self.nz = sizes
        self.y, self.x, self.z, self.c = pos
        self.order = order
        self.pc = self.c if order > 0 else 1 - self.c
        self.slot = self.x * self.nz + self.z
        self.xs = [(self.x + i) % self.nx for i in range(self.nx)]
        self.base = [x * 2 * self.nz + self.c for x in self.xs]
        self.mate = self.z + 1 - 2 * (self.z % 2)
        self.first = self.z % 2 == (0 if order > 0 else 1)
        self.far = (self.z + self.nz // 2) % self.nz
        self.passed = (self.mate + self.nz // 2) % self.nz
        (self.own, self.exch, self.s, self.gin, self.pout, self.pin, self.bkin, self.bkout, self.given, self.both, self.on) = bufs
        self.re, self.ri, self.ro, self.rb, self.rg, self.sends = sems

    def device(self, x, z, c):
        return (self.y, (x * self.nz + z) * 2 + c)

    def partner(self):
        return self.device(self.x, self.z, 1 - self.c)

    def remote(self, src, dst, which, recv, to):
        return pltpu.make_async_remote_copy(
            src_ref=src, dst_ref=dst, send_sem=self.sends.at[which], recv_sem=recv, device_id=to, device_id_type=MESH
        )

    def exch_copy(self, m):
        return self.remote(self.own.at[(1 - self.c) * HALF + m], self.exch.at[m], 0, self.re.at[m], self.partner())

    def clear(self):
        for x in range(self.nx):
            self.gin[x * self.nz + self.far] = jnp.zeros((DIM // self.nx, DIM), F32)

    def give_copy(self):
        to = self.device(self.x, self.mate, self.c)
        return self.remote(self.s.at[self.far], self.given, 4, self.rg, to)

    def on_copy(self):
        to = self.device(self.x, self.mate, self.c)
        return self.remote(self.on, self.pin.at[self.passed], 5, self.ro.at[self.passed], to)

    def in_copy(self, src, m, i):
        return self.remote(src.at[self.xs[i]], self.gin.at[self.slot], 1, self.ri, (self.y, self.base[i] + 2 * m))

    def out_copy(self, i, z):
        to = (self.y, self.base[i] + 2 * z)
        return self.remote(self.pout.at[self.xs[i] * self.nz + z], self.pin.at[self.z, self.x], 2, self.ro.at[self.z], to)

    def bk_copy(self, m):
        return self.remote(self.bkout.at[m], self.bkin.at[m], 3, self.rb.at[m], self.partner())

    def add_chip(self, m):
        self.exch_copy(m).wait_recv()
        parts = (self.nx, DIM // self.nx, DIM)
        self.s[m] = (self.own[self.c * HALF + m] + self.exch[m]).reshape(parts)

        @pl.when(m == self.far)
        def _():
            self.give_copy().start()

        @pl.when((m != self.far) & (m != self.passed))
        def _():
            for i in range(1, self.nx):
                self.in_copy(self.s.at[m], m, i).start()

            @pl.when(m == self.z)
            def _():
                self.gin[self.slot] = self.s[m, self.x]

            @pl.when(m != self.z)
            def _():
                self.in_copy(self.s.at[m], m, 0).start()

    def pass_in(self):
        self.give_copy().wait_recv()
        self.both[...] = self.s[self.passed] + self.given[...]
        for i in range(self.nx):
            self.in_copy(self.both, self.passed, i).start()

    def scan(self):
        slots = self.nx * self.nz
        some = pl.ds(0, slots - self.nx - 1)
        self.remote(self.gin.at[some], self.gin.at[some], 1, self.ri, self.partner()).wait_recv()
        total = jnp.zeros((DIM // self.nx, DIM), F32)
        for i in range(slots):
            slot = i if self.order > 0 else slots - 1 - i
            self.pout[slot] = total
            total = total + self.gin[slot]
        self.pin[self.z, self.x] = self.pout[self.slot]

        @pl.loop(0, self.nz - 2)
        def _(e):
            to = ring(SEND, e, self.z, self.nz)
            for i in range(self.nx):
                self.out_copy(i, to).start()

        for i in range(1, self.nx):
            self.out_copy(i, self.z).start()

    def arrived(self, m, parts):
        part = self.pin.at[m, pl.ds(0, parts)]
        self.remote(part, part, 2, self.ro.at[m], self.partner()).wait_recv()

    def finish(self, m):
        @pl.when(m == self.z)
        def _():
            self.arrived(m, self.nx - 1)

        @pl.when(m != self.z)
        def _():
            self.arrived(m, self.nx)

        @pl.when(m == self.passed)
        def _():
            before = self.pin[m]
            self.on[...] = jnp.where(self.first, before + self.s[m], before)
            self.on_copy().start()
            self.pin[m] = jnp.where(self.first, before, before + self.given[...])

        before = self.pin[m].reshape(DIM, DIM)
        self.bkout[m] = jnp.where(self.pc == 0, before + self.own[self.c * HALF + m], before)
        self.bk_copy(m).start()
        return jnp.where(self.pc == 1, before + self.exch[m], before)

    def finished(self, m):
        self.bk_copy(m).wait_recv()
        return self.bkin[m]

    def drain(self):
        some = pl.ds(0, self.nx * (self.nz - 1) - 1)
        self.remote(self.exch, self.exch, 0, self.re.at[0], self.partner()).wait_send()
        self.remote(self.gin.at[some], self.gin.at[some], 1, self.ri, self.partner()).wait_send()
        self.remote(self.pout.at[some], self.pout.at[some], 2, self.ro.at[0], self.partner()).wait_send()
        self.remote(self.bkout, self.bkin, 3, self.rb.at[0], self.partner()).wait_send()
        self.give_copy().wait_send()
        self.on_copy().wait_send()


def kernel(
    sizes,
    q_hbm,
    k_hbm,
    v_hbm,
    g_hbm,
    gain_ref,
    dq_ref,
    dk_ref,
    dv_ref,
    dgain_ref,
    *scratch,
):
    ny, nx, nz = sizes
    scratch = list(scratch)

    def take(n):
        out = scratch[:n]
        del scratch[:n]
        return out

    q, k, v, g = take(4)
    dq, dk, dv = dq_ref.at[0], dk_ref.at[0], dv_ref.at[0]
    scores, d_out, prior = take(3)
    out_loc, dk_loc, dv_loc = take(3)
    gtile, gin1, acc1, gin2, acc2, gin3, acc3, gin4 = take(8)
    bufs1, sems1 = take(11), take(6)
    bufs2, sems2 = take(11), take(6)
    in_sem, gsend, g1r, g2r, g3r, g4r = take(6)

    y = lax.axis_index("dp")
    ctx = lax.axis_index("ctx")
    x = ctx // (2 * nz)
    z = (ctx // 2) % nz
    c = ctx % 2
    pos = (y, x, z, c)

    def device(y_, x_, z_, c_):
        return (y_, (x_ * nz + z_) * 2 + c_)

    loads = [pltpu.make_async_copy(src.at[0], dst, in_sem.at[i]) for i, (src, dst) in enumerate(((k_hbm, k), (v_hbm, v), (q_hbm, q), (g_hbm, g)))]
    for load in loads:
        load.start()

    def y_peer(i):
        return device((y + i) % ny, x, z, c)

    def x_peer(i):
        return device(y, (x + i) % nx, z, c)

    def z_peer(i):
        return device(y, x, (z + i) % nz, c)

    partner = device(y, x, z, 1 - c)
    barrier = pltpu.get_barrier_semaphore()
    pl.semaphore_signal(barrier, inc=1, device_id=partner, device_id_type=MESH)
    for i in range(1, ny):
        pl.semaphore_signal(barrier, inc=1, device_id=y_peer(i), device_id_type=MESH)

    @pl.loop(1, nx * nz)
    def _(i):
        to = (x * nz + z + i) % (nx * nz)
        pl.semaphore_signal(barrier, inc=1, device_id=(y, to * 2 + c), device_id_type=MESH)

    one = Scan((nx, nz), pos, 1, bufs1, sems1)
    two = Scan((nx, nz), pos, -1, bufs2, sems2)
    one.clear()
    two.clear()

    def col(h):
        return pl.ds(pl.multiple_of(h * DIM, DIM), DIM)

    mine, other = c * HALF, (1 - c) * HALF

    def columns(ref, heads):
        return [ref[:, col(h)] for h in heads]

    def local_states(heads):
        ks, vs = columns(k, heads), columns(v, heads)
        states = [dot(kh, vh, 0, 0) for kh, vh in zip(ks, vs)]
        for h, state in zip(heads, states):
            one.own[h] = state

    loads[0].wait()
    loads[1].wait()

    def place(e):
        return ring(MAKE, jnp.int32(e), z, nz)

    for i in range(0, HALF, 4):
        local_states([other + place(i + u) for u in range(4)])
        if i == 0:
            pl.semaphore_wait(barrier, nx * nz + ny - 1)
        for u in range(4):
            one.exch_copy(place(i + u)).start()

    for i in range(0, HALF, 4):
        local_states([mine + place(i + u) for u in range(4)])
        for u in range(4):
            one.add_chip(place(i + u))
    one.pass_in()

    loads[2].wait()
    loads[3].wait()

    keep = lax.broadcasted_iota(jnp.int32, (DIM, DIM), 0) >= lax.broadcasted_iota(jnp.int32, (DIM, DIM), 1)

    def before_one(heads):
        qs, ks, vs = columns(q, heads), columns(k, heads), columns(v, heads)
        raw = [dot(qh, kh, 1, 1) for qh, kh in zip(qs, ks)]
        lows = [jnp.where(keep, r, 0.0).astype(BF16) for r in raw]
        outs = [dot(low, vh, 1, 0) for low, vh in zip(lows, vs)]
        for h, low, out in zip(heads, lows, outs):
            scores[h] = low
            out_loc[h] = out

    def pass_one(heads, states):
        qs = columns(q, heads)
        gfs = [gh.astype(F32) for gh in columns(g, heads)]
        gains = columns(gain_ref, heads)
        locs = [out_loc[h] for h in heads]
        lows = [state.astype(BF16) for state in states]
        outs = [loc + dot(qh, low, 1, 0) for loc, qh, low in zip(locs, qs, lows)]
        invs = [lax.rsqrt(jnp.mean(out * out, axis=1, keepdims=True) + EPSILON) for out in outs]
        normeds = [out * inv for out, inv in zip(outs, invs)]
        gns = [gf * gain for gf, gain in zip(gfs, gains)]
        means = [jnp.mean(gn * normed, axis=1, keepdims=True) for gn, normed in zip(gns, normeds)]
        ds = [((gn - normed * mean) * inv).astype(BF16) for gn, normed, mean, inv in zip(gns, normeds, means, invs)]
        grads = [dot(qh, d, 0, 0) for qh, d in zip(qs, ds)]
        terms = [jnp.sum((gf * normed).reshape(DIM // 8, 8, DIM), axis=0) for gf, normed in zip(gfs, normeds)]
        for h, low, d, grad, term in zip(heads, lows, ds, grads, terms):
            prior[h] = low
            d_out[h] = d
            two.own[h] = grad
            gtile[h] = term

    def between(heads):
        ds, lows, scs = [d_out[h] for h in heads], [prior[h] for h in heads], [scores[h] for h in heads]
        qs, ks, vs = columns(q, heads), columns(k, heads), columns(v, heads)
        raw = [dot(d, vh, 1, 1) for d, vh in zip(ds, vs)]
        dvs = [dot(sc, d, 0, 0) for sc, d in zip(scs, ds)]
        pqs = [dot(d, low, 1, 1) for d, low in zip(ds, lows)]
        gss = [jnp.where(keep, r, 0.0).astype(BF16) for r in raw]
        dqs = [(dot(gs, kh, 1, 0) + pq).astype(BF16) for gs, kh, pq in zip(gss, ks, pqs)]
        dks = [dot(gs, qh, 0, 0) for gs, qh in zip(gss, qs)]
        for h, dqh, dkh, dvh in zip(heads, dqs, dks, dvs):
            dq[:, col(h)] = dqh
            dk_loc[h] = dkh
            dv_loc[h] = dvh

    def pass_two(heads, states):
        ks, vs = columns(k, heads), columns(v, heads)
        dks, dvs = [dk_loc[h] for h in heads], [dv_loc[h] for h in heads]
        lows = [state.astype(BF16) for state in states]
        dks = [(part + dot(vh, low, 1, 1)).astype(BF16) for part, vh, low in zip(dks, vs, lows)]
        dvs = [(part + dot(kh, low, 1, 0)).astype(BF16) for part, kh, low in zip(dvs, ks, lows)]
        for h, dkh, dvh in zip(heads, dks, dvs):
            dk[:, col(h)] = dkh
            dv[:, col(h)] = dvh

    ry, rx = HEADS // ny, HEADS // ny // nx

    def g1_copy(i):
        src = gtile.at[pl.ds(((y + i) % ny) * ry, ry)]
        return pltpu.make_async_remote_copy(
            src_ref=src, dst_ref=gin1.at[i - 1], send_sem=gsend.at[0], recv_sem=g1r.at[i - 1], device_id=y_peer(i), device_id_type=MESH
        )

    def g2_copy(i):
        src = acc1.at[pl.ds(((x + i) % nx) * rx, rx)]
        return pltpu.make_async_remote_copy(
            src_ref=src, dst_ref=gin2.at[i - 1], send_sem=gsend.at[1], recv_sem=g2r.at[i - 1], device_id=x_peer(i), device_id_type=MESH
        )

    def g3_copy(i):
        return pltpu.make_async_remote_copy(
            src_ref=acc2, dst_ref=gin3.at[i - 1], send_sem=gsend.at[2], recv_sem=g3r.at[i - 1], device_id=z_peer(i), device_id_type=MESH
        )

    def g4_copy():
        return pltpu.make_async_remote_copy(
            src_ref=acc3, dst_ref=gin4, send_sem=gsend.at[3], recv_sem=g4r, device_id=partner, device_id_type=MESH
        )

    def gain_step(stage):
        if stage == 0:
            for i in range(1, ny):
                g1_copy(i).start()
        elif stage == 1:
            total = gtile[pl.ds(y * ry, ry)]
            for i in range(1, ny):
                g1_copy(i).wait_recv()
                total = total + gin1[i - 1]
            acc1[...] = total
            for i in range(1, nx):
                g2_copy(i).start()
        elif stage == 2:
            total = acc1[pl.ds(x * rx, rx)]
            for i in range(1, nx):
                g2_copy(i).wait_recv()
                total = total + gin2[i - 1]
            acc2[...] = total
            for i in range(1, nz):
                g3_copy(i).start()
        elif stage == 3:
            total = acc2[...]
            for i in range(1, nz):
                g3_copy(i).wait_recv()
                total = total + gin3[i - 1]
            acc3[...] = total
            g4_copy().start()
        else:
            g4_copy().wait_recv()
            scale = 1.0 / math.sqrt(ny * nx * nz * 2 * DIM)
            total = jnp.sum(acc3[...] + gin4[...], axis=1, keepdims=True) * scale
            dgain_ref[...] = jnp.broadcast_to(total, dgain_ref.shape)

    def arrival(e):
        return ring(WORK, e, z, nz)

    def finishing(scan, work, after, last, final):
        @pl.loop(0, HALF + LAG + SUM_LAG)
        def _(e):
            @pl.when(e >= LAG + SUM_LAG)
            def _():
                last(arrival(e - LAG - SUM_LAG))

            @pl.when(e == HALF + LAG)
            def _():
                final()

            @pl.when(e < LAG)
            def _():
                m = arrival(e)
                work([mine + m], [scan.finish(m)])

            @pl.when((e >= LAG) & (e < HALF))
            def _():
                m, n = arrival(e), arrival(e - LAG)
                state = scan.finish(m)
                work([mine + m, other + n], [state, scan.finished(n)])
                after(n)

            @pl.when((e >= HALF) & (e < HALF + LAG))
            def _():
                n = arrival(e - LAG)
                work([other + n], [scan.finished(n)])
                after(n)

    def nothing(*_):
        pass

    @pl.loop(0, HALF)
    def _(m):
        before_one([mine + m, other + m])

    one.scan()
    finishing(one, pass_one, lambda m: two.exch_copy(m).start(), two.add_chip, two.pass_in)
    gain_step(0)

    @pl.loop(0, HALF)
    def _(m):
        between([mine + m, other + m])

        @pl.when(m == HALF // 2)
        def _():
            gain_step(1)

    gain_step(2)
    two.scan()
    gain_step(3)
    finishing(two, pass_two, nothing, nothing, nothing)
    gain_step(4)

    one.drain()
    two.drain()
    for i in range(1, ny):
        g1_copy(i).wait_send()
    for i in range(1, nx):
        g2_copy(i).wait_send()
    for i in range(1, nz):
        g3_copy(i).wait_send()
    g4_copy().wait_send()


def hand_over(nz, a, b, c, gain, a_out, b_out, c_out, gain_out, gain_buf, sems):
    stores = []
    for row in range(0, DIM, BLOCK):
        for src, dst in ((a, a_out), (b, b_out), (c, c_out)):
            part = pl.ds(row, BLOCK)
            stores.append(pltpu.make_async_copy(src.at[0, part], dst.at[0, part], sems.at[len(stores)]))
    load_gain = pltpu.make_async_copy(gain, gain_buf, sems.at[len(stores)])
    load_gain.start()
    for store in stores:
        store.start()
    load_gain.wait()
    share = gain_out.shape[1]
    place = lax.rem(lax.axis_index("ctx"), 2 * nz) * share
    turned = pltpu.roll(gain_buf[place // DIM], (DIM - place % DIM) % DIM, 1)
    gain_out[...] = turned[0:1, :share]
    for store in stores:
        store.wait()


def build(mesh, nx, nz):
    ny = mesh.shape["dp"]
    width = HEADS * DIM
    ry, rx = HEADS // ny, HEADS // ny // nx

    def scan_scratch():
        state = pltpu.VMEM((HALF, DIM, DIM), F32)
        parts = pltpu.VMEM((HALF, nx, DIM // nx, DIM), F32)
        slots = pltpu.VMEM((nx * nz, DIM // nx, DIM), F32)
        return [
            pltpu.VMEM((HEADS, DIM, DIM), F32),
            state,
            parts,
            slots,
            slots,
            parts,
            state,
            state,
            *[pltpu.VMEM((nx, DIM // nx, DIM), F32)] * 3,
            pltpu.SemaphoreType.DMA((HALF,)),
            pltpu.SemaphoreType.DMA,
            *[pltpu.SemaphoreType.DMA((HALF,))] * 2,
            pltpu.SemaphoreType.DMA,
            pltpu.SemaphoreType.DMA((6,)),
        ]

    scratch = [
        *[pltpu.VMEM((DIM, width), BF16)] * 4,
        *[pltpu.VMEM((HEADS, DIM, DIM), BF16)] * 3,
        *[pltpu.VMEM((HEADS, DIM, DIM), F32)] * 3,
        pltpu.VMEM((HEADS, 8, DIM), F32),
        pltpu.VMEM((ny - 1, ry, 8, DIM), F32),
        pltpu.VMEM((ry, 8, DIM), F32),
        pltpu.VMEM((nx - 1, rx, 8, DIM), F32),
        pltpu.VMEM((rx, 8, DIM), F32),
        pltpu.VMEM((nz - 1, rx, 8, DIM), F32),
        pltpu.VMEM((rx, 8, DIM), F32),
        pltpu.VMEM((rx, 8, DIM), F32),
        *scan_scratch(),
        *scan_scratch(),
        pltpu.SemaphoreType.DMA((4,)),
        pltpu.SemaphoreType.DMA((4,)),
        pltpu.SemaphoreType.DMA((ny - 1,)),
        pltpu.SemaphoreType.DMA((nx - 1,)),
        pltpu.SemaphoreType.DMA((nz - 1,)),
        pltpu.SemaphoreType.DMA,
    ]

    def body(queries, key_rows, value_rows, out_grad, norm_gain):
        rows = jax.ShapeDtypeStruct(queries.shape, BF16)
        dq, dk, dv, dgain = pl.pallas_call(
            functools.partial(kernel, (ny, nx, nz)),
            out_shape=(*[pltpu.VMEM(queries.shape, BF16)] * 3, pltpu.VMEM((rx, 8, DIM), F32)),
            in_specs=[pl.BlockSpec(memory_space=pl.ANY)] * 4 + [pl.BlockSpec(memory_space=pltpu.VMEM)],
            out_specs=[pl.BlockSpec(memory_space=pltpu.VMEM)] * 4,
            scratch_shapes=scratch,
            compiler_params=pltpu.CompilerParams(
                collective_id=0, has_side_effects=True, vmem_limit_bytes=62 * 1024 * 1024
            ),
        )(queries, key_rows, value_rows, out_grad, norm_gain.reshape(1, width))
        share = rx * DIM // (2 * nz)
        dq, dk, dv, dgain = pl.pallas_call(
            functools.partial(hand_over, nz),
            out_shape=(rows, rows, rows, jax.ShapeDtypeStruct((1, share), F32)),
            in_specs=[pl.BlockSpec(memory_space=pl.ANY)] * 4,
            out_specs=[pl.BlockSpec(memory_space=pl.ANY)] * 3 + [pl.BlockSpec(memory_space=pltpu.VMEM)],
            scratch_shapes=[pltpu.VMEM((rx, 8, DIM), F32), pltpu.SemaphoreType.DMA((3 * (DIM // BLOCK) + 1,))],
            compiler_params=pltpu.CompilerParams(vmem_limit_bytes=8 * 1024 * 1024),
        )(dq, dk, dv, dgain)
        return dq, dk, dv, dgain.reshape(share)

    placed = P("dp", "ctx", None)
    return jax.shard_map(
        body,
        mesh=mesh,
        in_specs=(placed, placed, placed, placed, P()),
        out_specs=(placed, placed, placed, P(("dp", "ctx"))),
        check_vma=False,
    )


def solution(mesh):
    return build(mesh, 4, 8)
```

```python
import functools
import math

import jax
import jax.numpy as jnp
from jax import lax
from jax.experimental import pallas as pl
from jax.experimental.pallas import tpu as pltpu
from jax.sharding import PartitionSpec as P

HEADS = 16
HALF = 8
DIM = 128
EPSILON = 1e-05
MESH = pl.DeviceIdType.MESH
F32 = jnp.float32
BF16 = jnp.bfloat16

LAG = 2
SUM_LAG = 2
BLOCK = 32


def dot(a, b, ca, cb):
    return lax.dot_general(a, b, (((ca,), (cb,)), ((), ())), preferred_element_type=F32)


def listed(places, e):
    packed = sum(place << (3 * i) for i, place in enumerate(places))
    return lax.shift_right_logical(jnp.int32(packed), jnp.int32(3) * e) % 8


MAKE = (4, 5, 3, 6, 2, 7, 1, 0)
SEND = (5, 3, 6, 2, 7, 1)
WORK = (5, 0, 3, 4, 6, 2, 7, 1)


def ring(places, e, z, nz):
    away = listed(places, e)
    return (z + away + (z % 2) * (nz - 2 * away)) % nz


class Scan:
    def __init__(self, sizes, pos, order, bufs, sems):
        self.nx, self.nz = sizes
        self.y, self.x, self.z, self.c = pos
        self.order = order
        self.pc = self.c if order > 0 else 1 - self.c
        self.slot = self.x * self.nz + self.z
        self.xs = [(self.x + i) % self.nx for i in range(self.nx)]
        self.base = [x * 2 * self.nz + self.c for x in self.xs]
        self.mate = self.z + 1 - 2 * (self.z % 2)
        self.first = self.z % 2 == (0 if order > 0 else 1)
        self.far = (self.z + self.nz // 2) % self.nz
        self.passed = (self.mate + self.nz // 2) % self.nz
        (self.own, self.exch, self.s, self.gin, self.pout, self.pin, self.bkin, self.bkout, self.given, self.both, self.on) = bufs
        self.re, self.ri, self.ro, self.rb, self.rg, self.sends = sems

    def device(self, x, z, c):
        return (self.y, (x * self.nz + z) * 2 + c)

    def partner(self):
        return self.device(self.x, self.z, 1 - self.c)

    def remote(self, src, dst, which, recv, to):
        return pltpu.make_async_remote_copy(
            src_ref=src, dst_ref=dst, send_sem=self.sends.at[which], recv_sem=recv, device_id=to, device_id_type=MESH
        )

    def exch_copy(self, m):
        return self.remote(self.own.at[(1 - self.c) * HALF + m], self.exch.at[m], 0, self.re.at[m], self.partner())

    def clear(self):
        for x in range(self.nx):
            self.gin[x * self.nz + self.far] = jnp.zeros((DIM // self.nx, DIM), F32)

    def give_copy(self):
        to = self.device(self.x, self.mate, self.c)
        return self.remote(self.s.at[self.far], self.given, 4, self.rg, to)

    def on_copy(self):
        to = self.device(self.x, self.mate, self.c)
        return self.remote(self.on, self.pin.at[self.passed], 5, self.ro.at[self.passed], to)

    def in_copy(self, src, m, i):
        return self.remote(src.at[self.xs[i]], self.gin.at[self.slot], 1, self.ri, (self.y, self.base[i] + 2 * m))

    def out_copy(self, i, z):
        to = (self.y, self.base[i] + 2 * z)
        return self.remote(self.pout.at[self.xs[i] * self.nz + z], self.pin.at[self.z, self.x], 2, self.ro.at[self.z], to)

    def bk_copy(self, m):
        return self.remote(self.bkout.at[m], self.bkin.at[m], 3, self.rb.at[m], self.partner())

    def add_chip(self, m):
        self.exch_copy(m).wait_recv()
        parts = (self.nx, DIM // self.nx, DIM)
        self.s[m] = (self.own[self.c * HALF + m] + self.exch[m]).reshape(parts)

        @pl.when(m == self.far)
        def _():
            self.give_copy().start()

        @pl.when((m != self.far) & (m != self.passed))
        def _():
            for i in range(1, self.nx):
                self.in_copy(self.s.at[m], m, i).start()

            @pl.when(m == self.z)
            def _():
                self.gin[self.slot] = self.s[m, self.x]

            @pl.when(m != self.z)
            def _():
                self.in_copy(self.s.at[m], m, 0).start()

    def pass_in(self):
        self.give_copy().wait_recv()
        self.both[...] = self.s[self.passed] + self.given[...]
        for i in range(self.nx):
            self.in_copy(self.both, self.passed, i).start()

    def scan(self):
        slots = self.nx * self.nz
        some = pl.ds(0, slots - self.nx - 1)
        self.remote(self.gin.at[some], self.gin.at[some], 1, self.ri, self.partner()).wait_recv()
        total = jnp.zeros((DIM // self.nx, DIM), F32)
        for i in range(slots):
            slot = i if self.order > 0 else slots - 1 - i
            self.pout[slot] = total
            total = total + self.gin[slot]
        self.pin[self.z, self.x] = self.pout[self.slot]

        @pl.loop(0, self.nz - 2)
        def _(e):
            to = ring(SEND, e, self.z, self.nz)
            for i in range(self.nx):
                self.out_copy(i, to).start()

        for i in range(1, self.nx):
            self.out_copy(i, self.z).start()

    def arrived(self, m, parts):
        part = self.pin.at[m, pl.ds(0, parts)]
        self.remote(part, part, 2, self.ro.at[m], self.partner()).wait_recv()

    def finish(self, m):
        @pl.when(m == self.z)
        def _():
            self.arrived(m, self.nx - 1)

        @pl.when(m != self.z)
        def _():
            self.arrived(m, self.nx)

        @pl.when(m == self.passed)
        def _():
            before = self.pin[m]
            self.on[...] = jnp.where(self.first, before + self.s[m], before)
            self.on_copy().start()
            self.pin[m] = jnp.where(self.first, before, before + self.given[...])

        before = self.pin[m].reshape(DIM, DIM)
        self.bkout[m] = jnp.where(self.pc == 0, before + self.own[self.c * HALF + m], before)
        self.bk_copy(m).start()
        return jnp.where(self.pc == 1, before + self.exch[m], before)

    def finished(self, m):
        self.bk_copy(m).wait_recv()
        return self.bkin[m]

    def drain(self):
        some = pl.ds(0, self.nx * (self.nz - 1) - 1)
        self.remote(self.exch, self.exch, 0, self.re.at[0], self.partner()).wait_send()
        self.remote(self.gin.at[some], self.gin.at[some], 1, self.ri, self.partner()).wait_send()
        self.remote(self.pout.at[some], self.pout.at[some], 2, self.ro.at[0], self.partner()).wait_send()
        self.remote(self.bkout, self.bkin, 3, self.rb.at[0], self.partner()).wait_send()
        self.give_copy().wait_send()
        self.on_copy().wait_send()


def kernel(
    sizes,
    q_hbm,
    k_hbm,
    v_hbm,
    g_hbm,
    gain_ref,
    dq_ref,
    dk_ref,
    dv_ref,
    dgain_ref,
    *scratch,
):
    ny, nx, nz = sizes
    scratch = list(scratch)

    def take(n):
        out = scratch[:n]
        del scratch[:n]
        return out

    q, k, v, g = take(4)
    dq, dk, dv = dq_ref.at[0], dk_ref.at[0], dv_ref.at[0]
    scores, d_out, prior = take(3)
    out_loc, dk_loc, dv_loc = take(3)
    gtile, gin1, acc1, gin2, acc2, gin3, acc3, gin4 = take(8)
    bufs1, sems1 = take(11), take(6)
    bufs2, sems2 = take(11), take(6)
    in_sem, gsend, g1r, g2r, g3r, g4r = take(6)

    y = lax.axis_index("dp")
    ctx = lax.axis_index("ctx")
    x = ctx // (2 * nz)
    z = (ctx // 2) % nz
    c = ctx % 2
    pos = (y, x, z, c)

    def device(y_, x_, z_, c_):
        return (y_, (x_ * nz + z_) * 2 + c_)

    def load(src, dst, first, i):
        part = pl.ds(pl.multiple_of(first * DIM, HALF * DIM), HALF * DIM)
        return pltpu.make_async_copy(src.at[0, :, part], dst.at[:, part], in_sem.at[i])

    loads = [load(src, dst, (1 - c) * HALF, i) for i, (src, dst) in enumerate(((k_hbm, k), (v_hbm, v)))]
    loads += [load(src, dst, c * HALF, 2 + i) for i, (src, dst) in enumerate(((k_hbm, k), (v_hbm, v)))]
    loads += [pltpu.make_async_copy(src.at[0], dst, in_sem.at[4 + i]) for i, (src, dst) in enumerate(((q_hbm, q), (g_hbm, g)))]
    for load in loads:
        load.start()

    def y_peer(i):
        return device((y + i) % ny, x, z, c)

    def x_peer(i):
        return device(y, (x + i) % nx, z, c)

    def z_peer(i):
        return device(y, x, (z + i) % nz, c)

    partner = device(y, x, z, 1 - c)
    barrier = pltpu.get_barrier_semaphore()
    pl.semaphore_signal(barrier, inc=1, device_id=partner, device_id_type=MESH)
    for i in range(1, ny):
        pl.semaphore_signal(barrier, inc=1, device_id=y_peer(i), device_id_type=MESH)

    @pl.loop(1, nx * nz)
    def _(i):
        to = (x * nz + z + i) % (nx * nz)
        pl.semaphore_signal(barrier, inc=1, device_id=(y, to * 2 + c), device_id_type=MESH)

    one = Scan((nx, nz), pos, 1, bufs1, sems1)
    two = Scan((nx, nz), pos, -1, bufs2, sems2)
    one.clear()
    two.clear()

    def col(h):
        return pl.ds(pl.multiple_of(h * DIM, DIM), DIM)

    mine, other = c * HALF, (1 - c) * HALF

    def columns(ref, heads):
        return [ref[:, col(h)] for h in heads]

    def local_states(heads):
        ks, vs = columns(k, heads), columns(v, heads)
        states = [dot(kh, vh, 0, 0) for kh, vh in zip(ks, vs)]
        for h, state in zip(heads, states):
            one.own[h] = state

    loads[0].wait()
    loads[1].wait()

    def place(e):
        return ring(MAKE, jnp.int32(e), z, nz)

    for i in range(0, HALF, 4):
        local_states([other + place(i + u) for u in range(4)])
        if i == 0:
            pl.semaphore_wait(barrier, nx * nz + ny - 1)
        for u in range(4):
            one.exch_copy(place(i + u)).start()

    loads[2].wait()
    loads[3].wait()

    for i in range(0, HALF, 4):
        local_states([mine + place(i + u) for u in range(4)])
        if i == 4:
            one.pass_in()
        for u in range(4):
            one.add_chip(place(i + u))

    loads[4].wait()
    loads[5].wait()

    keep = lax.broadcasted_iota(jnp.int32, (DIM, DIM), 0) >= lax.broadcasted_iota(jnp.int32, (DIM, DIM), 1)

    def before_one(heads):
        qs, ks, vs = columns(q, heads), columns(k, heads), columns(v, heads)
        raw = [dot(qh, kh, 1, 1) for qh, kh in zip(qs, ks)]
        lows = [jnp.where(keep, r, 0.0).astype(BF16) for r in raw]
        outs = [dot(low, vh, 1, 0) for low, vh in zip(lows, vs)]
        for h, low, out in zip(heads, lows, outs):
            scores[h] = low
            out_loc[h] = out

    def pass_one(heads, states):
        qs = columns(q, heads)
        gfs = [gh.astype(F32) for gh in columns(g, heads)]
        gains = columns(gain_ref, heads)
        locs = [out_loc[h] for h in heads]
        lows = [state.astype(BF16) for state in states]
        outs = [loc + dot(qh, low, 1, 0) for loc, qh, low in zip(locs, qs, lows)]
        invs = [lax.rsqrt(jnp.mean(out * out, axis=1, keepdims=True) + EPSILON) for out in outs]
        normeds = [out * inv for out, inv in zip(outs, invs)]
        gns = [gf * gain for gf, gain in zip(gfs, gains)]
        means = [jnp.mean(gn * normed, axis=1, keepdims=True) for gn, normed in zip(gns, normeds)]
        ds = [((gn - normed * mean) * inv).astype(BF16) for gn, normed, mean, inv in zip(gns, normeds, means, invs)]
        grads = [dot(qh, d, 0, 0) for qh, d in zip(qs, ds)]
        terms = [jnp.sum((gf * normed).reshape(DIM // 8, 8, DIM), axis=0) for gf, normed in zip(gfs, normeds)]
        for h, low, d, grad, term in zip(heads, lows, ds, grads, terms):
            prior[h] = low
            d_out[h] = d
            two.own[h] = grad
            gtile[h] = term

    def between(heads):
        ds, lows, scs = [d_out[h] for h in heads], [prior[h] for h in heads], [scores[h] for h in heads]
        qs, ks, vs = columns(q, heads), columns(k, heads), columns(v, heads)
        raw = [dot(d, vh, 1, 1) for d, vh in zip(ds, vs)]
        dvs = [dot(sc, d, 0, 0) for sc, d in zip(scs, ds)]
        pqs = [dot(d, low, 1, 1) for d, low in zip(ds, lows)]
        gss = [jnp.where(keep, r, 0.0).astype(BF16) for r in raw]
        dqs = [(dot(gs, kh, 1, 0) + pq).astype(BF16) for gs, kh, pq in zip(gss, ks, pqs)]
        dks = [dot(gs, qh, 0, 0) for gs, qh in zip(gss, qs)]
        for h, dqh, dkh, dvh in zip(heads, dqs, dks, dvs):
            dq[:, col(h)] = dqh
            dk_loc[h] = dkh
            dv_loc[h] = dvh

    def pass_two(heads, states):
        ks, vs = columns(k, heads), columns(v, heads)
        dks, dvs = [dk_loc[h] for h in heads], [dv_loc[h] for h in heads]
        lows = [state.astype(BF16) for state in states]
        dks = [(part + dot(vh, low, 1, 1)).astype(BF16) for part, vh, low in zip(dks, vs, lows)]
        dvs = [(part + dot(kh, low, 1, 0)).astype(BF16) for part, kh, low in zip(dvs, ks, lows)]
        for h, dkh, dvh in zip(heads, dks, dvs):
            dk[:, col(h)] = dkh
            dv[:, col(h)] = dvh

    ry, rx = HEADS // ny, HEADS // ny // nx

    def g1_copy(i):
        src = gtile.at[pl.ds(((y + i) % ny) * ry, ry)]
        return pltpu.make_async_remote_copy(
            src_ref=src, dst_ref=gin1.at[i - 1], send_sem=gsend.at[0], recv_sem=g1r.at[i - 1], device_id=y_peer(i), device_id_type=MESH
        )

    def g2_copy(i):
        src = acc1.at[pl.ds(((x + i) % nx) * rx, rx)]
        return pltpu.make_async_remote_copy(
            src_ref=src, dst_ref=gin2.at[i - 1], send_sem=gsend.at[1], recv_sem=g2r.at[i - 1], device_id=x_peer(i), device_id_type=MESH
        )

    def g3_copy(i):
        return pltpu.make_async_remote_copy(
            src_ref=acc2, dst_ref=gin3.at[i - 1], send_sem=gsend.at[2], recv_sem=g3r.at[i - 1], device_id=z_peer(i), device_id_type=MESH
        )

    def g4_copy():
        return pltpu.make_async_remote_copy(
            src_ref=acc3, dst_ref=gin4, send_sem=gsend.at[3], recv_sem=g4r, device_id=partner, device_id_type=MESH
        )

    def gain_step(stage):
        if stage == 0:
            for i in range(1, ny):
                g1_copy(i).start()
        elif stage == 1:
            total = gtile[pl.ds(y * ry, ry)]
            for i in range(1, ny):
                g1_copy(i).wait_recv()
                total = total + gin1[i - 1]
            acc1[...] = total
            for i in range(1, nx):
                g2_copy(i).start()
        elif stage == 2:
            total = acc1[pl.ds(x * rx, rx)]
            for i in range(1, nx):
                g2_copy(i).wait_recv()
                total = total + gin2[i - 1]
            acc2[...] = total
            for i in range(1, nz):
                g3_copy(i).start()
        elif stage == 3:
            total = acc2[...]
            for i in range(1, nz):
                g3_copy(i).wait_recv()
                total = total + gin3[i - 1]
            acc3[...] = total
            g4_copy().start()
        else:
            g4_copy().wait_recv()
            scale = 1.0 / math.sqrt(ny * nx * nz * 2 * DIM)
            total = jnp.sum(acc3[...] + gin4[...], axis=1, keepdims=True) * scale
            dgain_ref[...] = jnp.broadcast_to(total, dgain_ref.shape)

    def arrival(e):
        return ring(WORK, e, z, nz)

    def finishing(scan, work, after, last, final):
        @pl.loop(0, HALF + LAG + SUM_LAG)
        def _(e):
            @pl.when(e >= LAG + SUM_LAG)
            def _():
                last(arrival(e - LAG - SUM_LAG))

            @pl.when(e == HALF + LAG - 1)
            def _():
                final()

            @pl.when(e < LAG)
            def _():
                m = arrival(e)
                work([mine + m], [scan.finish(m)])

            @pl.when((e >= LAG) & (e < HALF))
            def _():
                m, n = arrival(e), arrival(e - LAG)
                state = scan.finish(m)
                work([mine + m, other + n], [state, scan.finished(n)])
                after(n)

            @pl.when((e >= HALF) & (e < HALF + LAG))
            def _():
                n = arrival(e - LAG)
                work([other + n], [scan.finished(n)])
                after(n)

    def nothing(*_):
        pass

    @pl.loop(0, HALF)
    def _(m):
        before_one([mine + m, other + m])

    one.scan()
    finishing(one, pass_one, lambda m: two.exch_copy(m).start(), two.add_chip, two.pass_in)
    gain_step(0)

    @pl.loop(0, HALF)
    def _(m):
        between([mine + m, other + m])

        @pl.when(m == HALF // 2)
        def _():
            gain_step(1)

    gain_step(2)
    two.scan()
    gain_step(3)
    finishing(two, pass_two, nothing, nothing, nothing)
    gain_step(4)

    one.drain()
    two.drain()
    for i in range(1, ny):
        g1_copy(i).wait_send()
    for i in range(1, nx):
        g2_copy(i).wait_send()
    for i in range(1, nz):
        g3_copy(i).wait_send()
    g4_copy().wait_send()


def hand_over(nz, a, b, c, gain, a_out, b_out, c_out, gain_out, gain_buf, sems):
    stores = []
    for row in range(0, DIM, BLOCK):
        for src, dst in ((a, a_out), (b, b_out), (c, c_out)):
            part = pl.ds(row, BLOCK)
            stores.append(pltpu.make_async_copy(src.at[0, part], dst.at[0, part], sems.at[len(stores)]))
    load_gain = pltpu.make_async_copy(gain, gain_buf, sems.at[len(stores)])
    load_gain.start()
    for store in stores:
        store.start()
    load_gain.wait()
    share = gain_out.shape[1]
    place = lax.rem(lax.axis_index("ctx"), 2 * nz) * share
    turned = pltpu.roll(gain_buf[place // DIM], (DIM - place % DIM) % DIM, 1)
    gain_out[...] = turned[0:1, :share]
    for store in stores:
        store.wait()


def build(mesh, nx, nz):
    ny = mesh.shape["dp"]
    width = HEADS * DIM
    ry, rx = HEADS // ny, HEADS // ny // nx

    def scan_scratch():
        state = pltpu.VMEM((HALF, DIM, DIM), F32)
        parts = pltpu.VMEM((HALF, nx, DIM // nx, DIM), F32)
        slots = pltpu.VMEM((nx * nz, DIM // nx, DIM), F32)
        return [
            pltpu.VMEM((HEADS, DIM, DIM), F32),
            state,
            parts,
            slots,
            slots,
            parts,
            state,
            state,
            *[pltpu.VMEM((nx, DIM // nx, DIM), F32)] * 3,
            pltpu.SemaphoreType.DMA((HALF,)),
            pltpu.SemaphoreType.DMA,
            *[pltpu.SemaphoreType.DMA((HALF,))] * 2,
            pltpu.SemaphoreType.DMA,
            pltpu.SemaphoreType.DMA((6,)),
        ]

    scratch = [
        *[pltpu.VMEM((DIM, width), BF16)] * 4,
        *[pltpu.VMEM((HEADS, DIM, DIM), BF16)] * 3,
        *[pltpu.VMEM((HEADS, DIM, DIM), F32)] * 3,
        pltpu.VMEM((HEADS, 8, DIM), F32),
        pltpu.VMEM((ny - 1, ry, 8, DIM), F32),
        pltpu.VMEM((ry, 8, DIM), F32),
        pltpu.VMEM((nx - 1, rx, 8, DIM), F32),
        pltpu.VMEM((rx, 8, DIM), F32),
        pltpu.VMEM((nz - 1, rx, 8, DIM), F32),
        pltpu.VMEM((rx, 8, DIM), F32),
        pltpu.VMEM((rx, 8, DIM), F32),
        *scan_scratch(),
        *scan_scratch(),
        pltpu.SemaphoreType.DMA((6,)),
        pltpu.SemaphoreType.DMA((4,)),
        pltpu.SemaphoreType.DMA((ny - 1,)),
        pltpu.SemaphoreType.DMA((nx - 1,)),
        pltpu.SemaphoreType.DMA((nz - 1,)),
        pltpu.SemaphoreType.DMA,
    ]

    def body(queries, key_rows, value_rows, out_grad, norm_gain):
        rows = jax.ShapeDtypeStruct(queries.shape, BF16)
        dq, dk, dv, dgain = pl.pallas_call(
            functools.partial(kernel, (ny, nx, nz)),
            out_shape=(*[pltpu.VMEM(queries.shape, BF16)] * 3, pltpu.VMEM((rx, 8, DIM), F32)),
            in_specs=[pl.BlockSpec(memory_space=pl.ANY)] * 4 + [pl.BlockSpec(memory_space=pltpu.VMEM)],
            out_specs=[pl.BlockSpec(memory_space=pltpu.VMEM)] * 4,
            scratch_shapes=scratch,
            compiler_params=pltpu.CompilerParams(
                collective_id=0, has_side_effects=True, vmem_limit_bytes=62 * 1024 * 1024
            ),
        )(queries, key_rows, value_rows, out_grad, norm_gain.reshape(1, width))
        share = rx * DIM // (2 * nz)
        dq, dk, dv, dgain = pl.pallas_call(
            functools.partial(hand_over, nz),
            out_shape=(rows, rows, rows, jax.ShapeDtypeStruct((1, share), F32)),
            in_specs=[pl.BlockSpec(memory_space=pl.ANY)] * 4,
            out_specs=[pl.BlockSpec(memory_space=pl.ANY)] * 3 + [pl.BlockSpec(memory_space=pltpu.VMEM)],
            scratch_shapes=[pltpu.VMEM((rx, 8, DIM), F32), pltpu.SemaphoreType.DMA((3 * (DIM // BLOCK) + 1,))],
            compiler_params=pltpu.CompilerParams(vmem_limit_bytes=8 * 1024 * 1024),
        )(dq, dk, dv, dgain)
        return dq, dk, dv, dgain.reshape(share)

    placed = P("dp", "ctx", None)
    return jax.shard_map(
        body,
        mesh=mesh,
        in_specs=(placed, placed, placed, placed, P()),
        out_specs=(placed, placed, placed, P(("dp", "ctx"))),
        check_vma=False,
    )


def solution(mesh):
    return build(mesh, 4, 8)
```
